128 devices in a mesh: batch: 2 (over y_lo), seq: 16 (over y_hi, x, core), tensor: 4 (over z).
Axes of the slice: x: 4, y: 4 (y_hi: 2, y_lo: 2; y = y_hi * 2 + y_lo), z: 4, core: 2. Of those that a mesh axis runs over, the one named last changes fastest.
Arguments:
- hidden_in: float32 [2, 2, 2048, 1024], P(None, 'batch', 'seq'), may hold values from -6 to 6
- document_ids: int32 [2, 2, 2048], P(None, 'batch', 'seq'), may hold values from 0 to 2, as said below
- first_gain: float32 [2, 1024], replicated, may hold values from 0.1 to 1.9
- first_shift: float32 [2, 1024], replicated, may hold values from -1.75 to 1.75
- second_gain: float32 [2, 1024], replicated, may hold values from 0.1 to 1.9
- second_shift: float32 [2, 1024], replicated, may hold values from -1.75 to 1.75
- attn_weight: bfloat16 [2, 1024, 3072], P(None, ('batch', 'seq'), 'tensor'), may hold values from -0.1875 to 0.1875
- attn_bias: float32 [2, 3072], P(None, 'tensor'), may hold values from -1.75 to 1.75
- dense_weight: bfloat16 [2, 1024, 1024], P(None, 'tensor', ('batch', 'seq')), may hold values from -1.5 to 1.5
- dense_bias: float32 [2, 1024], replicated, may hold values from -1.75 to 1.75
- expand_weight: bfloat16 [2, 1024, 4096], P(None, ('batch', 'seq'), 'tensor'), may hold values from -0.1875 to 0.1875
- expand_bias: float32 [2, 4096], P(None, 'tensor'), may hold values from -3 to 3
- shrink_weight: bfloat16 [2, 4096, 1024], P(None, 'tensor', ('batch', 'seq')), may hold values from -0.125 to 0.125
- shrink_bias: float32 [2, 1024], replicated, may hold values from -1.75 to 1.75
- output_grad: float32 [2, 2, 2048, 1024], P(None, 'batch', 'seq'), may hold values from -6 to 6
Outputs:
- hidden_out: float32 [2, 2, 2048, 1024], P(None, 'batch', 'seq')
- input_grad: float32 [2, 2, 2048, 1024], P(None, 'batch', 'seq')
- grad_first_gain: float32 [2, 1024], replicated
- grad_first_shift: float32 [2, 1024], replicated
- grad_second_gain: float32 [2, 1024], replicated
- grad_second_shift: float32 [2, 1024], replicated
- grad_attn_weight: float32 [2, 1024, 3072], P(None, ('batch', 'seq'), 'tensor')
- grad_attn_bias: float32 [2, 3072], P(None, 'tensor')
- grad_dense_weight: float32 [2, 1024, 1024], P(None, 'tensor', ('batch', 'seq'))
- grad_dense_bias: float32 [2, 1024], replicated
- grad_expand_weight: float32 [2, 1024, 4096], P(None, ('batch', 'seq'), 'tensor')
- grad_expand_bias: float32 [2, 4096], P(None, 'tensor')
- grad_shrink_weight: float32 [2, 4096, 1024], P(None, 'tensor', ('batch', 'seq'))
- grad_shrink_bias: float32 [2, 1024], replicated
The draws below stay inside these ranges and needn't reach their ends.
Inputs may be any that keep to these rules, and one draw needn't show every extreme that they name: `document_ids`: in every sequence the ids never fall and take each of the values 0, 1 and 2 on at least one token; id 1 begins within the first 128 tokens and ends within the last 128 tokens.
All inputs are finite; a program needn't handle non-finite values.
Results may differ from the reference program's by a relative error of at most 0.025.
Values may be sent and summed in bfloat16 or wider, within the bound.
A program may use at most 192 MiB of HBM per device.

```python
import jax
import jax.numpy as jnp
from jax import lax

D = 1024
HEADS = 16
HEAD = 64
FF = 4096
ROT = 16
LAYERS = 2
MICRO = 2
GROUP = 128
SEQ_LEN = 2048
SEQS = 2


def draw_document_ids(key, part):
    key = jax.random.fold_in(key, 7)
    first_key, second_key = jax.random.split(key)
    opening = jax.random.randint(first_key, (MICRO, SEQS, 1), 1, GROUP)
    closing = jax.random.randint(second_key, (MICRO, SEQS, 1), SEQ_LEN - GROUP + 1, SEQ_LEN)
    positions = jnp.arange(SEQ_LEN, dtype=jnp.int32)[None, None, :]
    return (positions >= opening).astype(jnp.int32) + (positions >= closing).astype(jnp.int32)


def levels(own_key, extent, cuts, least, largest):
    def one(position, shards_of):
        heights = jax.random.uniform(jax.random.fold_in(jax.random.fold_in(own_key, 6), position), (shards_of,), jnp.float32, least / len(cuts), largest / len(cuts))
        return jnp.repeat(jnp.exp(heights), extent[position] // shards_of).reshape((-1,) + (1,) * (len(extent) - position - 1))

    loudness = one(*cuts[0])
    for cut in cuts[1:]:
        loudness = loudness * one(*cut)
    return loudness


def gaussian(key, extent, width, limit, cuts=(), held_as=jnp.bfloat16):
    array = jax.random.normal(key, extent, jnp.float32) * width
    if len(cuts) > 0:
        array = levels(key, extent, cuts, -0.22, 0.18) * array
    return jnp.clip(array, min=-limit, max=limit).astype(held_as)


def setup_inputs(seed: int = 0) -> dict:
    streams_of = jax.random.split(jax.random.key(seed), 16)
    return {
        "hidden_in": gaussian(streams_of[0], (MICRO, SEQS, SEQ_LEN, D), 1.0, 6.0, ((1, 2), (2, 16)), jnp.float32),
        "document_ids": draw_document_ids(jax.random.fold_in(streams_of[15], 71), 0),
        "first_gain": jnp.clip(1.0 + 0.18 * jax.random.normal(streams_of[2], (LAYERS, D), jnp.float32), 0.1, 1.9),
        "first_shift": gaussian(streams_of[3], (LAYERS, D), 0.3, 1.75, (), jnp.float32),
        "second_gain": jnp.clip(1.0 + 0.18 * jax.random.normal(streams_of[4], (LAYERS, D), jnp.float32), 0.1, 1.9),
        "second_shift": gaussian(streams_of[5], (LAYERS, D), 0.3, 1.75, (), jnp.float32),
        "attn_weight": gaussian(streams_of[6], (LAYERS, D, 3 * D), D ** -0.5, 0.1875, ((1, 32), (2, 4))),
        "attn_bias": gaussian(streams_of[7], (LAYERS, 3 * D), 0.3, 1.75, ((1, 4),), jnp.float32),
        "dense_weight": gaussian(streams_of[8], (LAYERS, D, D), (D // 64) ** -0.5, 1.5, ((1, 4), (2, 32))),
        "dense_bias": gaussian(streams_of[9], (LAYERS, D), 0.3, 1.75, (), jnp.float32),
        "expand_weight": gaussian(streams_of[10], (LAYERS, D, FF), D ** -0.5, 0.1875, ((1, 32), (2, 4))),
        "expand_bias": gaussian(streams_of[11], (LAYERS, FF), 0.5, 3.0, ((1, 4),), jnp.float32),
        "shrink_weight": gaussian(streams_of[12], (LAYERS, FF, D), (FF // 2) ** -0.5, 0.125, ((1, 4), (2, 32))),
        "shrink_bias": gaussian(streams_of[13], (LAYERS, D), 0.3, 1.75, (), jnp.float32),
        "output_grad": gaussian(streams_of[14], (MICRO, SEQS, SEQ_LEN, D), 1.0, 6.0, ((1, 2), (2, 16)), jnp.float32),
    }


@jax.custom_vjp
def low(v):
    return lax.optimization_barrier(v.astype(jnp.bfloat16)).astype(jnp.float32)

@jax.custom_vjp
def low_back(v):
    return v

def low_keep(v):
    return (low(v), None)

def low_pass(kept, grad):
    return (grad,)

def back_keep(v):
    return (v, None)

def back_low(kept, grad):
    return (low(grad),)
low.defvjp(low_keep, low_pass)
low_back.defvjp(back_keep, back_low)
HIGHEST = lax.Precision.HIGHEST

def layer_norm(values, gain, shift):
    centre = lax.optimization_barrier(jnp.mean(values, axis=-1, keepdims=True))
    centred = values - centre
    spread = lax.optimization_barrier(jnp.mean(centred * centred, axis=-1, keepdims=True))
    return centred * lax.rsqrt(spread + 1e-05) * gain + shift

def rotary_angles(positions):
    inverse = 10000.0 ** (-jnp.arange(0, ROT, 2).astype(jnp.float32) / ROT)
    return positions.astype(jnp.float32)[:, None] * inverse[None, :]

def rotate(vectors, angles):
    halfway = ROT // 2
    cosine = jnp.cos(angles)
    sine_part = jnp.sin(angles)
    cosine = jnp.concatenate([cosine, cosine], axis=-1)[:, None, :]
    sine_part = jnp.concatenate([sine_part, sine_part], axis=-1)[:, None, :]
    leading = vectors[..., :ROT]
    turned = jnp.concatenate([-leading[..., halfway:], leading[..., :halfway]], axis=-1)
    return jnp.concatenate([leading * cosine + turned * sine_part, vectors[..., ROT:]], axis=-1)

def attend(queries, key_heads, value_heads, allowed):
    scaling = HEAD ** (-0.5)

    def one_head(pieces):
        head_query, head_keys, head_values = pieces
        scores = low_back(jnp.dot(head_query, head_keys.T, precision=HIGHEST) * scaling)
        softmaxed = jax.nn.softmax(jnp.where(allowed > 0, scores, -1000000000.0), axis=-1)
        return jnp.dot(low(softmaxed), head_values, precision=HIGHEST)
    per_head = lax.map(jax.checkpoint(one_head), (queries.transpose(1, 0, 2), key_heads.transpose(1, 0, 2), value_heads.transpose(1, 0, 2)))
    return per_head.transpose(1, 0, 2).reshape(SEQ_LEN, D)

def block(params, hidden, allowed, angles, layer_at):
    first_gain, first_shift, second_gain, second_shift, attn_weight, attn_bias, dense_weight, dense_bias, expand_weight, expand_bias, shrink_weight, shrink_bias = [item[layer_at] for item in params]
    normed_one = low(layer_norm(hidden, first_gain, first_shift))
    normed_two = low(layer_norm(hidden, second_gain, second_shift))
    projected = low_back(jnp.dot(normed_one, attn_weight, precision=HIGHEST) + attn_bias)
    projected = projected.reshape(SEQ_LEN, HEADS, 3, HEAD)
    queries = low(rotate(projected[:, :, 0], angles))
    key_heads = low(rotate(projected[:, :, 1], angles))
    value_heads = low(projected[:, :, 2])
    context = low(low_back(attend(queries, key_heads, value_heads, allowed)))
    expanded = low_back(jnp.dot(normed_two, expand_weight, precision=HIGHEST) + expand_bias)
    active = low(jax.nn.gelu(expanded, approximate=False))
    branch = low_back(jnp.dot(context, dense_weight, precision=HIGHEST) + dense_bias + jnp.dot(active, shrink_weight, precision=HIGHEST) + shrink_bias)
    return hidden + branch

def reference(hidden_in, document_ids, first_gain, first_shift, second_gain, second_shift, attn_weight, attn_bias, dense_weight, dense_bias, expand_weight, expand_bias, shrink_weight, shrink_bias, output_grad):
    params = tuple((item.astype(jnp.float32) for item in (first_gain, first_shift, second_gain, second_shift, attn_weight, attn_bias, dense_weight, dense_bias, expand_weight, expand_bias, shrink_weight, shrink_bias)))
    total_rows = MICRO * SEQS
    rows_in = hidden_in.astype(jnp.float32).reshape(total_rows, SEQ_LEN, D)
    idents_in = document_ids.reshape(total_rows, SEQ_LEN)
    positions = jnp.arange(SEQ_LEN, dtype=jnp.int32)
    angles = rotary_angles(positions)
    causal = positions[:, None] >= positions[None, :]

    def forward(weights, inputs):

        def one_sequence(couple):
            hidden, idents = couple
            allowed = (causal & (idents[:, None] == idents[None, :])).astype(jnp.int32)
            for layer_at in range(LAYERS):
                hidden = block(weights, hidden, allowed, angles, layer_at)
            return hidden
        return lax.map(jax.checkpoint(one_sequence), (inputs, idents_in))
    outputs, pullback = jax.vjp(forward, params, rows_in)
    grads, grad_rows = pullback(output_grad.astype(jnp.float32).reshape(total_rows, SEQ_LEN, D))
    shape_out = (MICRO, SEQS, SEQ_LEN, D)
    return (outputs.reshape(shape_out), grad_rows.reshape(shape_out), grads[0], grads[1], grads[2], grads[3], grads[4], grads[5], grads[6], grads[7], grads[8], grads[9], grads[10], grads[11])
```

```python
import functools

import jax
import jax.numpy as jnp
from jax import lax
from jax.experimental import pallas as pl
from jax.experimental.pallas import tpu as pltpu
from jax.sharding import PartitionSpec as P

HEAD = 64
ROT = 16
LAYERS = 2
MASKED = -1000000000.0
MESH = pl.DeviceIdType.MESH
F32, BF16 = jnp.float32, jnp.bfloat16
VLIM = 56 * 1024 * 1024


def dot(a, b, ca, cb):
    return lax.dot_general(a, b, (((ca,), (cb,)), ((), ())), preferred_element_type=F32)


def places():
    s = lax.axis_index("seq")
    return s, s // 2, lax.rem(s, 2)


def greet(peers):
    barrier = pltpu.get_barrier_semaphore()
    for peer in peers:
        pl.semaphore_signal(barrier, inc=1, device_id=peer, device_id_type=MESH)
    pl.semaphore_wait(barrier, len(peers))


def remote(src, dst, send, recv, peer):
    return pltpu.make_async_remote_copy(
        src_ref=src, dst_ref=dst, send_sem=send, recv_sem=recv, device_id=peer, device_id_type=MESH
    )


def chip_peers():
    _, c, k = places()
    return [{"seq": lax.rem(c + d, 8) * 2 + k} for d in range(1, 8)]


def comm_call(body, out_shape, scratch, ident, in_space, out_space, n_in, name):
    single = not isinstance(out_shape, (tuple, list))
    return pl.pallas_call(
        body,
        out_shape=out_shape,
        in_specs=[pl.BlockSpec(memory_space=in_space)] * n_in,
        out_specs=pl.BlockSpec(memory_space=out_space)
        if single
        else [pl.BlockSpec(memory_space=out_space)] * len(out_shape),
        scratch_shapes=scratch,
        compiler_params=pltpu.CompilerParams(
            collective_id=ident, has_side_effects=True, vmem_limit_bytes=VLIM
        ),
        name=name,
    )


def gather_kernel(src, out, ssem, rsem, fs, fr, lsem):
    b = lax.axis_index("batch")
    s, c, k = places()
    p = b * 8 + c
    partner = {"seq": s + 1 - 2 * k}
    others = []
    for d in range(1, 16):
        p2 = lax.rem(p + d, 16)
        others.append({"batch": p2 // 8, "seq": lax.rem(p2, 8) * 2 + k})
    greet(others + [partner])
    mine = b * 16 + s
    local = pltpu.make_async_copy(src, out.at[mine], lsem)
    local.start()
    copies = [
        remote(src, out.at[mine], ssem.at[d], rsem.at[d], peer) for d, peer in enumerate(others)
    ]
    for copy in copies:
        copy.start()
    onward = [remote(src, out.at[mine], fs.at[0], fr.at[0], partner)]
    onward[0].start()
    for d in range(1, 16):
        copies[d - 1].wait_recv()
        p2 = lax.rem(p - d + 16, 16)
        at = out.at[(p2 // 8) * 16 + lax.rem(p2, 8) * 2 + k]
        copy = remote(at, at, fs.at[d], fr.at[d], partner)
        copy.start()
        onward.append(copy)
    local.wait()
    for copy in copies:
        copy.wait_send()
    for copy in onward:
        copy.wait()


def gather_weights(shard):
    rows, cols = shard.shape
    dma = pltpu.SemaphoreType.DMA
    return comm_call(
        gather_kernel,
        jax.ShapeDtypeStruct((32, rows, cols), shard.dtype),
        [dma((15,)), dma((15,)), dma((16,)), dma((16,)), dma(())],
        1,
        pl.ANY,
        pl.ANY,
        1,
        "gather_weights",
    )(shard).reshape(32 * rows, cols)


def heads_out_kernel(src, kv_out, q_out, ssem, rsem, fs, fr, lsem):
    s, c, k = places()
    partner = {"seq": s + 1 - 2 * k}
    others = chip_peers()
    greet(others + [partner])
    copies = []
    for d, peer in enumerate(others):
        c2 = lax.rem(c + d + 1, 8)
        copies.append(
            remote(src.at[c2, 0], kv_out.at[s], ssem.at[0, d], rsem.at[0, d], peer)
        )
        copies[-1].start()
    copies_q = []
    for d, peer in enumerate(others):
        c2 = lax.rem(c + d + 1, 8)
        copies_q.append(
            remote(src.at[c2, 1], q_out.at[c], ssem.at[1, d], rsem.at[1, d], peer)
        )
        copies_q[-1].start()
    onward = [remote(src.at[c, 0], kv_out.at[s], fs.at[0], fr.at[0], partner)]
    onward[0].start()
    own_kv = pltpu.make_async_copy(src.at[c, 0], kv_out.at[s], lsem.at[0])
    own_q = pltpu.make_async_copy(src.at[c, 1], q_out.at[c], lsem.at[1])
    own_kv.start()
    own_q.start()
    for d in range(1, 8):
        copies[d - 1].wait_recv()
        at = kv_out.at[lax.rem(c - d + 8, 8) * 2 + k]
        copy = remote(at, at, fs.at[d], fr.at[d], partner)
        copy.start()
        onward.append(copy)
    own_kv.wait()
    own_q.wait()
    for copy in copies:
        copy.wait_send()
    for copy in copies_q:
        copy.wait()
    for copy in onward:
        copy.wait()


def heads_out(qkv):
    dma = pltpu.SemaphoreType.DMA
    return comm_call(
        heads_out_kernel,
        (
            jax.ShapeDtypeStruct((16, 128, 128), BF16),
            jax.ShapeDtypeStruct((8, 128, 128), BF16),
        ),
        [dma((2, 7)), dma((2, 7)), dma((8,)), dma((8,)), dma((2,))],
        2,
        pl.ANY,
        pl.ANY,
        1,
        "heads_out",
    )(qkv)


def swap_kernel(src, out, ssem, rsem, lsem):
    _, c, _ = places()
    others = chip_peers()
    greet(others)
    copies = []
    for d, peer in enumerate(others):
        c2 = lax.rem(c + d + 1, 8)
        copies.append(remote(src.at[c2], out.at[c], ssem.at[d], rsem.at[d], peer))
        copies[-1].start()
    own = pltpu.make_async_copy(src.at[c], out.at[c], lsem)
    own.start()
    own.wait()
    for copy in copies:
        copy.wait()


def swap_chips(blocks):
    dma = pltpu.SemaphoreType.DMA
    return comm_call(
        swap_kernel,
        jax.ShapeDtypeStruct(blocks.shape, blocks.dtype),
        [dma((7,)), dma((7,)), dma(())],
        3,
        pl.ANY,
        pl.ANY,
        1,
        "swap_chips",
    )(blocks)


def heads_back_kernel(dq, dkv, dq_out, dkv_out, other, total, ssem, rsem, psem, lsem):
    s, c, k = places()
    partner = {"seq": s + 1 - 2 * k}
    others = chip_peers()
    greet(others + [partner])
    theirs = remote(dkv.at[1 - k], other, psem.at[0], psem.at[1], partner)
    theirs.start()
    copies = []
    for d, peer in enumerate(others):
        c2 = lax.rem(c + d + 1, 8)
        copies.append(remote(dq.at[c2], dq_out.at[c], ssem.at[0, d], rsem.at[0, d], peer))
        copies[-1].start()
    own_q = pltpu.make_async_copy(dq.at[c], dq_out.at[c], lsem)
    own_q.start()
    theirs.wait()
    total[...] = (dkv[k] + other[...]).astype(BF16)
    for d, peer in enumerate(others):
        c2 = lax.rem(c + d + 1, 8)
        copies.append(
            remote(total.at[c2], dkv_out.at[c], ssem.at[1, d], rsem.at[1, d], peer)
        )
        copies[-1].start()
    own_q.wait()
    own_kv = pltpu.make_async_copy(total.at[c], dkv_out.at[c], lsem)
    own_kv.start()
    own_kv.wait()
    for copy in copies:
        copy.wait()


def heads_back(dq, dkv):
    dma = pltpu.SemaphoreType.DMA
    shape = jax.ShapeDtypeStruct((8, 128, 128), BF16)
    return comm_call(
        heads_back_kernel,
        (shape, shape),
        [
            pltpu.VMEM((8, 128, 128), F32),
            pltpu.VMEM((8, 128, 128), BF16),
            dma((2, 7)),
            dma((2, 7)),
            dma((2,)),
            dma(()),
        ],
        4,
        pltpu.VMEM,
        pltpu.VMEM,
        2,
        "heads_back",
    )(dq, dkv)


def tensor_sum_kernel(part, out, got, ssem, rsem):
    t = lax.axis_index("tensor")
    peers = [{"tensor": lax.rem(t + d, 4)} for d in range(1, 4)]
    greet(peers)
    copies = []
    for d, peer in enumerate(peers):
        copies.append(
            remote(part.at[lax.rem(t + d + 1, 4)], got.at[d], ssem.at[0, d], rsem.at[0, d], peer)
        )
        copies[-1].start()
    for copy in copies:
        copy.wait_recv()
    total = part[t].astype(F32) + got[0].astype(F32) + got[1].astype(F32) + got[2].astype(F32)
    out[t] = total.astype(BF16)
    for d, peer in enumerate(peers):
        copies.append(remote(out.at[t], out.at[t], ssem.at[1, d], rsem.at[1, d], peer))
        copies[-1].start()
    for copy in copies[:3]:
        copy.wait_send()
    for copy in copies[3:]:
        copy.wait()


def tensor_sum(part):
    dma = pltpu.SemaphoreType.DMA
    return comm_call(
        tensor_sum_kernel,
        jax.ShapeDtypeStruct(part.shape, BF16),
        [pltpu.VMEM((3, *part.shape[1:]), BF16), dma((2, 3)), dma((2, 3))],
        5,
        pltpu.VMEM,
        pltpu.VMEM,
        1,
        "tensor_sum",
    )(part)


def scatter_kernel(count, *refs):
    ins, outs = refs[:count], refs[count : 2 * count]
    rest = refs[2 * count :]
    pair, sums, got = rest[:count], rest[count : 2 * count], rest[2 * count : 3 * count]
    ps, pr, ssem, rsem = rest[3 * count :]
    b = lax.axis_index("batch")
    s, c, k = places()
    p = b * 8 + c
    partner = {"seq": s + 1 - 2 * k}
    others = []
    for d in range(1, 16):
        p2 = lax.rem(p + d, 16)
        others.append({"batch": p2 // 8, "seq": lax.rem(p2, 8) * 2 + k})
    greet(others + [partner])
    first = []
    for d in range(16):
        p2 = lax.rem(p + d + 1, 16)
        for a in range(count):
            copy = remote(
                ins[a].at[p2, 1 - k], pair[a].at[p2], ps.at[a, d], pr.at[a, d], partner
            )
            copy.start()
            first.append(copy)
    second = []
    for d in range(16):
        p2 = lax.rem(p + d + 1, 16)
        for a in range(count):
            first[d * count + a].wait_recv()
            total = ins[a][p2, k].astype(F32) + pair[a][p2].astype(F32)
            if d < 15:
                sums[a][d] = total.astype(BF16)
                copy = remote(sums[a].at[d], got[a].at[d], ssem.at[a, d], rsem.at[a, d], others[d])
                copy.start()
                second.append(copy)
            else:
                outs[a][...] = total
    for d in range(15):
        for a in range(count):
            second[d * count + a].wait_recv()
            outs[a][...] += got[a][d].astype(F32)
    for copy in first:
        copy.wait_send()
    for copy in second:
        copy.wait_send()


def scatter_sum(arrays):
    count = len(arrays)
    dma = pltpu.SemaphoreType.DMA
    shaped = [a.reshape(16, 2, 32, a.shape[1]) for a in arrays]
    widths = [a.shape[1] for a in arrays]
    return comm_call(
        functools.partial(scatter_kernel, count),
        tuple(jax.ShapeDtypeStruct((32, w), F32) for w in widths),
        [pltpu.VMEM((16, 32, w), BF16) for w in widths]
        + [pltpu.VMEM((15, 32, w), BF16) for w in widths]
        + [pltpu.VMEM((15, 32, w), BF16) for w in widths]
        + [dma((count, 16)), dma((count, 16)), dma((count, 15)), dma((count, 15))],
        6,
        pltpu.VMEM,
        pltpu.VMEM,
        count,
        "scatter_sum",
    )(*shaped)


def turned(values, cosine, sine):
    lane = lax.broadcasted_iota(jnp.int32, values.shape, 1)
    swapped = jnp.where(
        lane < 8, pltpu.roll(values, 120, axis=1), pltpu.roll(values, 8, axis=1)
    )
    return values * cosine + swapped * sine


def normal(values):
    centred = values - jnp.mean(values, axis=-1, keepdims=True)
    rstd = lax.rsqrt(jnp.mean(centred * centred, axis=-1, keepdims=True) + 1e-05)
    return centred * rstd, rstd


def project_kernel(x, g1, b1, g2, b2, bias, weight, cosine, sine, h1, h2, qkv):
    hat, _ = normal(x[...])
    h1[...] = (hat * g1[...] + b1[...]).astype(BF16)
    h2[...] = (hat * g2[...] + b2[...]).astype(BF16)
    proj = dot(h1[...], weight[...], 1, 0) + bias[...]
    cos, sin = cosine[...], sine[...]
    lane = lax.broadcasted_iota(jnp.int32, (128, 128), 1)
    for m in range(2):
        rows = proj[m * 128 : (m + 1) * 128]
        for h in range(4):
            pair = rows[:, 128 * h : 128 * (h + 1)]
            qkv[m * 4 + h, 0] = turned(pair, cos, sin).astype(BF16)
            q = rows[:, 512 + 128 * (h // 2) : 640 + 128 * (h // 2)]
            if h % 2:
                q = pltpu.roll(q, 64, axis=1)
            q = turned(q, cos, sin) * 0.125
            qkv[m * 4 + h, 1] = jnp.where(lane < 64, q, 0.0).astype(BF16)


def local_call(body, out_shape, in_specs, name, scratch=()):
    return pl.pallas_call(
        body,
        out_shape=out_shape,
        grid=(1,),
        in_specs=in_specs,
        out_specs=jax.tree.map(lambda o: whole(o.shape), out_shape),
        scratch_shapes=scratch,
        compiler_params=pltpu.CompilerParams(vmem_limit_bytes=VLIM),
        name=name,
    )


def whole(shape):
    return pl.BlockSpec(shape, lambda i: (0,) * len(shape))


def columns(width, at):
    return pl.BlockSpec((1024, width), lambda i: (0, at))


def wholes(*arrays):
    return [whole(a.shape) for a in arrays]


def project(x, g1, b1, g2, b2, bias, gathered, cosine, sine):
    sds = jax.ShapeDtypeStruct
    return local_call(
        project_kernel,
        (
            sds((256, 1024), BF16),
            sds((256, 1024), BF16),
            sds((8, 2, 128, 128), BF16),
        ),
        wholes(x, g1, b1, g2, b2, bias) + [columns(768, 0)] + wholes(cosine, sine),
        "project",
    )(x, g1, b1, g2, b2, bias, gathered, cosine, sine)


def scores_of(q, keys, low, high):
    s = dot(q, keys, 1, 1)
    place = lax.broadcasted_iota(jnp.int32, s.shape, 1)
    return jnp.where((place >= low) & (place <= high), s, MASKED)


def attend_kernel(kv, q, low, high, ctx, lse):
    for i in range(8):
        n = 256 * (i + 1)
        keys = kv[0 : 2 * (i + 1)].reshape(n, 128)
        s = scores_of(q[i], keys, low[i], high[i])
        top = jnp.max(s, axis=-1, keepdims=True)
        e = jnp.exp(s - top)
        total = jnp.sum(e, axis=-1, keepdims=True)
        soft = (e * (1.0 / total)).astype(BF16)
        ctx[i] = dot(soft, keys, 1, 0).astype(BF16)
        lse[i] = top + jnp.log(total)


def attend(kv, q, low, high):
    sds = jax.ShapeDtypeStruct
    return local_call(
        attend_kernel,
        (sds((8, 128, 128), BF16), sds((8, 128, 1), F32)),
        wholes(kv, q, low, high),
        "attend",
    )(kv, q, low, high)


def attend_back_kernel(kv, q, dctx, lse, low, high, dq, dkv, total):
    for i in reversed(range(8)):
        n = 256 * (i + 1)
        keys = kv[0 : 2 * (i + 1)].reshape(n, 128)
        s = scores_of(q[i], keys, low[i], high[i])
        soft = jnp.exp(s - lse[i])
        dsoft = dot(dctx[i], keys, 1, 1)
        term = jnp.sum(soft * dsoft, axis=-1, keepdims=True)
        ds = (soft * (dsoft - term)).astype(BF16)
        dq[i] = (dot(ds, keys, 1, 0) * 0.125).astype(BF16)
        both = jnp.concatenate([ds, soft.astype(BF16)], axis=0)
        right = jnp.concatenate([q[i], dctx[i]], axis=0)
        fresh = dot(both, right, 0, 0)
        if i == 7:
            total[...] = fresh
        else:
            total[0:n] += fresh
    for i in range(8):
        dkv[0, i] = total[256 * i : 256 * i + 128]
        dkv[1, i] = total[256 * i + 128 : 256 * i + 256]


def attend_back(kv, q, dctx, lse, low, high):
    sds = jax.ShapeDtypeStruct
    return local_call(
        attend_back_kernel,
        (sds((8, 128, 128), BF16), sds((2, 8, 128, 128), F32)),
        wholes(kv, q, dctx, lse, low, high),
        "attend_back",
        [pltpu.VMEM((2048, 128), F32)],
    )(kv, q, dctx, lse, low, high)


def in_quarters(value, ref):
    for t in range(4):
        ref[t] = value[:, 256 * t : 256 * (t + 1)].astype(BF16)


def feed_kernel(ctx_in, h2, dense, expand, shrink, bias, u, act, ctx, part):
    lane = lax.broadcasted_iota(jnp.int32, (128, 128), 1)
    for m in range(2):
        for h in range(2):
            left = pltpu.roll(ctx_in[m * 4 + 2 * h].astype(F32), 64, axis=1)
            right = ctx_in[m * 4 + 2 * h + 1].astype(F32)
            ctx[m * 128 : (m + 1) * 128, 128 * h : 128 * (h + 1)] = jnp.where(
                lane < 64, left, right
            ).astype(BF16)
    inner = dot(h2[...], expand[...], 1, 0) + bias[...]
    u[...] = inner
    act[...] = (0.5 * inner * (1.0 + lax.erf(inner * 0.7071067811865476))).astype(BF16)
    in_quarters(dot(ctx[...], dense[...], 1, 1) + dot(act[...], shrink[...], 1, 1), part)


def feed(ctx_in, h2, gathered, bias):
    sds = jax.ShapeDtypeStruct
    return local_call(
        feed_kernel,
        (
            sds((256, 1024), F32),
            sds((256, 1024), BF16),
            sds((256, 256), BF16),
            sds((4, 256, 256), BF16),
        ),
        wholes(ctx_in, h2) + [columns(256, 3), columns(1024, 1), columns(1024, 2)] + wholes(bias),
        "feed",
    )(ctx_in, h2, gathered, gathered, gathered, bias)


def feed_back_kernel(
    grad, x, g2, u, act, ctx, h2, dense, expand, shrink, dctx, wgrad, z2, small
):
    gb = grad[...].astype(BF16)
    dact = dot(gb, shrink[...], 1, 0)
    inner = u[...]
    slope = 0.5 * (1.0 + lax.erf(inner * 0.7071067811865476)) + inner * (
        0.3989422804014327 * jnp.exp(-0.5 * inner * inner)
    )
    du = (dact * slope).astype(BF16)
    dc = dot(gb, dense[...], 1, 0)
    lane = lax.broadcasted_iota(jnp.int32, (128, 128), 1)
    for m in range(2):
        for h in range(4):
            piece = dc[m * 128 : (m + 1) * 128, 128 * (h // 2) : 128 * (h // 2 + 1)]
            if h % 2 == 0:
                piece = pltpu.roll(piece, 64, axis=1)
            dctx[m * 4 + h] = jnp.where(lane >= 64, piece, 0.0).astype(BF16)
    wgrad[:, 0:256] = dot(gb, ctx[...], 0, 0).astype(BF16)
    wgrad[:, 256:1280] = dot(h2[...], du, 0, 0).astype(BF16)
    wgrad[:, 1280:2304] = dot(gb, act[...], 0, 0).astype(BF16)
    dh2 = dot(du, expand[...], 1, 1)
    hat, _ = normal(x[...])
    z2[...] = dh2 * g2[...]
    small[0:1] = jnp.sum(dh2 * hat, axis=0, keepdims=True)
    small[1:2] = jnp.sum(dh2, axis=0, keepdims=True)
    small[2:3] = jnp.sum(gb.astype(F32), axis=0, keepdims=True)
    small[3:4] = jnp.sum(du.astype(F32), axis=0, keepdims=True)


def feed_back(grad, x, g2, u, act, ctx, h2, gathered):
    sds = jax.ShapeDtypeStruct
    return local_call(
        feed_back_kernel,
        (
            sds((8, 128, 128), BF16),
            sds((1024, 2304), BF16),
            sds((256, 1024), F32),
            sds((4, 1024), F32),
        ),
        wholes(grad, x, g2, u, act, ctx, h2)
        + [columns(256, 3), columns(1024, 1), columns(1024, 2)],
        "feed_back",
    )(grad, x, g2, u, act, ctx, h2, gathered, gathered, gathered)


def project_back_kernel(
    dq, dkv, cosine, sine, h1, weight, z2, x, g1, wgrad, part, small, bias_grad, dproj
):
    cos, sin = cosine[...], -sine[...]
    lane = lax.broadcasted_iota(jnp.int32, (128, 128), 1)
    for m in range(2):
        rows = pl.ds(m * 128, 128)
        for h in range(4):
            dproj[rows, 128 * h : 128 * (h + 1)] = turned(
                dkv[m * 4 + h].astype(F32), cos, sin
            ).astype(BF16)
        for h in range(2):
            left = turned(dq[m * 4 + 2 * h].astype(F32), cos, sin)
            right = turned(dq[m * 4 + 2 * h + 1].astype(F32), cos, sin)
            dproj[rows, 512 + 128 * h : 640 + 128 * h] = jnp.where(
                lane < 64, left, pltpu.roll(right, 64, axis=1)
            ).astype(BF16)
    dp = dproj[...]
    wgrad[...] = dot(h1[...], dp, 0, 0).astype(BF16)
    bias_grad[...] = jnp.sum(dp.astype(F32), axis=0, keepdims=True)
    dh1 = dot(dp, weight[...], 1, 1)
    hat, _ = normal(x[...])
    small[0:1] = jnp.sum(dh1 * hat, axis=0, keepdims=True)
    small[1:2] = jnp.sum(dh1, axis=0, keepdims=True)
    in_quarters(dh1 * g1[...] + z2[...], part)


def project_back(dq, dkv, cosine, sine, h1, gathered, z2, x, g1):
    sds = jax.ShapeDtypeStruct
    return local_call(
        project_back_kernel,
        (
            sds((1024, 768), BF16),
            sds((4, 256, 256), BF16),
            sds((2, 1024), F32),
            sds((1, 768), F32),
        ),
        wholes(dq, dkv, cosine, sine, h1) + [columns(768, 0)] + wholes(z2, x, g1),
        "project_back",
        [pltpu.VMEM((256, 768), BF16)],
    )(dq, dkv, cosine, sine, h1, gathered, z2, x, g1)


def head_order(value):
    lead = value.shape[:-1]
    parts = value.reshape(*lead, 4, 3, HEAD)
    keys = parts[..., 1:3, :].reshape(*lead, 512)
    return jnp.concatenate([keys, parts[..., 0, :].reshape(*lead, 256)], axis=-1)


def head_order_back(value):
    lead = value.shape[:-1]
    keys = value[..., :512].reshape(*lead, 4, 2, HEAD)
    queries = value[..., 512:].reshape(*lead, 4, 1, HEAD)
    return jnp.concatenate([queries, keys], axis=-2).reshape(*lead, 768)


def from_quarters(value):
    return value.transpose(1, 0, 2).reshape(256, 1024).astype(F32)


def local(
    hidden_in,
    document_ids,
    first_gain,
    first_shift,
    second_gain,
    second_shift,
    attn_weight,
    attn_bias,
    dense_weight,
    dense_bias,
    expand_weight,
    expand_bias,
    shrink_weight,
    shrink_bias,
    output_grad,
):
    seq_at = lax.axis_index("seq")
    chip, core = seq_at // 2, lax.rem(seq_at, 2)
    unit_micro = chip // 4
    lead = jnp.arange(ROT // 2, dtype=F32) * 2
    inverse = 10000.0 ** (-lead / ROT)
    place = (seq_at * 128 + jnp.arange(128, dtype=jnp.int32)).astype(F32)
    angles = place[:, None] * inverse[None, :]
    cos, sin = jnp.cos(angles), jnp.sin(angles)
    ones, zeros = jnp.ones((128, 112), F32), jnp.zeros((128, 112), F32)
    cosine = jnp.concatenate([cos, cos, ones], axis=1)
    sine = jnp.concatenate([-sin, sin, zeros], axis=1)

    idents = lax.all_gather(document_ids, "seq", axis=2, tiled=True)
    mine = lax.dynamic_index_in_dim(idents[:, 0], unit_micro, 0, keepdims=False)
    count0 = jnp.sum((mine == 0).astype(jnp.int32))
    count1 = jnp.sum((mine == 1).astype(jnp.int32))
    start = jnp.where(mine == 0, 0, jnp.where(mine == 1, count0, count0 + count1))
    high = jnp.arange(2048, dtype=jnp.int32).reshape(8, 2, 128)
    high = lax.dynamic_index_in_dim(high, core, 1, keepdims=False)[..., None]
    low = lax.dynamic_index_in_dim(start.reshape(8, 2, 128), core, 1, keepdims=False)[..., None]

    shards = jnp.concatenate(
        [
            head_order(attn_weight),
            jnp.swapaxes(dense_weight, 1, 2),
            expand_weight,
            jnp.swapaxes(shrink_weight, 1, 2),
        ],
        axis=2,
    )
    weights = [gather_weights(shards[layer]) for layer in range(LAYERS)]
    bias_order = head_order(attn_bias)

    x = hidden_in.reshape(256, 1024)
    kept = []
    for layer in range(LAYERS):
        row = slice(layer, layer + 1)
        h1, h2, qkv = project(
            x,
            first_gain[row],
            first_shift[row],
            second_gain[row],
            second_shift[row],
            bias_order[row],
            weights[layer],
            cosine,
            sine,
        )
        kv, q = heads_out(qkv)
        ctx_out, lse = attend(kv, q, low, high)
        ctx_in = swap_chips(ctx_out)
        u, act, ctx, part = feed(ctx_in, h2, weights[layer], expand_bias[row])
        kept.append((x, h1, h2, kv, q, lse, u, act, ctx))
        x = x + from_quarters(tensor_sum(part)) + dense_bias[row] + shrink_bias[row]
    hidden_out = x.reshape(2, 1, 128, 1024)

    grad = output_grad.reshape(256, 1024)
    wide, narrow, by_all, by_rows = [None] * 2, [None] * 2, [None] * 2, [None] * 2
    for layer in reversed(range(LAYERS)):
        row = slice(layer, layer + 1)
        x, h1, h2, kv, q, lse, u, act, ctx = kept[layer]
        dctx, wide[layer], z2, small2 = feed_back(
            grad, x, second_gain[row], u, act, ctx, h2, weights[layer]
        )
        dctx_in = swap_chips(dctx)
        dq, dkv = attend_back(kv, q, dctx_in, lse, low, high)
        dq_in, dkv_in = heads_back(dq, dkv)
        narrow[layer], part, small1, bias_grad = project_back(
            dq_in, dkv_in, cosine, sine, h1, weights[layer], z2, x, first_gain[row]
        )
        z = from_quarters(tensor_sum(part))
        hat, rstd = normal(x)
        grad = grad + rstd * (
            z
            - jnp.mean(z, axis=-1, keepdims=True)
            - hat * jnp.mean(z * hat, axis=-1, keepdims=True)
        )
        by_all[layer] = jnp.concatenate([small1, small2[:2]], axis=0)
        by_rows[layer] = jnp.concatenate([bias_grad[0], small2[2], small2[3]], axis=0)
    input_grad = grad.reshape(2, 1, 128, 1024)

    sums = scatter_sum([narrow[0], narrow[1], wide[0], wide[1]])
    narrow_sum = head_order_back(jnp.stack(sums[:2]))
    wide_sum = jnp.stack(sums[2:])
    norms = lax.psum(jnp.stack(by_all), ("batch", "seq", "tensor"))
    rows = lax.psum(jnp.stack(by_rows), ("batch", "seq"))
    branch_bias = rows[:, 768:1792]
    return (
        hidden_out,
        input_grad,
        norms[:, 0],
        norms[:, 1],
        norms[:, 2],
        norms[:, 3],
        narrow_sum,
        head_order_back(rows[:, :768]),
        jnp.swapaxes(wide_sum[..., :256], 1, 2),
        branch_bias,
        wide_sum[..., 256:1280],
        rows[:, 1792:],
        jnp.swapaxes(wide_sum[..., 1280:], 1, 2),
        branch_bias,
    )


def solution(mesh):
    rows, spread, split = P(None, "batch", "seq", None), P(None, ("batch", "seq"), "tensor"), P(
        None, "tensor"
    )
    across = P(None, "tensor", ("batch", "seq"))
    return jax.shard_map(
        local,
        mesh=mesh,
        in_specs=(
            rows,
            P(None, "batch", "seq"),
            P(),
            P(),
            P(),
            P(),
            spread,
            split,
            across,
            P(),
            spread,
            split,
            across,
            P(),
            rows,
        ),
        out_specs=(
            rows,
            rows,
            P(),
            P(),
            P(),
            P(),
            spread,
            split,
            across,
            P(),
            spread,
            split,
            across,
            P(),
        ),
        check_vma=False,
    )
```

```python
import functools

import jax
import jax.numpy as jnp
from jax import lax
from jax.experimental import pallas as pl
from jax.experimental.pallas import tpu as pltpu
from jax.sharding import PartitionSpec as P

HEAD = 64
ROT = 16
LAYERS = 2
MASKED = -1000000000.0
MESH = pl.DeviceIdType.MESH
F32, BF16 = jnp.float32, jnp.bfloat16
VLIM = 56 * 1024 * 1024


def dot(a, b, ca, cb):
    return lax.dot_general(a, b, (((ca,), (cb,)), ((), ())), preferred_element_type=F32)


def places():
    s = lax.axis_index("seq")
    return s, s // 2, lax.rem(s, 2)


def greet(peers):
    barrier = pltpu.get_barrier_semaphore()
    for peer in peers:
        pl.semaphore_signal(barrier, inc=1, device_id=peer, device_id_type=MESH)
    pl.semaphore_wait(barrier, len(peers))


def remote(src, dst, send, recv, peer):
    return pltpu.make_async_remote_copy(
        src_ref=src, dst_ref=dst, send_sem=send, recv_sem=recv, device_id=peer, device_id_type=MESH
    )


def chip_peers():
    _, c, k = places()
    return [{"seq": lax.rem(c + d, 8) * 2 + k} for d in range(1, 8)]


def comm_call(body, out_shape, scratch, ident, in_space, out_space, n_in, name):
    single = not isinstance(out_shape, (tuple, list))
    return pl.pallas_call(
        body,
        out_shape=out_shape,
        in_specs=[pl.BlockSpec(memory_space=in_space)] * n_in,
        out_specs=pl.BlockSpec(memory_space=out_space)
        if single
        else [pl.BlockSpec(memory_space=out_space)] * len(out_shape),
        scratch_shapes=scratch,
        compiler_params=pltpu.CompilerParams(
            collective_id=ident, has_side_effects=True, vmem_limit_bytes=VLIM
        ),
        name=name,
    )


class Spot:
    def __init__(self):
        b = lax.axis_index("batch")
        s, c, self.core = places()
        self.pos = (lax.rem(c, 4), (c // 4) * 2 + b)
        self.partner = {"seq": s + 1 - 2 * self.core}

    def ring(self, r):
        k = self.core
        return [r, lax.rem(r + 3 - 2 * k, 4), lax.rem(r + 1 + 2 * k, 4), lax.rem(r + 2, 4)]

    def device(self, x, y):
        return {"batch": lax.rem(y, 2), "seq": ((y // 2) * 4 + x) * 2 + self.core}

    def neighbours(self):
        x, y = self.pos
        xs, ys = self.ring(x), self.ring(y)
        return [self.device(x2, y) for x2 in xs[1:3]] + [self.device(x, y2) for y2 in ys[1:3]]


def flat(x, y):
    return lax.rem(y, 2) * 8 + (y // 2) * 4 + x


def drive(jobs):
    jobs = list(jobs)
    while jobs:
        for job in list(jobs):
            try:
                next(job)
            except StopIteration:
                jobs.remove(job)


def ring_gather(spot, src, out, first, ss, rs, fs, fr, ls):
    k = spot.core
    along, other = spot.ring(spot.pos[first]), spot.ring(spot.pos[1 - first])

    def place(i, j):
        at = (along[i], other[j])
        return at if first == 0 else at[::-1]

    def slot(i, j):
        return out.at[flat(*place(i, j)), k]

    sent, passed = [], []

    def send(i, j, idx, to):
        piece = slot(i, j)
        copy = remote(src if (i, j) == (0, 0) else piece, piece, ss.at[idx], rs.at[idx], to)
        copy.start()
        sent.append(copy)
        return copy

    def share(i, j):
        piece, idx = slot(i, j), 4 * i + j
        copy = remote(
            src if idx == 0 else piece, piece, fs.at[idx], fr.at[idx], spot.partner
        )
        copy.start()
        passed.append(copy)

    ahead1, behind1 = spot.device(*place(2, 0)), spot.device(*place(1, 0))
    ahead2, behind2 = spot.device(*place(0, 2)), spot.device(*place(0, 1))
    own = pltpu.make_async_copy(src, slot(0, 0), ls)
    own.start()
    m0 = send(0, 0, 0, ahead1)
    m1 = send(0, 0, 1, behind1)

    def second(i):
        return send(i, 0, 3 + 3 * i, ahead2), send(i, 0, 4 + 3 * i, behind2)

    n = {0: second(0)}
    share(0, 0)
    yield
    m0.wait_recv()
    m2 = send(1, 0, 2, ahead1)
    n[1] = second(1)
    share(1, 0)
    yield
    m1.wait_recv()
    n[2] = second(2)
    share(2, 0)
    yield
    far = {}

    def middle(i):
        n[i][0].wait_recv()
        far[i] = send(i, 1, 5 + 3 * i, ahead2)
        share(i, 1)
        n[i][1].wait_recv()
        share(i, 2)

    middle(0)
    yield
    m2.wait_recv()
    n[3] = second(3)
    share(3, 0)
    yield
    for i in range(1, 4):
        middle(i)
        yield
    for i in range(4):
        far[i].wait_recv()
        share(i, 3)
        yield
    own.wait()
    for copy in sent:
        copy.wait_send()
    for copy in passed:
        copy.wait()


def gather_sems():
    dma = pltpu.SemaphoreType.DMA
    return [dma((15,)), dma((15,)), dma((16,)), dma((16,)), dma(())]


def gather_kernel(firsts, *refs):
    count = len(firsts)
    srcs, outs, sems = refs[:count], refs[count : 2 * count], refs[2 * count :]
    spot = Spot()
    greet(spot.neighbours() + [spot.partner])
    drive(
        ring_gather(spot, srcs[a], outs[a], firsts[a], *sems[5 * a : 5 * a + 5])
        for a in range(count)
    )


def gather_plane(arrays, firsts, ident):
    count = len(arrays)
    return comm_call(
        functools.partial(gather_kernel, firsts),
        tuple(jax.ShapeDtypeStruct((16, 2, *a.shape), a.dtype) for a in arrays),
        [sem for _ in arrays for sem in gather_sems()],
        ident,
        pl.ANY,
        pl.ANY,
        count,
        "gather_plane",
    )(*arrays)


def heads_out_kernel(src, kv_out, q_out, ssem, rsem, fs, fr, lsem):
    s, c, k = places()
    partner = {"seq": s + 1 - 2 * k}
    others = chip_peers()
    greet(others + [partner])
    copies = []
    for d, peer in enumerate(others):
        c2 = lax.rem(c + d + 1, 8)
        copies.append(
            remote(src.at[c2, 0], kv_out.at[s], ssem.at[0, d], rsem.at[0, d], peer)
        )
        copies[-1].start()
    copies_q = []
    for d, peer in enumerate(others):
        c2 = lax.rem(c + d + 1, 8)
        copies_q.append(
            remote(src.at[c2, 1], q_out.at[c], ssem.at[1, d], rsem.at[1, d], peer)
        )
        copies_q[-1].start()
    onward = [remote(src.at[c, 0], kv_out.at[s], fs.at[0], fr.at[0], partner)]
    onward[0].start()
    own_kv = pltpu.make_async_copy(src.at[c, 0], kv_out.at[s], lsem.at[0])
    own_q = pltpu.make_async_copy(src.at[c, 1], q_out.at[c], lsem.at[1])
    own_kv.start()
    own_q.start()
    for d in range(1, 8):
        copies[d - 1].wait_recv()
        at = kv_out.at[lax.rem(c - d + 8, 8) * 2 + k]
        copy = remote(at, at, fs.at[d], fr.at[d], partner)
        copy.start()
        onward.append(copy)
    own_kv.wait()
    own_q.wait()
    for copy in copies:
        copy.wait_send()
    for copy in copies_q:
        copy.wait()
    for copy in onward:
        copy.wait()


def heads_out(qkv):
    dma = pltpu.SemaphoreType.DMA
    return comm_call(
        heads_out_kernel,
        (
            jax.ShapeDtypeStruct((16, 128, 128), BF16),
            jax.ShapeDtypeStruct((8, 128, 128), BF16),
        ),
        [dma((2, 7)), dma((2, 7)), dma((8,)), dma((8,)), dma((2,))],
        2,
        pl.ANY,
        pl.ANY,
        1,
        "heads_out",
    )(qkv)


def swap_kernel(src, out, ssem, rsem, lsem):
    _, c, _ = places()
    others = chip_peers()
    greet(others)
    copies = []
    for d, peer in enumerate(others):
        c2 = lax.rem(c + d + 1, 8)
        copies.append(remote(src.at[c2], out.at[c], ssem.at[d], rsem.at[d], peer))
        copies[-1].start()
    own = pltpu.make_async_copy(src.at[c], out.at[c], lsem)
    own.start()
    own.wait()
    for copy in copies:
        copy.wait()


def swap_chips(blocks):
    dma = pltpu.SemaphoreType.DMA
    return comm_call(
        swap_kernel,
        jax.ShapeDtypeStruct(blocks.shape, blocks.dtype),
        [dma((7,)), dma((7,)), dma(())],
        3,
        pl.ANY,
        pl.ANY,
        1,
        "swap_chips",
    )(blocks)


def heads_back_kernel(dq, dkv, dq_out, dkv_out, other, total, ssem, rsem, psem, lsem):
    s, c, k = places()
    partner = {"seq": s + 1 - 2 * k}
    others = chip_peers()
    greet(others + [partner])
    theirs = remote(dkv.at[1 - k], other, psem.at[0], psem.at[1], partner)
    theirs.start()
    copies = []
    for d, peer in enumerate(others):
        c2 = lax.rem(c + d + 1, 8)
        copies.append(remote(dq.at[c2], dq_out.at[c], ssem.at[0, d], rsem.at[0, d], peer))
        copies[-1].start()
    own_q = pltpu.make_async_copy(dq.at[c], dq_out.at[c], lsem)
    own_q.start()
    theirs.wait()
    total[...] = (dkv[k] + other[...]).astype(BF16)
    for d, peer in enumerate(others):
        c2 = lax.rem(c + d + 1, 8)
        copies.append(
            remote(total.at[c2], dkv_out.at[c], ssem.at[1, d], rsem.at[1, d], peer)
        )
        copies[-1].start()
    own_q.wait()
    own_kv = pltpu.make_async_copy(total.at[c], dkv_out.at[c], lsem)
    own_kv.start()
    own_kv.wait()
    for copy in copies:
        copy.wait()


def heads_back(dq, dkv):
    dma = pltpu.SemaphoreType.DMA
    shape = jax.ShapeDtypeStruct((8, 128, 128), BF16)
    return comm_call(
        heads_back_kernel,
        (shape, shape),
        [
            pltpu.VMEM((8, 128, 128), F32),
            pltpu.VMEM((8, 128, 128), BF16),
            dma((2, 7)),
            dma((2, 7)),
            dma((2,)),
            dma(()),
        ],
        4,
        pltpu.VMEM,
        pltpu.VMEM,
        2,
        "heads_back",
    )(dq, dkv)


def ring_sum(spot, part, out, rows, buf, held, ss, rs):
    t, behind, ahead, across = spot.ring(lax.axis_index("tensor"))
    to_ahead, to_behind = {"tensor": ahead}, {"tensor": behind}
    sent = []

    def send(src, dst, idx, to):
        copy = remote(src, dst, ss.at[idx], rs.at[idx], to)
        copy.start()
        sent.append(copy)
        return copy

    far = send(part.at[across, rows], buf.at[0, rows], 0, to_ahead)
    back = send(part.at[behind, rows], buf.at[2, rows], 2, to_behind)
    yield
    far.wait_recv()
    held[rows] = (part[ahead, rows].astype(F32) + buf[0, rows].astype(F32)).astype(BF16)
    on = send(held.at[rows], buf.at[1, rows], 1, to_ahead)
    yield
    back.wait_recv()
    on.wait_recv()
    total = part[t, rows].astype(F32) + buf[1, rows].astype(F32) + buf[2, rows].astype(F32)
    out[t, rows] = total.astype(BF16)
    mine, theirs = out.at[t, rows], out.at[behind, rows]
    first = send(mine, mine, 3, to_ahead)
    second = send(mine, mine, 4, to_behind)
    yield
    first.wait_recv()
    third = send(theirs, theirs, 5, to_ahead)
    yield
    second.wait_recv()
    third.wait_recv()
    for copy in sent:
        copy.wait_send()


def direct_sum(vec, vec_out, got, ss, rs):
    t = lax.axis_index("tensor")
    copies = []
    for d in range(3):
        to = {"tensor": lax.rem(t + d + 1, 4)}
        copies.append(remote(vec, got.at[t], ss.at[d], rs.at[d], to))
        copies[-1].start()
    got[t] = vec[...]
    yield
    yield
    yield
    for copy in copies:
        copy.wait()
    vec_out[...] = (got[0] + got[1]) + (got[2] + got[3])


def tensor_sum_kernel(count, *refs):
    (part, *vec), (out, *vec_out) = refs[: 1 + count], refs[1 + count : 2 + 2 * count]
    buf, held, s0, r0, s1, r1, *rest = refs[2 + 2 * count :]
    spot = Spot()
    t = lax.axis_index("tensor")
    greet([{"tensor": lax.rem(t + d, 4)} for d in range(1, 4)])
    jobs = [
        ring_sum(spot, part, out, pl.ds(0, 128), buf, held, s0, r0),
        ring_sum(spot, part, out, pl.ds(128, 128), buf, held, s1, r1),
    ]
    if count:
        jobs.append(direct_sum(vec[0], vec_out[0], *rest))
    drive(jobs)


def tensor_sum(part, vec=None):
    dma = pltpu.SemaphoreType.DMA
    count = 0 if vec is None else 1
    shape = jax.ShapeDtypeStruct(part.shape, BF16)
    scratch = [
        pltpu.VMEM((3, *part.shape[1:]), BF16),
        pltpu.VMEM(part.shape[1:], BF16),
    ] + [dma((6,))] * 4
    if vec is not None:
        scratch += [pltpu.VMEM((4, *vec.shape), F32), dma((3,)), dma((3,))]
    return comm_call(
        functools.partial(tensor_sum_kernel, count),
        (shape,) if vec is None else (shape, jax.ShapeDtypeStruct(vec.shape, F32)),
        scratch,
        5 + 2 * count,
        pltpu.VMEM,
        pltpu.VMEM,
        1 + count,
        "tensor_sum",
    )(*((part,) if vec is None else (part, vec)))


def ring_scatter(spot, src, out, first, pair, left, got, ps, pr, ss, rs):
    k = spot.core
    along, other = spot.ring(spot.pos[first]), spot.ring(spot.pos[1 - first])
    kind = pair.dtype

    def place(i, j):
        at = (along[i], other[j])
        return at if first == 0 else at[::-1]

    order = (3, 2, 1, 0)
    theirs = (0, 2, 1, 3)
    pairs, sent = {}, []
    for i in order:
        for j in order:
            at = flat(*place(theirs[i], theirs[j]))
            idx = 4 * i + j
            copy = remote(src.at[at, 1 - k], pair.at[idx], ps.at[idx], pr.at[idx], spot.partner)
            copy.start()
            pairs[idx] = copy
    yield

    def both(i, j):
        pairs[4 * i + j].wait_recv()
        return src[flat(*place(i, j)), k].astype(F32) + pair[4 * i + j].astype(F32)

    def send(value, idx, to):
        left[idx] = value.astype(kind)
        copy = remote(left.at[idx], got.at[idx], ss.at[idx], rs.at[idx], to)
        copy.start()
        sent.append(copy)
        return copy

    ahead1, behind1 = spot.device(*place(2, 0)), spot.device(*place(1, 0))
    ahead2, behind2 = spot.device(*place(0, 2)), spot.device(*place(0, 1))
    far, on, back = {}, {}, {}
    for j in order:
        far[j] = send(both(3, j), j, ahead1)
        back[j] = send(both(1, j), 8 + j, behind1)
        yield
    for j in order:
        far[j].wait_recv()
        on[j] = send(both(2, j) + got[j].astype(F32), 4 + j, ahead1)
        yield

    def settled(j):
        on[j].wait_recv()
        back[j].wait_recv()
        return both(0, j) + got[4 + j].astype(F32) + got[8 + j].astype(F32)

    far2 = send(settled(3), 12, ahead2)
    yield
    ready = settled(2)
    back2 = send(settled(1), 14, behind2)
    yield
    far2.wait_recv()
    on2 = send(ready + got[12].astype(F32), 13, ahead2)
    total = settled(0)
    yield
    back2.wait_recv()
    total = total + got[14].astype(F32)
    on2.wait_recv()
    out[...] = total + got[13].astype(F32)
    for copy in pairs.values():
        copy.wait_send()
    for copy in sent:
        copy.wait_send()


def small_total(scatter, gather):
    yield from scatter
    yield from gather()


def scatter_kernel(count, *refs):
    ins, outs = refs[: count + 1], refs[count + 1 : 2 * count + 2]
    rest = refs[2 * count + 2 :]
    spot = Spot()
    greet(spot.neighbours() + [spot.partner])
    args = [rest[7 * a : 7 * a + 7] for a in range(count + 1)]
    jobs = [
        ring_scatter(spot, ins[a], outs[a], (a + 1) % 2, *args[a]) for a in range(count)
    ]
    piece, *sems = rest[7 * count + 7 :]
    small = ring_scatter(spot, ins[count], piece, 0, *args[count])
    jobs.append(
        small_total(small, lambda: ring_gather(spot, piece, outs[count], 0, *sems))
    )
    drive(jobs)


def scatter_sum(arrays, small):
    dma = pltpu.SemaphoreType.DMA
    ins = [a.reshape(16, 2, 32, a.shape[1]) for a in arrays] + [small]
    scratch = []
    for a in ins:
        scratch += [
            pltpu.VMEM((16, *a.shape[2:]), a.dtype),
            pltpu.VMEM((15, *a.shape[2:]), a.dtype),
            pltpu.VMEM((15, *a.shape[2:]), a.dtype),
            dma((16,)),
            dma((16,)),
            dma((15,)),
            dma((15,)),
        ]
    return comm_call(
        functools.partial(scatter_kernel, len(arrays)),
        tuple(jax.ShapeDtypeStruct(a.shape[2:], F32) for a in ins[:-1])
        + (jax.ShapeDtypeStruct(small.shape, F32),),
        scratch + [pltpu.VMEM(small.shape[2:], F32)] + gather_sems(),
        6,
        pltpu.VMEM,
        pltpu.VMEM,
        len(ins),
        "scatter_sum",
    )(*ins)


def turned(values, cosine, sine):
    lane = lax.broadcasted_iota(jnp.int32, values.shape, 1)
    swapped = jnp.where(
        lane < 8, pltpu.roll(values, 120, axis=1), pltpu.roll(values, 8, axis=1)
    )
    return values * cosine + swapped * sine


def normal(values):
    centred = values - jnp.mean(values, axis=-1, keepdims=True)
    rstd = lax.rsqrt(jnp.mean(centred * centred, axis=-1, keepdims=True) + 1e-05)
    return centred * rstd, rstd


def with_branch(x, branch, shift, out):
    for t in range(4):
        at = slice(256 * t, 256 * (t + 1))
        out[:, at] = x[:, at] + branch[t].astype(F32) + shift[:, at]


def norm_back(grad, z, x, out):
    hat, rstd = normal(x[...])
    flow = jnp.concatenate([z[t].astype(F32) for t in range(4)], axis=1)
    out[...] = grad[...] + rstd * (
        flow
        - jnp.mean(flow, axis=-1, keepdims=True)
        - hat * jnp.mean(flow * hat, axis=-1, keepdims=True)
    )


def project_kernel(*refs):
    if len(refs) == 15:
        x, branch, shift, *rest, x_out = refs
        with_branch(x, branch, shift, x_out)
        project_rows(x_out, *rest)
    else:
        project_rows(*refs)


def project_rows(x, g1, b1, g2, b2, bias, weight, cosine, sine, h1, h2, qkv):
    hat, _ = normal(x[...])
    h1[...] = (hat * g1[...] + b1[...]).astype(BF16)
    h2[...] = (hat * g2[...] + b2[...]).astype(BF16)
    proj = dot(h1[...], weight[...], 1, 0) + bias[...]
    cos, sin = cosine[...], sine[...]
    lane = lax.broadcasted_iota(jnp.int32, (128, 128), 1)
    for m in range(2):
        rows = proj[m * 128 : (m + 1) * 128]
        for h in range(4):
            pair = rows[:, 128 * h : 128 * (h + 1)]
            qkv[m * 4 + h, 0] = turned(pair, cos, sin).astype(BF16)
            q = rows[:, 512 + 128 * (h // 2) : 640 + 128 * (h // 2)]
            if h % 2:
                q = pltpu.roll(q, 64, axis=1)
            q = turned(q, cos, sin) * 0.125
            qkv[m * 4 + h, 1] = jnp.where(lane < 64, q, 0.0).astype(BF16)


def local_call(body, out_shape, in_specs, name, scratch=()):
    return pl.pallas_call(
        body,
        out_shape=out_shape,
        grid=(1,),
        in_specs=in_specs,
        out_specs=jax.tree.map(lambda o: whole(o.shape), out_shape),
        scratch_shapes=scratch,
        compiler_params=pltpu.CompilerParams(vmem_limit_bytes=VLIM),
        name=name,
    )


def whole(shape):
    return pl.BlockSpec(shape, lambda i: (0,) * len(shape))


def columns(width, at):
    return pl.BlockSpec((1024, width), lambda i: (0, at))


def wholes(*arrays):
    return [whole(a.shape) for a in arrays]


def project(x, g1, b1, g2, b2, bias, gathered, cosine, sine, branch=None, shift=None):
    sds = jax.ShapeDtypeStruct
    more = () if branch is None else (branch, shift)
    return local_call(
        project_kernel,
        (
            sds((256, 1024), BF16),
            sds((256, 1024), BF16),
            sds((8, 2, 128, 128), BF16),
        )
        + ((sds((256, 1024), F32),) if more else ()),
        wholes(x, *more, g1, b1, g2, b2, bias) + [columns(768, 0)] + wholes(cosine, sine),
        "project",
    )(x, *more, g1, b1, g2, b2, bias, gathered, cosine, sine)


def add_branch(x, branch, shift):
    return local_call(
        with_branch,
        jax.ShapeDtypeStruct(x.shape, F32),
        wholes(x, branch, shift),
        "add_branch",
    )(x, branch, shift)


def add_norm_back(grad, z, x):
    return local_call(
        norm_back,
        jax.ShapeDtypeStruct(grad.shape, F32),
        wholes(grad, z, x),
        "add_norm_back",
    )(grad, z, x)


def scores_of(q, keys, low, high):
    s = dot(q, keys, 1, 1)
    place = lax.broadcasted_iota(jnp.int32, s.shape, 1)
    return jnp.where((place >= low) & (place <= high), s, MASKED)


def attend_kernel(kv, q, low, high, ctx, lse):
    for i in range(8):
        n = 256 * (i + 1)
        keys = kv[0 : 2 * (i + 1)].reshape(n, 128)
        s = scores_of(q[i], keys, low[i], high[i])
        top = jnp.max(s, axis=-1, keepdims=True)
        e = jnp.exp(s - top)
        total = jnp.sum(e, axis=-1, keepdims=True)
        soft = (e * (1.0 / total)).astype(BF16)
        ctx[i] = dot(soft, keys, 1, 0).astype(BF16)
        lse[i] = top + jnp.log(total)


def attend(kv, q, low, high):
    sds = jax.ShapeDtypeStruct
    return local_call(
        attend_kernel,
        (sds((8, 128, 128), BF16), sds((8, 128, 1), F32)),
        wholes(kv, q, low, high),
        "attend",
    )(kv, q, low, high)


def attend_back_kernel(kv, q, dctx, lse, low, high, dq, dkv, total):
    for i in reversed(range(8)):
        n = 256 * (i + 1)
        keys = kv[0 : 2 * (i + 1)].reshape(n, 128)
        s = scores_of(q[i], keys, low[i], high[i])
        soft = jnp.exp(s - lse[i])
        dsoft = dot(dctx[i], keys, 1, 1)
        term = jnp.sum(soft * dsoft, axis=-1, keepdims=True)
        ds = (soft * (dsoft - term)).astype(BF16)
        dq[i] = (dot(ds, keys, 1, 0) * 0.125).astype(BF16)
        both = jnp.concatenate([ds, soft.astype(BF16)], axis=0)
        right = jnp.concatenate([q[i], dctx[i]], axis=0)
        fresh = dot(both, right, 0, 0)
        if i == 7:
            total[...] = fresh
        else:
            total[0:n] += fresh
    for i in range(8):
        dkv[0, i] = total[256 * i : 256 * i + 128]
        dkv[1, i] = total[256 * i + 128 : 256 * i + 256]


def attend_back(kv, q, dctx, lse, low, high):
    sds = jax.ShapeDtypeStruct
    return local_call(
        attend_back_kernel,
        (sds((8, 128, 128), BF16), sds((2, 8, 128, 128), F32)),
        wholes(kv, q, dctx, lse, low, high),
        "attend_back",
        [pltpu.VMEM((2048, 128), F32)],
    )(kv, q, dctx, lse, low, high)


def in_quarters(value, ref):
    for t in range(4):
        ref[t] = value[:, 256 * t : 256 * (t + 1)].astype(BF16)


def feed_kernel(ctx_in, h2, dense, expand, shrink, bias, u, act, ctx, part):
    lane = lax.broadcasted_iota(jnp.int32, (128, 128), 1)
    for m in range(2):
        for h in range(2):
            left = pltpu.roll(ctx_in[m * 4 + 2 * h].astype(F32), 64, axis=1)
            right = ctx_in[m * 4 + 2 * h + 1].astype(F32)
            ctx[m * 128 : (m + 1) * 128, 128 * h : 128 * (h + 1)] = jnp.where(
                lane < 64, left, right
            ).astype(BF16)
    inner = dot(h2[...], expand[...], 1, 0) + bias[...]
    u[...] = inner
    act[...] = (0.5 * inner * (1.0 + lax.erf(inner * 0.7071067811865476))).astype(BF16)
    in_quarters(dot(ctx[...], dense[...], 1, 1) + dot(act[...], shrink[...], 1, 1), part)


def feed(ctx_in, h2, gathered, bias):
    sds = jax.ShapeDtypeStruct
    return local_call(
        feed_kernel,
        (
            sds((256, 1024), F32),
            sds((256, 1024), BF16),
            sds((256, 256), BF16),
            sds((4, 256, 256), BF16),
        ),
        wholes(ctx_in, h2) + [columns(256, 3), columns(1024, 1), columns(1024, 2)] + wholes(bias),
        "feed",
    )(ctx_in, h2, gathered, gathered, gathered, bias)


def feed_back_kernel(*refs):
    if len(refs) == 17:
        before, z, x_before, *rest, grad = refs
        norm_back(before, z, x_before, grad)
        feed_back_rows(grad, *rest)
    else:
        feed_back_rows(*refs)


def feed_back_rows(
    grad, x, g2, u, act, ctx, h2, dense, expand, shrink, dctx, wgrad, z2, small
):
    gb = grad[...].astype(BF16)
    dact = dot(gb, shrink[...], 1, 0)
    inner = u[...]
    slope = 0.5 * (1.0 + lax.erf(inner * 0.7071067811865476)) + inner * (
        0.3989422804014327 * jnp.exp(-0.5 * inner * inner)
    )
    du = (dact * slope).astype(BF16)
    dc = dot(gb, dense[...], 1, 0)
    lane = lax.broadcasted_iota(jnp.int32, (128, 128), 1)
    for m in range(2):
        for h in range(4):
            piece = dc[m * 128 : (m + 1) * 128, 128 * (h // 2) : 128 * (h // 2 + 1)]
            if h % 2 == 0:
                piece = pltpu.roll(piece, 64, axis=1)
            dctx[m * 4 + h] = jnp.where(lane >= 64, piece, 0.0).astype(BF16)
    wgrad[:, 768:1024] = dot(gb, ctx[...], 0, 0).astype(BF16)
    wgrad[:, 1024:2048] = dot(h2[...], du, 0, 0).astype(BF16)
    wgrad[:, 2048:3072] = dot(gb, act[...], 0, 0).astype(BF16)
    dh2 = dot(du, expand[...], 1, 1)
    hat, _ = normal(x[...])
    z2[...] = dh2 * g2[...]
    small[0:1] = jnp.sum(dh2 * hat, axis=0, keepdims=True)
    small[1:2] = jnp.sum(dh2, axis=0, keepdims=True)
    small[2:3] = jnp.sum(gb.astype(F32), axis=0, keepdims=True)
    small[3:4] = jnp.sum(du.astype(F32), axis=0, keepdims=True)


def feed_back(grad, x, g2, u, act, ctx, h2, gathered, z=None, x_before=None):
    sds = jax.ShapeDtypeStruct
    more = () if z is None else (z, x_before)
    return local_call(
        feed_back_kernel,
        (
            sds((8, 128, 128), BF16),
            sds((1024, 3072), BF16),
            sds((256, 1024), F32),
            sds((4, 1024), F32),
        )
        + ((sds((256, 1024), F32),) if more else ()),
        wholes(grad, *more, x, g2, u, act, ctx, h2)
        + [columns(256, 3), columns(1024, 1), columns(1024, 2)],
        "feed_back",
    )(grad, *more, x, g2, u, act, ctx, h2, gathered, gathered, gathered)


def project_back_kernel(
    dq, dkv, cosine, sine, h1, weight, z2, x, g1, _, wgrad, part, small, bias_grad, dproj, narrow, sem
):
    cos, sin = cosine[...], -sine[...]
    lane = lax.broadcasted_iota(jnp.int32, (128, 128), 1)
    for m in range(2):
        rows = pl.ds(m * 128, 128)
        for h in range(4):
            dproj[rows, 128 * h : 128 * (h + 1)] = turned(
                dkv[m * 4 + h].astype(F32), cos, sin
            ).astype(BF16)
        for h in range(2):
            left = turned(dq[m * 4 + 2 * h].astype(F32), cos, sin)
            right = turned(dq[m * 4 + 2 * h + 1].astype(F32), cos, sin)
            dproj[rows, 512 + 128 * h : 640 + 128 * h] = jnp.where(
                lane < 64, left, pltpu.roll(right, 64, axis=1)
            ).astype(BF16)
    dp = dproj[...]
    narrow[...] = dot(h1[...], dp, 0, 0).astype(BF16)
    copy = pltpu.make_async_copy(narrow, wgrad.at[:, 0:768], sem)
    copy.start()
    bias_grad[...] = jnp.sum(dp.astype(F32), axis=0, keepdims=True)
    dh1 = dot(dp, weight[...], 1, 1)
    hat, _ = normal(x[...])
    small[0:1] = jnp.sum(dh1 * hat, axis=0, keepdims=True)
    small[1:2] = jnp.sum(dh1, axis=0, keepdims=True)
    in_quarters(dh1 * g1[...] + z2[...], part)
    copy.wait()


def project_back(dq, dkv, cosine, sine, h1, gathered, z2, x, g1, wgrad):
    sds = jax.ShapeDtypeStruct
    return pl.pallas_call(
        project_back_kernel,
        out_shape=(
            sds((1024, 3072), BF16),
            sds((4, 256, 256), BF16),
            sds((2, 1024), F32),
            sds((1, 768), F32),
        ),
        grid=(1,),
        in_specs=wholes(dq, dkv, cosine, sine, h1)
        + [columns(768, 0)]
        + wholes(z2, x, g1)
        + [pl.BlockSpec(memory_space=pl.ANY)],
        out_specs=(
            pl.BlockSpec(memory_space=pl.ANY),
            whole((4, 256, 256)),
            whole((2, 1024)),
            whole((1, 768)),
        ),
        scratch_shapes=[
            pltpu.VMEM((256, 768), BF16),
            pltpu.VMEM((1024, 768), BF16),
            pltpu.SemaphoreType.DMA(()),
        ],
        input_output_aliases={9: 0},
        compiler_params=pltpu.CompilerParams(vmem_limit_bytes=VLIM),
        name="project_back",
    )(dq, dkv, cosine, sine, h1, gathered, z2, x, g1, wgrad)


def head_order(value):
    lead = value.shape[:-1]
    parts = value.reshape(*lead, 4, 3, HEAD)
    keys = parts[..., 1:3, :].reshape(*lead, 512)
    return jnp.concatenate([keys, parts[..., 0, :].reshape(*lead, 256)], axis=-1)


def head_order_back(value):
    lead = value.shape[:-1]
    keys = value[..., :512].reshape(*lead, 4, 2, HEAD)
    queries = value[..., 512:].reshape(*lead, 4, 1, HEAD)
    return jnp.concatenate([queries, keys], axis=-2).reshape(*lead, 768)


def from_quarters(value):
    return value.transpose(1, 0, 2).reshape(256, 1024).astype(F32)


def local(
    hidden_in,
    document_ids,
    first_gain,
    first_shift,
    second_gain,
    second_shift,
    attn_weight,
    attn_bias,
    dense_weight,
    dense_bias,
    expand_weight,
    expand_bias,
    shrink_weight,
    shrink_bias,
    output_grad,
):
    seq_at = lax.axis_index("seq")
    chip, core = seq_at // 2, lax.rem(seq_at, 2)
    unit_micro = chip // 4
    lead = jnp.arange(ROT // 2, dtype=F32) * 2
    inverse = 10000.0 ** (-lead / ROT)
    place = (seq_at * 128 + jnp.arange(128, dtype=jnp.int32)).astype(F32)
    angles = place[:, None] * inverse[None, :]
    cos, sin = jnp.cos(angles), jnp.sin(angles)
    ones, zeros = jnp.ones((128, 112), F32), jnp.zeros((128, 112), F32)
    cosine = jnp.concatenate([cos, cos, ones], axis=1)
    sine = jnp.concatenate([-sin, sin, zeros], axis=1)

    shards = jnp.concatenate(
        [
            head_order(attn_weight),
            jnp.swapaxes(dense_weight, 1, 2),
            expand_weight,
            jnp.swapaxes(shrink_weight, 1, 2),
        ],
        axis=2,
    )
    idents = jnp.pad(document_ids[:, 0], ((0, 6), (0, 0)))
    early, late, idents = gather_plane([shards[0], shards[1], idents], (0, 1, 0), 1)
    weights = [early.reshape(1024, 3072), late.reshape(1024, 3072)]
    idents = idents.reshape(2, 16, 8, 128)
    idents = lax.dynamic_index_in_dim(idents, lax.axis_index("batch"), 0, keepdims=False)
    mine = lax.dynamic_index_in_dim(idents, unit_micro, 1, keepdims=False).reshape(2048)
    count0 = jnp.sum((mine == 0).astype(jnp.int32))
    count1 = jnp.sum((mine == 1).astype(jnp.int32))
    start = jnp.where(mine == 0, 0, jnp.where(mine == 1, count0, count0 + count1))
    high = jnp.arange(2048, dtype=jnp.int32).reshape(8, 2, 128)
    high = lax.dynamic_index_in_dim(high, core, 1, keepdims=False)[..., None]
    low = lax.dynamic_index_in_dim(start.reshape(8, 2, 128), core, 1, keepdims=False)[..., None]
    bias_order = head_order(attn_bias)

    x = hidden_in.reshape(256, 1024)
    shift = dense_bias + shrink_bias
    kept = []
    branch = ()
    for layer in range(LAYERS):
        row = slice(layer, layer + 1)
        h1, h2, qkv, *fresh = project(
            x,
            first_gain[row],
            first_shift[row],
            second_gain[row],
            second_shift[row],
            bias_order[row],
            weights[layer],
            cosine,
            sine,
            *branch,
        )
        x = fresh[0] if fresh else x
        kv, q = heads_out(qkv)
        ctx_out, lse = attend(kv, q, low, high)
        ctx_in = swap_chips(ctx_out)
        u, act, ctx, part = feed(ctx_in, h2, weights[layer], expand_bias[row])
        kept.append((x, h1, h2, kv, q, lse, u, act, ctx))
        branch = (tensor_sum(part)[0], shift[row])
    hidden_out = add_branch(x, *branch).reshape(2, 1, 128, 1024)

    grad = output_grad.reshape(256, 1024)
    wgrads, by_all, by_rows = [None] * 2, [None] * 2, [None] * 2
    before = ()
    for layer in reversed(range(LAYERS)):
        row = slice(layer, layer + 1)
        x, h1, h2, kv, q, lse, u, act, ctx = kept[layer]
        dctx, wgrad, z2, small2, *fresh = feed_back(
            grad, x, second_gain[row], u, act, ctx, h2, weights[layer], *before
        )
        grad = fresh[0] if fresh else grad
        dctx_in = swap_chips(dctx)
        dq, dkv = attend_back(kv, q, dctx_in, lse, low, high)
        dq_in, dkv_in = heads_back(dq, dkv)
        wgrads[layer], part, small1, bias_grad = project_back(
            dq_in, dkv_in, cosine, sine, h1, weights[layer], z2, x, first_gain[row], wgrad
        )
        z, by_all[layer] = tensor_sum(part, jnp.concatenate([small1, small2[:2]], axis=0))
        before = (z, x)
        by_rows[layer] = jnp.concatenate([bias_grad[0], small2[2], small2[3]], axis=0)
    input_grad = add_norm_back(grad, *before).reshape(2, 1, 128, 1024)

    small = jnp.concatenate([v.reshape(-1) for v in by_all + by_rows]).reshape(32, 432)
    small = jnp.pad(small, ((0, 0), (0, 592))).reshape(16, 2, 8, 128)
    *sums, small = scatter_sum(wgrads, small)
    total = jnp.stack(sums)
    narrow_sum = head_order_back(total[..., :768])
    wide_sum = total[..., 768:]
    small = small.reshape(32, 1024)[:, :432].reshape(13824)
    norms, rows = small[:8192].reshape(2, 4, 1024), small[8192:].reshape(2, 2816)
    branch_bias = rows[:, 768:1792]
    return (
        hidden_out,
        input_grad,
        norms[:, 0],
        norms[:, 1],
        norms[:, 2],
        norms[:, 3],
        narrow_sum,
        head_order_back(rows[:, :768]),
        jnp.swapaxes(wide_sum[..., :256], 1, 2),
        branch_bias,
        wide_sum[..., 256:1280],
        rows[:, 1792:],
        jnp.swapaxes(wide_sum[..., 1280:], 1, 2),
        branch_bias,
    )


def solution(mesh):
    rows, spread, split = P(None, "batch", "seq", None), P(None, ("batch", "seq"), "tensor"), P(
        None, "tensor"
    )
    across = P(None, "tensor", ("batch", "seq"))
    return jax.shard_map(
        local,
        mesh=mesh,
        in_specs=(
            rows,
            P(None, "batch", "seq"),
            P(),
            P(),
            P(),
            P(),
            spread,
            split,
            across,
            P(),
            spread,
            split,
            across,
            P(),
            rows,
        ),
        out_specs=(
            rows,
            rows,
            P(),
            P(),
            P(),
            P(),
            spread,
            split,
            across,
            P(),
            spread,
            split,
            across,
            P(),
        ),
        check_vma=False,
    )
```

```python
import functools

import jax
import jax.numpy as jnp
from jax import lax
from jax.experimental import pallas as pl
from jax.experimental.pallas import tpu as pltpu
from jax.sharding import PartitionSpec as P

HEAD = 64
ROT = 16
LAYERS = 2
MASKED = -1000000000.0
MESH = pl.DeviceIdType.MESH
F32, BF16 = jnp.float32, jnp.bfloat16
VLIM = 56 * 1024 * 1024


def dot(a, b, ca, cb):
    return lax.dot_general(a, b, (((ca,), (cb,)), ((), ())), preferred_element_type=F32)


def places():
    s = lax.axis_index("seq")
    return s, s // 2, lax.rem(s, 2)


def greet(peers):
    barrier = pltpu.get_barrier_semaphore()
    for peer in peers:
        pl.semaphore_signal(barrier, inc=1, device_id=peer, device_id_type=MESH)
    pl.semaphore_wait(barrier, len(peers))


def remote(src, dst, send, recv, peer):
    return pltpu.make_async_remote_copy(
        src_ref=src, dst_ref=dst, send_sem=send, recv_sem=recv, device_id=peer, device_id_type=MESH
    )


def chip_peers():
    _, c, k = places()
    return [{"seq": lax.rem(c + d, 8) * 2 + k} for d in range(1, 8)]


def comm_call(body, out_shape, scratch, ident, in_space, out_space, n_in, name):
    single = not isinstance(out_shape, (tuple, list))
    return pl.pallas_call(
        body,
        out_shape=out_shape,
        in_specs=[pl.BlockSpec(memory_space=in_space)] * n_in,
        out_specs=pl.BlockSpec(memory_space=out_space)
        if single
        else [pl.BlockSpec(memory_space=out_space)] * len(out_shape),
        scratch_shapes=scratch,
        compiler_params=pltpu.CompilerParams(
            collective_id=ident, has_side_effects=True, vmem_limit_bytes=VLIM
        ),
        name=name,
    )


class Spot:
    def __init__(self):
        b = lax.axis_index("batch")
        s, c, self.core = places()
        self.pos = (lax.rem(c, 4), (c // 4) * 2 + b)
        self.partner = {"seq": s + 1 - 2 * self.core}

    def ring(self, r):
        k = self.core
        return [r, lax.rem(r + 3 - 2 * k, 4), lax.rem(r + 1 + 2 * k, 4), lax.rem(r + 2, 4)]

    def device(self, x, y):
        return {"batch": lax.rem(y, 2), "seq": ((y // 2) * 4 + x) * 2 + self.core}

    def neighbours(self):
        x, y = self.pos
        xs, ys = self.ring(x), self.ring(y)
        return [self.device(x2, y) for x2 in xs[1:3]] + [self.device(x, y2) for y2 in ys[1:3]]


def flat(x, y):
    return lax.rem(y, 2) * 8 + (y // 2) * 4 + x


def drive(jobs):
    jobs = list(jobs)
    while jobs:
        for job in list(jobs):
            try:
                next(job)
            except StopIteration:
                jobs.remove(job)


def ring_gather(spot, src, out, first, ss, rs, fs, fr, ls):
    k = spot.core
    along, other = spot.ring(spot.pos[first]), spot.ring(spot.pos[1 - first])

    def place(i, j):
        at = (along[i], other[j])
        return at if first == 0 else at[::-1]

    def slot(i, j):
        return out.at[flat(*place(i, j)), k]

    sent, passed = [], []

    def send(i, j, idx, to):
        piece = slot(i, j)
        copy = remote(src if (i, j) == (0, 0) else piece, piece, ss.at[idx], rs.at[idx], to)
        copy.start()
        sent.append(copy)
        return copy

    def share(i, j):
        piece, idx = slot(i, j), 4 * i + j
        copy = remote(
            src if idx == 0 else piece, piece, fs.at[idx], fr.at[idx], spot.partner
        )
        copy.start()
        passed.append(copy)

    ahead1, behind1 = spot.device(*place(2, 0)), spot.device(*place(1, 0))
    ahead2, behind2 = spot.device(*place(0, 2)), spot.device(*place(0, 1))
    own = pltpu.make_async_copy(src, slot(0, 0), ls)
    own.start()
    m0 = send(0, 0, 0, ahead1)
    m1 = send(0, 0, 1, behind1)

    def second(i):
        return send(i, 0, 3 + 3 * i, ahead2), send(i, 0, 4 + 3 * i, behind2)

    n = {0: second(0)}
    share(0, 0)
    yield
    m0.wait_recv()
    m2 = send(1, 0, 2, ahead1)
    n[1] = second(1)
    share(1, 0)
    yield
    m1.wait_recv()
    n[2] = second(2)
    share(2, 0)
    yield
    far = {}

    def middle(i):
        n[i][0].wait_recv()
        far[i] = send(i, 1, 5 + 3 * i, ahead2)
        share(i, 1)
        n[i][1].wait_recv()
        share(i, 2)

    middle(0)
    yield
    m2.wait_recv()
    n[3] = second(3)
    share(3, 0)
    yield
    for i in range(1, 4):
        middle(i)
        yield
    for i in range(4):
        far[i].wait_recv()
        share(i, 3)
        yield
    own.wait()
    for copy in sent:
        copy.wait_send()
    for copy in passed:
        copy.wait()


def gather_sems():
    dma = pltpu.SemaphoreType.DMA
    return [dma((15,)), dma((15,)), dma((16,)), dma((16,)), dma(())]


def gather_kernel(firsts, *refs):
    count = len(firsts)
    srcs, outs, sems = refs[:count], refs[count : 2 * count], refs[2 * count :]
    spot = Spot()
    greet(spot.neighbours() + [spot.partner])
    drive(
        ring_gather(spot, srcs[a], outs[a], firsts[a], *sems[5 * a : 5 * a + 5])
        for a in range(count)
    )


def gather_plane(arrays, firsts, ident):
    count = len(arrays)
    return comm_call(
        functools.partial(gather_kernel, firsts),
        tuple(jax.ShapeDtypeStruct((16, 2, *a.shape), a.dtype) for a in arrays),
        [sem for _ in arrays for sem in gather_sems()],
        ident,
        pl.ANY,
        pl.ANY,
        count,
        "gather_plane",
    )(*arrays)


def ring_sum(spot, part, out, rows, buf, held, ss, rs):
    t, behind, ahead, across = spot.ring(lax.axis_index("tensor"))
    to_ahead, to_behind = {"tensor": ahead}, {"tensor": behind}
    sent = []

    def send(src, dst, idx, to):
        copy = remote(src, dst, ss.at[idx], rs.at[idx], to)
        copy.start()
        sent.append(copy)
        return copy

    far = send(part.at[across, rows], buf.at[0, rows], 0, to_ahead)
    back = send(part.at[behind, rows], buf.at[2, rows], 2, to_behind)
    yield
    far.wait_recv()
    held[rows] = (part[ahead, rows].astype(F32) + buf[0, rows].astype(F32)).astype(BF16)
    on = send(held.at[rows], buf.at[1, rows], 1, to_ahead)
    yield
    back.wait_recv()
    on.wait_recv()
    total = part[t, rows].astype(F32) + buf[1, rows].astype(F32) + buf[2, rows].astype(F32)
    out[t, rows] = total.astype(BF16)
    mine, theirs = out.at[t, rows], out.at[behind, rows]
    first = send(mine, mine, 3, to_ahead)
    second = send(mine, mine, 4, to_behind)
    yield
    first.wait_recv()
    third = send(theirs, theirs, 5, to_ahead)
    yield
    second.wait_recv()
    third.wait_recv()
    for copy in sent:
        copy.wait_send()


def direct_sum(vec, vec_out, got, ss, rs):
    t = lax.axis_index("tensor")
    copies = []
    for d in range(3):
        to = {"tensor": lax.rem(t + d + 1, 4)}
        copies.append(remote(vec, got.at[t], ss.at[d], rs.at[d], to))
        copies[-1].start()
    got[t] = vec[...]
    yield
    yield
    yield
    for copy in copies:
        copy.wait()
    vec_out[...] = (got[0] + got[1]) + (got[2] + got[3])


def tensor_sum_kernel(count, *refs):
    (part, *vec), (out, *vec_out) = refs[: 1 + count], refs[1 + count : 2 + 2 * count]
    buf, held, s0, r0, s1, r1, *rest = refs[2 + 2 * count :]
    spot = Spot()
    t = lax.axis_index("tensor")
    greet([{"tensor": lax.rem(t + d, 4)} for d in range(1, 4)])
    jobs = [
        ring_sum(spot, part, out, pl.ds(0, 128), buf, held, s0, r0),
        ring_sum(spot, part, out, pl.ds(128, 128), buf, held, s1, r1),
    ]
    if count:
        jobs.append(direct_sum(vec[0], vec_out[0], *rest))
    drive(jobs)


def tensor_sum(part, vec=None):
    dma = pltpu.SemaphoreType.DMA
    count = 0 if vec is None else 1
    shape = jax.ShapeDtypeStruct(part.shape, BF16)
    scratch = [
        pltpu.VMEM((3, *part.shape[1:]), BF16),
        pltpu.VMEM(part.shape[1:], BF16),
    ] + [dma((6,))] * 4
    if vec is not None:
        scratch += [pltpu.VMEM((4, *vec.shape), F32), dma((3,)), dma((3,))]
    return comm_call(
        functools.partial(tensor_sum_kernel, count),
        (shape,) if vec is None else (shape, jax.ShapeDtypeStruct(vec.shape, F32)),
        scratch,
        6 + count,
        pltpu.VMEM,
        pltpu.VMEM,
        1 + count,
        "tensor_sum",
    )(*((part,) if vec is None else (part, vec)))


def ring_scatter(spot, src, out, first, pair, left, got, ps, pr, ss, rs):
    k = spot.core
    along, other = spot.ring(spot.pos[first]), spot.ring(spot.pos[1 - first])
    kind = pair.dtype

    def place(i, j):
        at = (along[i], other[j])
        return at if first == 0 else at[::-1]

    order = (3, 2, 1, 0)
    theirs = (0, 2, 1, 3)
    pairs, sent = {}, []
    for i in order:
        for j in order:
            at = flat(*place(theirs[i], theirs[j]))
            idx = 4 * i + j
            copy = remote(src.at[at, 1 - k], pair.at[idx], ps.at[idx], pr.at[idx], spot.partner)
            copy.start()
            pairs[idx] = copy
    yield

    def both(i, j):
        pairs[4 * i + j].wait_recv()
        return src[flat(*place(i, j)), k].astype(F32) + pair[4 * i + j].astype(F32)

    def send(value, idx, to):
        left[idx] = value.astype(kind)
        copy = remote(left.at[idx], got.at[idx], ss.at[idx], rs.at[idx], to)
        copy.start()
        sent.append(copy)
        return copy

    ahead1, behind1 = spot.device(*place(2, 0)), spot.device(*place(1, 0))
    ahead2, behind2 = spot.device(*place(0, 2)), spot.device(*place(0, 1))
    far, on, back = {}, {}, {}
    for j in order:
        far[j] = send(both(3, j), j, ahead1)
        back[j] = send(both(1, j), 8 + j, behind1)
        yield
    for j in order:
        far[j].wait_recv()
        on[j] = send(both(2, j) + got[j].astype(F32), 4 + j, ahead1)
        yield

    def settled(j):
        on[j].wait_recv()
        back[j].wait_recv()
        return both(0, j) + got[4 + j].astype(F32) + got[8 + j].astype(F32)

    far2 = send(settled(3), 12, ahead2)
    yield
    ready = settled(2)
    back2 = send(settled(1), 14, behind2)
    yield
    far2.wait_recv()
    on2 = send(ready + got[12].astype(F32), 13, ahead2)
    total = settled(0)
    yield
    back2.wait_recv()
    total = total + got[14].astype(F32)
    on2.wait_recv()
    out[...] = total + got[13].astype(F32)
    for copy in pairs.values():
        copy.wait_send()
    for copy in sent:
        copy.wait_send()


def small_total(scatter, gather):
    yield from scatter
    yield from gather()


def scatter_kernel(count, *refs):
    ins, outs = refs[: count + 1], refs[count + 1 : 2 * count + 2]
    rest = refs[2 * count + 2 :]
    spot = Spot()
    greet(spot.neighbours() + [spot.partner])
    args = [rest[7 * a : 7 * a + 7] for a in range(count + 1)]
    jobs = [
        ring_scatter(spot, ins[a], outs[a], (a + 1) % 2, *args[a]) for a in range(count)
    ]
    piece, *sems = rest[7 * count + 7 :]
    small = ring_scatter(spot, ins[count], piece, 0, *args[count])
    jobs.append(
        small_total(small, lambda: ring_gather(spot, piece, outs[count], 0, *sems))
    )
    drive(jobs)


def scatter_scratch(a):
    dma = pltpu.SemaphoreType.DMA
    return [
        pltpu.VMEM((16, *a.shape[2:]), a.dtype),
        pltpu.VMEM((15, *a.shape[2:]), a.dtype),
        pltpu.VMEM((15, *a.shape[2:]), a.dtype),
        dma((16,)),
        dma((16,)),
        dma((15,)),
        dma((15,)),
    ]


def scatter_sum(arrays, small):
    ins = [a.reshape(16, 2, 32, a.shape[1]) for a in arrays] + [small]
    scratch = [item for a in ins for item in scatter_scratch(a)]
    return comm_call(
        functools.partial(scatter_kernel, len(arrays)),
        tuple(jax.ShapeDtypeStruct(a.shape[2:], F32) for a in ins[:-1])
        + (jax.ShapeDtypeStruct(small.shape, F32),),
        scratch + [pltpu.VMEM(small.shape[2:], F32)] + gather_sems(),
        8,
        pltpu.VMEM,
        pltpu.VMEM,
        len(ins),
        "scatter_sum",
    )(*ins)


def turned(values, cosine, sine):
    lane = lax.broadcasted_iota(jnp.int32, values.shape, 1)
    swapped = jnp.where(
        lane < 8, pltpu.roll(values, 120, axis=1), pltpu.roll(values, 8, axis=1)
    )
    return values * cosine + swapped * sine


def normal(values):
    centred = values - jnp.mean(values, axis=-1, keepdims=True)
    rstd = lax.rsqrt(jnp.mean(centred * centred, axis=-1, keepdims=True) + 1e-05)
    return centred * rstd, rstd


def with_branch(x, branch, shift, out):
    for t in range(4):
        at = slice(256 * t, 256 * (t + 1))
        out[:, at] = x[:, at] + branch[t].astype(F32) + shift[:, at]


def norm_back(grad, z, x, out):
    hat, rstd = normal(x[...])
    flow = jnp.concatenate([z[t].astype(F32) for t in range(4)], axis=1)
    out[...] = grad[...] + rstd * (
        flow
        - jnp.mean(flow, axis=-1, keepdims=True)
        - hat * jnp.mean(flow * hat, axis=-1, keepdims=True)
    )


def project_kernel(*refs):
    if len(refs) == 15:
        x, branch, shift, *rest, x_out = refs
        with_branch(x, branch, shift, x_out)
        project_rows(x_out, *rest)
    else:
        project_rows(*refs)


def project_rows(x, g1, b1, g2, b2, bias, weight, cosine, sine, h1, h2, qkv):
    hat, _ = normal(x[...])
    h1[...] = (hat * g1[...] + b1[...]).astype(BF16)
    h2[...] = (hat * g2[...] + b2[...]).astype(BF16)
    proj = dot(h1[...], weight[...], 1, 0) + bias[...]
    cos, sin = cosine[...], sine[...]
    lane = lax.broadcasted_iota(jnp.int32, (128, 128), 1)
    for m in range(2):
        rows = proj[m * 128 : (m + 1) * 128]
        for h in range(4):
            pair = rows[:, 128 * h : 128 * (h + 1)]
            qkv[m * 4 + h, 0] = turned(pair, cos, sin).astype(BF16)
            q = rows[:, 512 + 128 * (h // 2) : 640 + 128 * (h // 2)]
            if h % 2:
                q = pltpu.roll(q, 64, axis=1)
            q = turned(q, cos, sin) * 0.125
            qkv[m * 4 + h, 1] = jnp.where(lane < 64, q, 0.0).astype(BF16)


def local_call(body, out_shape, in_specs, name, scratch=()):
    return pl.pallas_call(
        body,
        out_shape=out_shape,
        grid=(1,),
        in_specs=in_specs,
        out_specs=jax.tree.map(lambda o: whole(o.shape), out_shape),
        scratch_shapes=scratch,
        compiler_params=pltpu.CompilerParams(vmem_limit_bytes=VLIM),
        name=name,
    )


def whole(shape):
    return pl.BlockSpec(shape, lambda i: (0,) * len(shape))


def wholes(*arrays):
    return [whole(a.shape) for a in arrays]


def project(x, g1, b1, g2, b2, bias, gathered, cosine, sine, branch=None, shift=None):
    sds = jax.ShapeDtypeStruct
    more = () if branch is None else (branch, shift)
    return local_call(
        project_kernel,
        (
            sds((256, 1024), BF16),
            sds((256, 1024), BF16),
            sds((8, 2, 128, 128), BF16),
        )
        + ((sds((256, 1024), F32),) if more else ()),
        wholes(x, *more, g1, b1, g2, b2, bias, gathered, cosine, sine),
        "project",
    )(x, *more, g1, b1, g2, b2, bias, gathered, cosine, sine)


def add_branch(x, branch, shift):
    return local_call(
        with_branch,
        jax.ShapeDtypeStruct(x.shape, F32),
        wholes(x, branch, shift),
        "add_branch",
    )(x, branch, shift)


def add_norm_back(grad, z, x):
    return local_call(
        norm_back,
        jax.ShapeDtypeStruct(grad.shape, F32),
        wholes(grad, z, x),
        "add_norm_back",
    )(grad, z, x)


def scores_of(q, keys, low, high):
    s = dot(q, keys, 1, 1)
    place = lax.broadcasted_iota(jnp.int32, s.shape, 1)
    return jnp.where((place >= low) & (place <= high), s, MASKED)


def to_chip(i, src, dst, ss, rs, local):
    _, c, k = places()
    far = remote(src, dst, ss, rs, {"seq": 2 * i + k})
    near = pltpu.make_async_copy(src, dst, local)

    @pl.when(c != i)
    def _():
        far.start()

    @pl.when(c == i)
    def _():
        near.start()

    def left():
        @pl.when(c != i)
        def _():
            far.wait_send()

        @pl.when(c == i)
        def _():
            near.wait()

    return left


def from_chip(i, dst, ss, rs):
    _, c, k = places()

    @pl.when(c != i)
    def _():
        remote(dst, dst, ss, rs, {"seq": 2 * i + k}).wait_recv()


def seq_peers(spot):
    x, y = spot.pos
    ys = spot.ring(y)
    return chip_peers() + [spot.device(x, ys[1]), spot.device(x, ys[2]), spot.partner]


def attention(spot, src, low, high, kv_out, q_out, lse, ctx_in, ctx_out, *sems):
    ssem, rsem, fs, fr, lsem, cs, cr, cl = sems
    s, c, k = places()
    others = chip_peers()
    copies, copies_q = [], []
    for d, peer in enumerate(others):
        c2 = lax.rem(c + d + 1, 8)
        copies.append(remote(src.at[c2, 0], kv_out.at[s], ssem.at[0, d], rsem.at[0, d], peer))
        copies[-1].start()
    for d, peer in enumerate(others):
        c2 = lax.rem(c + d + 1, 8)
        copies_q.append(remote(src.at[c2, 1], q_out.at[c], ssem.at[1, d], rsem.at[1, d], peer))
        copies_q[-1].start()
    onward = [remote(src.at[c, 0], kv_out.at[s], fs.at[0], fr.at[0], spot.partner)]
    onward[0].start()
    own_kv = pltpu.make_async_copy(src.at[c, 0], kv_out.at[s], lsem.at[0])
    own_q = pltpu.make_async_copy(src.at[c, 1], q_out.at[c], lsem.at[1])
    own_kv.start()
    own_q.start()
    yield
    for d in range(1, 8):
        copies[d - 1].wait_recv()
        at = kv_out.at[lax.rem(c - d + 8, 8) * 2 + k]
        copy = remote(at, at, fs.at[d], fr.at[d], spot.partner)
        copy.start()
        onward.append(copy)
        if d % 2:
            yield
    own_kv.wait()
    own_q.wait()
    for copy in copies_q:
        copy.wait_recv()
    for copy in onward:
        copy.wait_recv()
    left = []
    for i in reversed(range(8)):
        n = 256 * (i + 1)
        keys = kv_out[0 : 2 * (i + 1)].reshape(n, 128)
        sc = scores_of(q_out[i], keys, low[i], high[i])
        top = jnp.max(sc, axis=-1, keepdims=True)
        e = jnp.exp(sc - top)
        total = jnp.sum(e, axis=-1, keepdims=True)
        soft = (e * (1.0 / total)).astype(BF16)
        ctx_out[i] = dot(soft, keys, 1, 0).astype(BF16)
        lse[i] = top + jnp.log(total)
        left.append(to_chip(i, ctx_out.at[i], ctx_in.at[c], cs.at[i], cr.at[c], cl))
        yield
    for i in reversed(range(8)):
        from_chip(i, ctx_in.at[i], cs.at[i], cr.at[i])
    for wait in left:
        wait()
    for copy in copies + copies_q + onward:
        copy.wait_send()


def attention_kernel(firsts, *refs):
    count = len(firsts)
    (src, low, high), srcs = refs[:3], refs[3 : 3 + count]
    refs = refs[3 + count :]
    (kv, q, lse, ctx_in), outs = refs[:4], refs[4 : 4 + count]
    refs = refs[4 + count :]
    spot = Spot()
    greet(seq_peers(spot))
    ctx_out, *sems = refs[:9]
    jobs = [attention(spot, src, low, high, kv, q, lse, ctx_in, ctx_out, *sems)]
    rest = refs[9:]
    for a in range(count):
        jobs.append(ring_gather(spot, srcs[a], outs[a], firsts[a], *rest[5 * a : 5 * a + 5]))
    drive(jobs)


def attend(qkv, low, high, shards, firsts, ident):
    sds, dma, count = jax.ShapeDtypeStruct, pltpu.SemaphoreType.DMA, len(shards)
    vmem, hbm = pl.BlockSpec(memory_space=pltpu.VMEM), pl.BlockSpec(memory_space=pl.ANY)
    return pl.pallas_call(
        functools.partial(attention_kernel, firsts),
        out_shape=(
            sds((16, 128, 128), BF16),
            sds((8, 128, 128), BF16),
            sds((8, 128, 1), F32),
            sds((8, 128, 128), BF16),
        )
        + tuple(sds((16, 2, *a.shape), a.dtype) for a in shards),
        in_specs=[vmem] * 3 + [hbm] * count,
        out_specs=[vmem] * 4 + [hbm] * count,
        scratch_shapes=[
            pltpu.VMEM((8, 128, 128), BF16),
            dma((2, 7)),
            dma((2, 7)),
            dma((8,)),
            dma((8,)),
            dma((2,)),
            dma((8,)),
            dma((8,)),
            dma(()),
        ]
        + [sem for _ in shards for sem in gather_sems()],
        compiler_params=pltpu.CompilerParams(
            collective_id=ident, has_side_effects=True, vmem_limit_bytes=VLIM
        ),
        name="attend",
    )(qkv, low, high, *shards)


def attention_back(
    spot, dctx, kv, q, lse, low, high, dq_in, dkv_in, dctx_in, dq, total, other, summed, *sems
):
    ds_, dr, dl, qs, qr, ql, ps, pr, ks, kr, kl = sems
    _, c, k = places()
    copies = []
    for d, peer in enumerate(chip_peers()):
        c2 = lax.rem(c + d + 1, 8)
        copies.append(remote(dctx.at[c2], dctx_in.at[c], ds_.at[d], dr.at[c], peer))
        copies[-1].start()
    own = pltpu.make_async_copy(dctx.at[c], dctx_in.at[c], dl)
    own.start()
    own.wait()
    yield
    left, pairs = [], {}

    def finish(i):
        pairs[i].wait_recv()
        summed[i] = (total[2 * i + k] + other[i]).astype(BF16)
        left.append(to_chip(i, summed.at[i], dkv_in.at[c], ks.at[i], kr.at[c], kl))

    for i in reversed(range(8)):
        n, blocks = 256 * (i + 1), 2 * (i + 1)
        from_chip(i, dctx_in.at[i], ds_.at[0], dr.at[i])
        keys = kv[0:blocks].reshape(n, 128)
        sc = scores_of(q[i], keys, low[i], high[i])
        soft = jnp.exp(sc - lse[i])
        dsoft = dot(dctx_in[i], keys, 1, 1)
        term = jnp.sum(soft * dsoft, axis=-1, keepdims=True)
        dscore = (soft * (dsoft - term)).astype(BF16)
        dq[i] = (dot(dscore, keys, 1, 0) * 0.125).astype(BF16)
        left.append(to_chip(i, dq.at[i], dq_in.at[c], qs.at[i], qr.at[c], ql))
        both = jnp.concatenate([dscore, soft.astype(BF16)], axis=0)
        right = jnp.concatenate([q[i], dctx_in[i]], axis=0)
        fresh = dot(both, right, 0, 0).reshape(blocks, 128, 128)
        if i == 7:
            total[...] = fresh
        else:
            total[0:blocks] += fresh
        pairs[i] = remote(total.at[2 * i + 1 - k], other.at[i], ps.at[i], pr.at[i], spot.partner)
        pairs[i].start()
        if i < 7:
            finish(i + 1)
        yield
    finish(0)
    for copy in pairs.values():
        copy.wait_send()
    yield
    for i in reversed(range(8)):
        from_chip(i, dq_in.at[i], qs.at[i], qr.at[i])
        from_chip(i, dkv_in.at[i], ks.at[i], kr.at[i])
    for wait in left:
        wait()
    for copy in copies:
        copy.wait_send()


def attention_back_kernel(firsts, *refs):
    count = len(firsts)
    ins, srcs = refs[:6], refs[6 : 6 + count]
    refs = refs[6 + count :]
    outs, sums = refs[:2], refs[2 : 2 + count]
    refs = refs[2 + count :]
    spot = Spot()
    greet(seq_peers(spot))
    jobs = [attention_back(spot, *ins, *outs, *refs[:16])]
    rest = refs[16:]
    for a in range(count):
        jobs.append(ring_scatter(spot, srcs[a], sums[a], firsts[a], *rest[7 * a : 7 * a + 7]))
    drive(jobs)


def attend_back(dctx, kv, q, lse, low, high, arrays, firsts, ident):
    sds, dma = jax.ShapeDtypeStruct, pltpu.SemaphoreType.DMA
    vmem = pl.BlockSpec(memory_space=pltpu.VMEM)
    ins = [a.reshape(16, 2, 32, a.shape[1]) for a in arrays]
    block, wide = (8, 128, 128), (16, 128, 128)
    return pl.pallas_call(
        functools.partial(attention_back_kernel, firsts),
        out_shape=(sds(block, BF16), sds(block, BF16))
        + tuple(sds(a.shape[2:], F32) for a in ins),
        in_specs=[vmem] * (6 + len(ins)),
        out_specs=[vmem] * (2 + len(ins)),
        scratch_shapes=[
            pltpu.VMEM(block, BF16),
            pltpu.VMEM(block, BF16),
            pltpu.VMEM(wide, F32),
            pltpu.VMEM(block, F32),
            pltpu.VMEM(block, BF16),
            dma((7,)),
            dma((8,)),
            dma(()),
            dma((8,)),
            dma((8,)),
            dma(()),
            dma((8,)),
            dma((8,)),
            dma((8,)),
            dma((8,)),
            dma(()),
        ]
        + [item for a in ins for item in scatter_scratch(a)],
        compiler_params=pltpu.CompilerParams(
            collective_id=ident, has_side_effects=True, vmem_limit_bytes=VLIM
        ),
        name="attend_back",
    )(dctx, kv, q, lse, low, high, *ins)


def in_quarters(value, ref):
    for t in range(4):
        ref[t] = value[:, 256 * t : 256 * (t + 1)].astype(BF16)


def feed_kernel(ctx_in, h2, outer, expand, bias, u, act, ctx, part):
    lane = lax.broadcasted_iota(jnp.int32, (128, 128), 1)
    for m in range(2):
        for h in range(2):
            left = pltpu.roll(ctx_in[m * 4 + 2 * h].astype(F32), 64, axis=1)
            right = ctx_in[m * 4 + 2 * h + 1].astype(F32)
            ctx[m * 128 : (m + 1) * 128, 128 * h : 128 * (h + 1)] = jnp.where(
                lane < 64, left, right
            ).astype(BF16)
    inner = dot(h2[...], expand[...], 1, 0) + bias[...]
    u[...] = inner
    act[...] = (0.5 * inner * (1.0 + lax.erf(inner * 0.7071067811865476))).astype(BF16)
    in_quarters(dot(ctx[...], outer[:, :256], 1, 1) + dot(act[...], outer[:, 256:], 1, 1), part)


def feed(ctx_in, h2, outer, expand, bias):
    sds = jax.ShapeDtypeStruct
    return local_call(
        feed_kernel,
        (
            sds((256, 1024), F32),
            sds((256, 1024), BF16),
            sds((256, 256), BF16),
            sds((4, 256, 256), BF16),
        ),
        wholes(ctx_in, h2, outer, expand, bias),
        "feed",
    )(ctx_in, h2, outer, expand, bias)


def feed_back_kernel(*refs):
    if len(refs) == 17:
        before, z, x_before, *rest, grad = refs
        norm_back(before, z, x_before, grad)
        feed_back_rows(grad, *rest)
    else:
        feed_back_rows(*refs)


def feed_back_rows(
    grad, x, g2, u, act, ctx, h2, outer, expand, dctx, w_outer, w_expand, z2, small
):
    gb = grad[...].astype(BF16)
    dact = dot(gb, outer[:, 256:], 1, 0)
    inner = u[...]
    slope = 0.5 * (1.0 + lax.erf(inner * 0.7071067811865476)) + inner * (
        0.3989422804014327 * jnp.exp(-0.5 * inner * inner)
    )
    du = (dact * slope).astype(BF16)
    dc = dot(gb, outer[:, :256], 1, 0)
    lane = lax.broadcasted_iota(jnp.int32, (128, 128), 1)
    for m in range(2):
        for h in range(4):
            piece = dc[m * 128 : (m + 1) * 128, 128 * (h // 2) : 128 * (h // 2 + 1)]
            if h % 2 == 0:
                piece = pltpu.roll(piece, 64, axis=1)
            dctx[m * 4 + h] = jnp.where(lane >= 64, piece, 0.0).astype(BF16)
    w_outer[:, :256] = dot(gb, ctx[...], 0, 0).astype(BF16)
    w_outer[:, 256:] = dot(gb, act[...], 0, 0).astype(BF16)
    w_expand[...] = dot(h2[...], du, 0, 0).astype(BF16)
    dh2 = dot(du, expand[...], 1, 1)
    hat, _ = normal(x[...])
    z2[...] = dh2 * g2[...]
    small[0:1] = jnp.sum(dh2 * hat, axis=0, keepdims=True)
    small[1:2] = jnp.sum(dh2, axis=0, keepdims=True)
    small[2:3] = jnp.sum(gb.astype(F32), axis=0, keepdims=True)
    small[3:4] = jnp.sum(du.astype(F32), axis=0, keepdims=True)


def feed_back(grad, x, g2, u, act, ctx, h2, outer, expand, z=None, x_before=None):
    sds = jax.ShapeDtypeStruct
    more = () if z is None else (z, x_before)
    args = (grad, *more, x, g2, u, act, ctx, h2, outer, expand)
    return local_call(
        feed_back_kernel,
        (
            sds((8, 128, 128), BF16),
            sds((1024, 1280), BF16),
            sds((1024, 1024), BF16),
            sds((256, 1024), F32),
            sds((4, 1024), F32),
        )
        + ((sds((256, 1024), F32),) if more else ()),
        wholes(*args),
        "feed_back",
    )(*args)


def project_back_kernel(
    dq, dkv, cosine, sine, h1, weight, z2, x, g1, wgrad, part, small, bias_grad, dproj
):
    cos, sin = cosine[...], -sine[...]
    lane = lax.broadcasted_iota(jnp.int32, (128, 128), 1)
    for m in range(2):
        rows = pl.ds(m * 128, 128)
        for h in range(4):
            dproj[rows, 128 * h : 128 * (h + 1)] = turned(
                dkv[m * 4 + h].astype(F32), cos, sin
            ).astype(BF16)
        for h in range(2):
            left = turned(dq[m * 4 + 2 * h].astype(F32), cos, sin)
            right = turned(dq[m * 4 + 2 * h + 1].astype(F32), cos, sin)
            dproj[rows, 512 + 128 * h : 640 + 128 * h] = jnp.where(
                lane < 64, left, pltpu.roll(right, 64, axis=1)
            ).astype(BF16)
    dp = dproj[...]
    wgrad[...] = dot(h1[...], dp, 0, 0).astype(BF16)
    bias_grad[...] = jnp.sum(dp.astype(F32), axis=0, keepdims=True)
    dh1 = dot(dp, weight[...], 1, 1)
    hat, _ = normal(x[...])
    small[0:1] = jnp.sum(dh1 * hat, axis=0, keepdims=True)
    small[1:2] = jnp.sum(dh1, axis=0, keepdims=True)
    in_quarters(dh1 * g1[...] + z2[...], part)


def project_back(dq, dkv, cosine, sine, h1, weight, z2, x, g1):
    sds = jax.ShapeDtypeStruct
    args = (dq, dkv, cosine, sine, h1, weight, z2, x, g1)
    return local_call(
        project_back_kernel,
        (
            sds((1024, 768), BF16),
            sds((4, 256, 256), BF16),
            sds((2, 1024), F32),
            sds((1, 768), F32),
        ),
        wholes(*args),
        "project_back",
        [pltpu.VMEM((256, 768), BF16)],
    )(*args)


def head_order(value):
    lead = value.shape[:-1]
    parts = value.reshape(*lead, 4, 3, HEAD)
    keys = parts[..., 1:3, :].reshape(*lead, 512)
    return jnp.concatenate([keys, parts[..., 0, :].reshape(*lead, 256)], axis=-1)


def head_order_back(value):
    lead = value.shape[:-1]
    keys = value[..., :512].reshape(*lead, 4, 2, HEAD)
    queries = value[..., 512:].reshape(*lead, 4, 1, HEAD)
    return jnp.concatenate([queries, keys], axis=-2).reshape(*lead, 768)


def from_quarters(value):
    return value.transpose(1, 0, 2).reshape(256, 1024).astype(F32)


def local(
    hidden_in,
    document_ids,
    first_gain,
    first_shift,
    second_gain,
    second_shift,
    attn_weight,
    attn_bias,
    dense_weight,
    dense_bias,
    expand_weight,
    expand_bias,
    shrink_weight,
    shrink_bias,
    output_grad,
):
    seq_at = lax.axis_index("seq")
    chip, core = seq_at // 2, lax.rem(seq_at, 2)
    unit_micro = chip // 4
    lead = jnp.arange(ROT // 2, dtype=F32) * 2
    inverse = 10000.0 ** (-lead / ROT)
    place = (seq_at * 128 + jnp.arange(128, dtype=jnp.int32)).astype(F32)
    angles = place[:, None] * inverse[None, :]
    cos, sin = jnp.cos(angles), jnp.sin(angles)
    ones, zeros = jnp.ones((128, 112), F32), jnp.zeros((128, 112), F32)
    cosine = jnp.concatenate([cos, cos, ones], axis=1)
    sine = jnp.concatenate([-sin, sin, zeros], axis=1)

    attn = head_order(attn_weight)
    outer = jnp.concatenate(
        [jnp.swapaxes(dense_weight, 1, 2), jnp.swapaxes(shrink_weight, 1, 2)], axis=2
    )
    idents = jnp.pad(document_ids[:, 0], ((0, 6), (0, 0)))
    left, right, idents = gather_plane([attn[0, :, :384], attn[0, :, 384:], idents], (0, 1, 0), 1)
    weight = jnp.concatenate([left.reshape(1024, 384), right.reshape(1024, 384)], axis=1)
    idents = idents.reshape(2, 16, 8, 128)
    idents = lax.dynamic_index_in_dim(idents, lax.axis_index("batch"), 0, keepdims=False)
    mine = lax.dynamic_index_in_dim(idents, unit_micro, 1, keepdims=False).reshape(2048)
    count0 = jnp.sum((mine == 0).astype(jnp.int32))
    count1 = jnp.sum((mine == 1).astype(jnp.int32))
    start = jnp.where(mine == 0, 0, jnp.where(mine == 1, count0, count0 + count1))
    high = jnp.arange(2048, dtype=jnp.int32).reshape(8, 2, 128)
    high = lax.dynamic_index_in_dim(high, core, 1, keepdims=False)[..., None]
    low = lax.dynamic_index_in_dim(start.reshape(8, 2, 128), core, 1, keepdims=False)[..., None]
    bias_order = head_order(attn_bias)

    x = hidden_in.reshape(256, 1024)
    shift = dense_bias + shrink_bias
    kept, weights = [], []
    branch = ()
    for layer in range(LAYERS):
        row = slice(layer, layer + 1)
        h1, h2, qkv, *fresh = project(
            x,
            first_gain[row],
            first_shift[row],
            second_gain[row],
            second_shift[row],
            bias_order[row],
            weight,
            cosine,
            sine,
            *branch,
        )
        x = fresh[0] if fresh else x
        shards = [outer[layer], expand_weight[layer]] + ([attn[1]] if layer == 0 else [])
        kv, q, lse, ctx_in, *wide = attend(
            qkv, low, high, shards, (0, 1, 1)[: len(shards)], 2 + layer
        )
        wide = [w.reshape(1024, w.shape[3]) for w in wide]
        u, act, ctx, part = feed(ctx_in, h2, *wide[:2], expand_bias[row])
        kept.append((x, h1, h2, kv, q, lse, u, act, ctx))
        weights.append((weight, *wide[:2]))
        weight = wide[-1]
        branch = (tensor_sum(part)[0], shift[row])
    hidden_out = add_branch(x, *branch).reshape(2, 1, 128, 1024)

    grad = output_grad.reshape(256, 1024)
    by_all, by_rows = [None] * 2, [None] * 2
    before, pending, sums = (), [], []
    for layer in reversed(range(LAYERS)):
        row = slice(layer, layer + 1)
        x, h1, h2, kv, q, lse, u, act, ctx = kept[layer]
        weight, *wide = weights[layer]
        dctx, w_outer, w_expand, z2, small2, *fresh = feed_back(
            grad, x, second_gain[row], u, act, ctx, h2, *wide, *before
        )
        grad = fresh[0] if fresh else grad
        wgrads = [w_outer, w_expand]
        dq_in, dkv_in, *ready = attend_back(
            dctx, kv, q, lse, low, high, wgrads + pending, (0, 1, 1)[: 2 + len(pending)], 4 + layer
        )
        sums += ready
        wgrad, part, small1, bias_grad = project_back(
            dq_in, dkv_in, cosine, sine, h1, weight, z2, x, first_gain[row]
        )
        pending = [wgrad]
        z, by_all[layer] = tensor_sum(part, jnp.concatenate([small1, small2[:2]], axis=0))
        before = (z, x)
        by_rows[layer] = jnp.concatenate([bias_grad[0], small2[2], small2[3]], axis=0)
    input_grad = add_norm_back(grad, *before).reshape(2, 1, 128, 1024)

    small = jnp.concatenate([v.reshape(-1) for v in by_all + by_rows]).reshape(32, 432)
    small = jnp.pad(small, ((0, 0), (0, 592))).reshape(16, 2, 8, 128)
    left, right, small = scatter_sum([pending[0][:, :384], pending[0][:, 384:]], small)
    narrow_sum = head_order_back(jnp.stack([jnp.concatenate([left, right], axis=1), sums[4]]))
    outer_sum, expand_sum = jnp.stack([sums[2], sums[0]]), jnp.stack([sums[3], sums[1]])
    small = small.reshape(32, 1024)[:, :432].reshape(13824)
    norms, rows = small[:8192].reshape(2, 4, 1024), small[8192:].reshape(2, 2816)
    branch_bias = rows[:, 768:1792]
    return (
        hidden_out,
        input_grad,
        norms[:, 0],
        norms[:, 1],
        norms[:, 2],
        norms[:, 3],
        narrow_sum,
        head_order_back(rows[:, :768]),
        jnp.swapaxes(outer_sum[..., :256], 1, 2),
        branch_bias,
        expand_sum,
        rows[:, 1792:],
        jnp.swapaxes(outer_sum[..., 256:], 1, 2),
        branch_bias,
    )


def solution(mesh):
    rows, spread, split = P(None, "batch", "seq", None), P(None, ("batch", "seq"), "tensor"), P(
        None, "tensor"
    )
    across = P(None, "tensor", ("batch", "seq"))
    return jax.shard_map(
        local,
        mesh=mesh,
        in_specs=(
            rows,
            P(None, "batch", "seq"),
            P(),
            P(),
            P(),
            P(),
            spread,
            split,
            across,
            P(),
            spread,
            split,
            across,
            P(),
            rows,
        ),
        out_specs=(
            rows,
            rows,
            P(),
            P(),
            P(),
            P(),
            spread,
            split,
            across,
            P(),
            spread,
            split,
            across,
            P(),
        ),
        check_vma=False,
    )
```

```python
import functools

import jax
import jax.numpy as jnp
from jax import lax
from jax.experimental import pallas as pl
from jax.experimental.pallas import tpu as pltpu
from jax.sharding import PartitionSpec as P

HEAD = 64
ROT = 16
LAYERS = 2
MASKED = -1000000000.0
MESH = pl.DeviceIdType.MESH
F32, BF16 = jnp.float32, jnp.bfloat16
VLIM = 56 * 1024 * 1024


def dot(a, b, ca, cb):
    return lax.dot_general(a, b, (((ca,), (cb,)), ((), ())), preferred_element_type=F32)


def places():
    s = lax.axis_index("seq")
    return s, s // 2, lax.rem(s, 2)


def greet(peers):
    barrier = pltpu.get_barrier_semaphore()
    for peer in peers:
        pl.semaphore_signal(barrier, inc=1, device_id=peer, device_id_type=MESH)
    pl.semaphore_wait(barrier, len(peers))


def remote(src, dst, send, recv, peer):
    return pltpu.make_async_remote_copy(
        src_ref=src, dst_ref=dst, send_sem=send, recv_sem=recv, device_id=peer, device_id_type=MESH
    )


def chip_peers():
    _, c, k = places()
    return [{"seq": lax.rem(c + d, 8) * 2 + k} for d in range(1, 8)]


def comm_call(body, out_shape, scratch, ident, in_space, out_space, n_in, name):
    single = not isinstance(out_shape, (tuple, list))
    return pl.pallas_call(
        body,
        out_shape=out_shape,
        in_specs=[pl.BlockSpec(memory_space=in_space)] * n_in,
        out_specs=pl.BlockSpec(memory_space=out_space)
        if single
        else [pl.BlockSpec(memory_space=out_space)] * len(out_shape),
        scratch_shapes=scratch,
        compiler_params=pltpu.CompilerParams(
            collective_id=ident, has_side_effects=True, vmem_limit_bytes=VLIM
        ),
        name=name,
    )


class Spot:
    def __init__(self):
        b = lax.axis_index("batch")
        s, c, self.core = places()
        self.pos = (lax.rem(c, 4), (c // 4) * 2 + b)
        self.partner = {"seq": s + 1 - 2 * self.core}

    def ring(self, r):
        k = self.core
        return [r, lax.rem(r + 3 - 2 * k, 4), lax.rem(r + 1 + 2 * k, 4), lax.rem(r + 2, 4)]

    def device(self, x, y):
        return {"batch": lax.rem(y, 2), "seq": ((y // 2) * 4 + x) * 2 + self.core}

    def neighbours(self):
        x, y = self.pos
        xs, ys = self.ring(x), self.ring(y)
        return [self.device(x2, y) for x2 in xs[1:3]] + [self.device(x, y2) for y2 in ys[1:3]]


def flat(x, y):
    return lax.rem(y, 2) * 8 + (y // 2) * 4 + x


def drive(jobs):
    jobs = list(jobs)
    while jobs:
        for job in list(jobs):
            try:
                next(job)
            except StopIteration:
                jobs.remove(job)


def ring_gather(spot, src, out, first, ss, rs, fs, fr, ls):
    k = spot.core
    along, other = spot.ring(spot.pos[first]), spot.ring(spot.pos[1 - first])

    def place(i, j):
        at = (along[i], other[j])
        return at if first == 0 else at[::-1]

    def slot(i, j):
        return out.at[flat(*place(i, j)), k]

    sent, passed = [], []

    def send(i, j, idx, to):
        piece = slot(i, j)
        copy = remote(src if (i, j) == (0, 0) else piece, piece, ss.at[idx], rs.at[idx], to)
        copy.start()
        sent.append(copy)
        return copy

    def share(i, j):
        piece, idx = slot(i, j), 4 * i + j
        copy = remote(
            src if idx == 0 else piece, piece, fs.at[idx], fr.at[idx], spot.partner
        )
        copy.start()
        passed.append(copy)

    ahead1, behind1 = spot.device(*place(2, 0)), spot.device(*place(1, 0))
    ahead2, behind2 = spot.device(*place(0, 2)), spot.device(*place(0, 1))
    own = pltpu.make_async_copy(src, slot(0, 0), ls)
    own.start()
    m0 = send(0, 0, 0, ahead1)
    m1 = send(0, 0, 1, behind1)

    def second(i):
        return send(i, 0, 3 + 3 * i, ahead2), send(i, 0, 4 + 3 * i, behind2)

    n = {0: second(0)}
    share(0, 0)
    yield
    m0.wait_recv()
    m2 = send(1, 0, 2, ahead1)
    n[1] = second(1)
    share(1, 0)
    yield
    m1.wait_recv()
    n[2] = second(2)
    share(2, 0)
    yield
    far = {}

    def middle(i):
        n[i][0].wait_recv()
        far[i] = send(i, 1, 5 + 3 * i, ahead2)
        share(i, 1)
        n[i][1].wait_recv()
        share(i, 2)

    middle(0)
    yield
    m2.wait_recv()
    n[3] = second(3)
    share(3, 0)
    yield
    for i in range(1, 4):
        middle(i)
        yield
    for i in range(4):
        far[i].wait_recv()
        share(i, 3)
        yield
    own.wait()
    for copy in sent:
        copy.wait_send()
    for copy in passed:
        copy.wait()


def gather_sems():
    dma = pltpu.SemaphoreType.DMA
    return [dma((15,)), dma((15,)), dma((16,)), dma((16,)), dma(())]


def gather_kernel(firsts, *refs):
    count = len(firsts)
    srcs, outs, sems = refs[:count], refs[count : 2 * count], refs[2 * count :]
    spot = Spot()
    greet(spot.neighbours() + [spot.partner])
    drive(
        ring_gather(spot, srcs[a], outs[a], firsts[a], *sems[5 * a : 5 * a + 5])
        for a in range(count)
    )


def gather_plane(arrays, firsts, ident):
    count = len(arrays)
    return comm_call(
        functools.partial(gather_kernel, firsts),
        tuple(jax.ShapeDtypeStruct((16, 2, *a.shape), a.dtype) for a in arrays),
        [sem for _ in arrays for sem in gather_sems()],
        ident,
        pl.ANY,
        pl.ANY,
        count,
        "gather_plane",
    )(*arrays)


def ring_sum(spot, part, out, rows, buf, held, ss, rs, make):
    t, behind, ahead, across = spot.ring(lax.axis_index("tensor"))
    to_ahead, to_behind = {"tensor": ahead}, {"tensor": behind}
    sent = []

    def send(src, dst, idx, to):
        copy = remote(src, dst, ss.at[idx], rs.at[idx], to)
        copy.start()
        sent.append(copy)
        return copy

    make("across", across)
    far = send(part.at[across, rows], buf.at[0, rows], 0, to_ahead)
    make("behind", behind)
    back = send(part.at[behind, rows], buf.at[2, rows], 2, to_behind)
    yield
    make("ahead", ahead)
    far.wait_recv()
    held[rows] = (part[ahead, rows].astype(F32) + buf[0, rows].astype(F32)).astype(BF16)
    on = send(held.at[rows], buf.at[1, rows], 1, to_ahead)
    make("own", t)
    yield
    back.wait_recv()
    on.wait_recv()
    total = part[t, rows].astype(F32) + buf[1, rows].astype(F32) + buf[2, rows].astype(F32)
    out[t, rows] = total.astype(BF16)
    mine, theirs = out.at[t, rows], out.at[behind, rows]
    first = send(mine, mine, 3, to_ahead)
    second = send(mine, mine, 4, to_behind)
    yield
    first.wait_recv()
    third = send(theirs, theirs, 5, to_ahead)
    yield
    second.wait_recv()
    third.wait_recv()
    for copy in sent:
        copy.wait_send()


def direct_sum(vec, vec_out, got, ss, rs):
    t = lax.axis_index("tensor")
    copies = []
    for d in range(3):
        to = {"tensor": lax.rem(t + d + 1, 4)}
        copies.append(remote(vec, got.at[t], ss.at[d], rs.at[d], to))
        copies[-1].start()
    got[t] = vec[...]
    yield
    yield
    yield
    for copy in copies:
        copy.wait()
    vec_out[...] = (got[0] + got[1]) + (got[2] + got[3])


def once(make):
    seen = set()

    def call(key, t):
        if key not in seen:
            seen.add(key)
            make(t)

    return call


def greet_tensor(wait):
    barrier = pltpu.get_barrier_semaphore()
    if wait:
        pl.semaphore_wait(barrier, 3)
    else:
        t = lax.axis_index("tensor")
        for d in range(1, 4):
            to = {"tensor": lax.rem(t + d, 4)}
            pl.semaphore_signal(barrier, inc=1, device_id=to, device_id_type=MESH)


def ring_jobs(spot, part, out, buf, held, sems, make):
    make = once(make)
    return [
        ring_sum(
            spot, part, out, pl.ds(64 * n, 64), buf, held, sems[2 * n], sems[2 * n + 1], make
        )
        for n in range(4)
    ]


def ring_scratch():
    quarters = (4, 256, 256)
    return [
        pltpu.VMEM(quarters, BF16),
        pltpu.VMEM(quarters, BF16),
        pltpu.VMEM((3, 256, 256), BF16),
        pltpu.VMEM((256, 256), BF16),
    ] + [pltpu.SemaphoreType.DMA((6,))] * 8


def quarter(t):
    return pl.ds(pl.multiple_of(t * 256, 256), 256)


def ring_scatter(spot, src, out, first, pair, left, got, ps, pr, ss, rs):
    k = spot.core
    along, other = spot.ring(spot.pos[first]), spot.ring(spot.pos[1 - first])
    kind = pair.dtype

    def place(i, j):
        at = (along[i], other[j])
        return at if first == 0 else at[::-1]

    order = (3, 2, 1, 0)
    theirs = (0, 2, 1, 3)
    pairs, sent = {}, []
    for i in order:
        for j in order:
            at = flat(*place(theirs[i], theirs[j]))
            idx = 4 * i + j
            copy = remote(src.at[at, 1 - k], pair.at[idx], ps.at[idx], pr.at[idx], spot.partner)
            copy.start()
            pairs[idx] = copy
    yield

    def both(i, j):
        pairs[4 * i + j].wait_recv()
        return src[flat(*place(i, j)), k].astype(F32) + pair[4 * i + j].astype(F32)

    def send(value, idx, to):
        left[idx] = value.astype(kind)
        copy = remote(left.at[idx], got.at[idx], ss.at[idx], rs.at[idx], to)
        copy.start()
        sent.append(copy)
        return copy

    ahead1, behind1 = spot.device(*place(2, 0)), spot.device(*place(1, 0))
    ahead2, behind2 = spot.device(*place(0, 2)), spot.device(*place(0, 1))
    far, on, back = {}, {}, {}
    for j in order:
        far[j] = send(both(3, j), j, ahead1)
        back[j] = send(both(1, j), 8 + j, behind1)
        yield
    for j in order:
        far[j].wait_recv()
        on[j] = send(both(2, j) + got[j].astype(F32), 4 + j, ahead1)
        yield

    def settled(j):
        on[j].wait_recv()
        back[j].wait_recv()
        return both(0, j) + got[4 + j].astype(F32) + got[8 + j].astype(F32)

    far2 = send(settled(3), 12, ahead2)
    yield
    ready = settled(2)
    back2 = send(settled(1), 14, behind2)
    yield
    far2.wait_recv()
    on2 = send(ready + got[12].astype(F32), 13, ahead2)
    total = settled(0)
    yield
    back2.wait_recv()
    total = total + got[14].astype(F32)
    on2.wait_recv()
    out[...] = total + got[13].astype(F32)
    for copy in pairs.values():
        copy.wait_send()
    for copy in sent:
        copy.wait_send()


def small_sum(spot, src, shared, pair, sums, got, pp, ss, rs, gs, gr, fs, fr):
    k = spot.core
    p = flat(*spot.pos)
    others = [plane_peer(lax.rem(p + d, 16), k) for d in range(1, 16)]
    first = remote(src.at[:, 1 - k], pair, pp.at[0], pp.at[1], spot.partner)
    first.start()
    yield
    first.wait_recv()
    sums[...] = src[:, k] + pair[...]
    sent = []
    for d, peer in enumerate(others):
        sent.append(
            remote(sums.at[lax.rem(p + d + 1, 16)], got.at[p], ss.at[d], rs.at[d], peer)
        )
        sent[-1].start()
    got[p] = sums[p]
    yield
    for copy in sent:
        copy.wait_recv()
    shared[p, k] = jnp.sum(got[...], axis=0)
    here = shared.at[p, k]
    spread = [remote(here, here, gs.at[d], gr.at[d], peer) for d, peer in enumerate(others)]
    onward = [remote(here, here, fs.at[0], fr.at[0], spot.partner)]
    for copy in spread + onward:
        copy.start()
    yield
    for d in range(1, 16):
        spread[d - 1].wait_recv()
        at = shared.at[lax.rem(p - d + 16, 16), k]
        onward.append(remote(at, at, fs.at[d], fr.at[d], spot.partner))
        onward[-1].start()
    yield
    for copy in [first] + sent + spread:
        copy.wait_send()
    for copy in onward:
        copy.wait()


def plane_peer(p, k):
    return {"batch": p // 8, "seq": lax.rem(p, 8) * 2 + k}


def scatter_kernel(count, *refs):
    ins, outs = refs[: count + 1], refs[count + 1 : 2 * count + 2]
    rest = refs[2 * count + 2 :]
    spot = Spot()
    p = flat(*spot.pos)
    greet([plane_peer(lax.rem(p + d, 16), spot.core) for d in range(1, 16)] + [spot.partner])
    jobs = [small_sum(spot, ins[count], outs[count], *rest[7 * count :])]
    for a in range(count):
        jobs.append(ring_scatter(spot, ins[a], outs[a], a % 2, *rest[7 * a : 7 * a + 7]))
    drive(jobs)


def scatter_scratch(a):
    dma = pltpu.SemaphoreType.DMA
    return [
        pltpu.VMEM((16, *a.shape[2:]), a.dtype),
        pltpu.VMEM((15, *a.shape[2:]), a.dtype),
        pltpu.VMEM((15, *a.shape[2:]), a.dtype),
        dma((16,)),
        dma((16,)),
        dma((15,)),
        dma((15,)),
    ]


def scatter_sum(arrays, small):
    dma = pltpu.SemaphoreType.DMA
    ins = [a.reshape(16, 2, 32, a.shape[1]) for a in arrays] + [small]
    scratch = [item for a in ins[:-1] for item in scatter_scratch(a)]
    scratch += [pltpu.VMEM((16, 8, 128), F32)] * 3
    scratch += [dma((2,)), dma((15,)), dma((15,)), dma((15,)), dma((15,)), dma((16,)), dma((16,))]
    return comm_call(
        functools.partial(scatter_kernel, len(arrays)),
        tuple(jax.ShapeDtypeStruct(a.shape[2:], F32) for a in ins[:-1])
        + (jax.ShapeDtypeStruct(small.shape, F32),),
        scratch,
        8,
        pltpu.VMEM,
        pltpu.VMEM,
        len(ins),
        "scatter_sum",
    )(*ins)


def turned(values, cosine, sine):
    lane = lax.broadcasted_iota(jnp.int32, values.shape, 1)
    swapped = jnp.where(
        lane < 8, pltpu.roll(values, 120, axis=1), pltpu.roll(values, 8, axis=1)
    )
    return values * cosine + swapped * sine


def normal(values):
    centred = values - jnp.mean(values, axis=-1, keepdims=True)
    rstd = lax.rsqrt(jnp.mean(centred * centred, axis=-1, keepdims=True) + 1e-05)
    return centred * rstd, rstd


def with_branch(x, branch, shift, out):
    for t in range(4):
        at = slice(256 * t, 256 * (t + 1))
        out[:, at] = x[:, at] + branch[t].astype(F32) + shift[:, at]


def norm_back(grad, z, x, out):
    hat, rstd = normal(x[...])
    flow = jnp.concatenate([z[t].astype(F32) for t in range(4)], axis=1)
    out[...] = grad[...] + rstd * (
        flow
        - jnp.mean(flow, axis=-1, keepdims=True)
        - hat * jnp.mean(flow * hat, axis=-1, keepdims=True)
    )


def project_kernel(x, g1, b1, g2, b2, bias, weight, cosine, sine, h1, h2, qkv):
    hat, _ = normal(x[...])
    h1[...] = (hat * g1[...] + b1[...]).astype(BF16)
    h2[...] = (hat * g2[...] + b2[...]).astype(BF16)
    proj = dot(h1[...], weight[...], 1, 0) + bias[...]
    cos, sin = cosine[...], sine[...]
    lane = lax.broadcasted_iota(jnp.int32, (128, 128), 1)
    for m in range(2):
        rows = proj[m * 128 : (m + 1) * 128]
        for h in range(4):
            pair = rows[:, 128 * h : 128 * (h + 1)]
            qkv[m * 4 + h, 0] = turned(pair, cos, sin).astype(BF16)
            q = rows[:, 512 + 128 * (h // 2) : 640 + 128 * (h // 2)]
            if h % 2:
                q = pltpu.roll(q, 64, axis=1)
            q = turned(q, cos, sin) * 0.125
            qkv[m * 4 + h, 1] = jnp.where(lane < 64, q, 0.0).astype(BF16)


def local_call(body, out_shape, in_specs, name, scratch=()):
    return pl.pallas_call(
        body,
        out_shape=out_shape,
        grid=(1,),
        in_specs=in_specs,
        out_specs=jax.tree.map(lambda o: whole(o.shape), out_shape),
        scratch_shapes=scratch,
        compiler_params=pltpu.CompilerParams(vmem_limit_bytes=VLIM),
        name=name,
    )


def whole(shape):
    return pl.BlockSpec(shape, lambda i: (0,) * len(shape))


def wholes(*arrays):
    return [whole(a.shape) for a in arrays]


def project(*args):
    sds = jax.ShapeDtypeStruct
    return local_call(
        project_kernel,
        (
            sds((256, 1024), BF16),
            sds((256, 1024), BF16),
            sds((8, 2, 128, 128), BF16),
        ),
        wholes(*args),
        "project",
    )(*args)


def scores_of(q, keys, low, high):
    s = dot(q, keys, 1, 1)
    place = lax.broadcasted_iota(jnp.int32, s.shape, 1)
    return jnp.where((place >= low) & (place <= high), s, MASKED)


def to_chip(i, src, dst, ss, rs, local):
    _, c, k = places()
    far = remote(src, dst, ss, rs, {"seq": 2 * i + k})
    near = pltpu.make_async_copy(src, dst, local)

    @pl.when(c != i)
    def _():
        far.start()

    @pl.when(c == i)
    def _():
        near.start()

    def left():
        @pl.when(c != i)
        def _():
            far.wait_send()

        @pl.when(c == i)
        def _():
            near.wait()

    return left


def from_chip(i, dst, ss, rs):
    _, c, k = places()

    @pl.when(c != i)
    def _():
        remote(dst, dst, ss, rs, {"seq": 2 * i + k}).wait_recv()


def seq_peers(spot):
    x, y = spot.pos
    ys = spot.ring(y)
    return chip_peers() + [spot.device(x, ys[1]), spot.device(x, ys[2]), spot.partner]


def attention(spot, src, low, high, kv_out, q_out, lse, ctx_in, ctx_out, *sems):
    ssem, rsem, fs, fr, lsem, cs, cr, cl = sems
    s, c, k = places()
    others = chip_peers()
    copies, copies_q = [], []
    for d, peer in enumerate(others):
        c2 = lax.rem(c + d + 1, 8)
        copies.append(remote(src.at[c2, 0], kv_out.at[s], ssem.at[0, d], rsem.at[0, d], peer))
        copies[-1].start()
    for d, peer in enumerate(others):
        c2 = lax.rem(c + d + 1, 8)
        copies_q.append(remote(src.at[c2, 1], q_out.at[c], ssem.at[1, d], rsem.at[1, d], peer))
        copies_q[-1].start()
    onward = [remote(src.at[c, 0], kv_out.at[s], fs.at[0], fr.at[0], spot.partner)]
    onward[0].start()
    own_kv = pltpu.make_async_copy(src.at[c, 0], kv_out.at[s], lsem.at[0])
    own_q = pltpu.make_async_copy(src.at[c, 1], q_out.at[c], lsem.at[1])
    own_kv.start()
    own_q.start()
    yield
    for d in range(1, 8):
        copies[d - 1].wait_recv()
        at = kv_out.at[lax.rem(c - d + 8, 8) * 2 + k]
        copy = remote(at, at, fs.at[d], fr.at[d], spot.partner)
        copy.start()
        onward.append(copy)
        if d % 2:
            yield
    own_kv.wait()
    own_q.wait()
    for copy in copies_q:
        copy.wait_recv()
    for copy in onward:
        copy.wait_recv()
    left = []
    for i in reversed(range(8)):
        n = 256 * (i + 1)
        keys = kv_out[0 : 2 * (i + 1)].reshape(n, 128)
        sc = scores_of(q_out[i], keys, low[i], high[i])
        top = jnp.max(sc, axis=-1, keepdims=True)
        e = jnp.exp(sc - top)
        total = jnp.sum(e, axis=-1, keepdims=True)
        soft = (e * (1.0 / total)).astype(BF16)
        ctx_out[i] = dot(soft, keys, 1, 0).astype(BF16)
        lse[i] = top + jnp.log(total)
        left.append(to_chip(i, ctx_out.at[i], ctx_in.at[c], cs.at[i], cr.at[c], cl))
        yield
    for i in reversed(range(8)):
        from_chip(i, ctx_in.at[i], cs.at[i], cr.at[i])
    for wait in left:
        wait()
    for copy in copies + copies_q + onward:
        copy.wait_send()


def attention_kernel(firsts, *refs):
    count = len(firsts)
    (src, low, high), srcs = refs[:3], refs[3 : 3 + count]
    refs = refs[3 + count :]
    (kv, q, lse, ctx_in), outs = refs[:4], refs[4 : 4 + count]
    refs = refs[4 + count :]
    spot = Spot()
    greet(seq_peers(spot))
    ctx_out, *sems = refs[:9]
    jobs = [attention(spot, src, low, high, kv, q, lse, ctx_in, ctx_out, *sems)]
    rest = refs[9:]
    for a in range(count):
        jobs.append(ring_gather(spot, srcs[a], outs[a], firsts[a], *rest[5 * a : 5 * a + 5]))
    drive(jobs)


def attend(qkv, low, high, shards, firsts, ident):
    sds, dma, count = jax.ShapeDtypeStruct, pltpu.SemaphoreType.DMA, len(shards)
    vmem, hbm = pl.BlockSpec(memory_space=pltpu.VMEM), pl.BlockSpec(memory_space=pl.ANY)
    return pl.pallas_call(
        functools.partial(attention_kernel, firsts),
        out_shape=(
            sds((16, 128, 128), BF16),
            sds((8, 128, 128), BF16),
            sds((8, 128, 1), F32),
            sds((8, 128, 128), BF16),
        )
        + tuple(sds((16, 2, *a.shape), a.dtype) for a in shards),
        in_specs=[vmem] * 3 + [hbm] * count,
        out_specs=[vmem] * 4 + [hbm] * count,
        scratch_shapes=[
            pltpu.VMEM((8, 128, 128), BF16),
            dma((2, 7)),
            dma((2, 7)),
            dma((8,)),
            dma((8,)),
            dma((2,)),
            dma((8,)),
            dma((8,)),
            dma(()),
        ]
        + [sem for _ in shards for sem in gather_sems()],
        compiler_params=pltpu.CompilerParams(
            collective_id=ident, has_side_effects=True, vmem_limit_bytes=VLIM
        ),
        name="attend",
    )(qkv, low, high, *shards)


def attention_back(
    spot, dctx, kv, q, lse, low, high, dq_in, dkv_in, dctx_in, dq, total, other, summed, *sems
):
    ds_, dr, dl, qs, qr, ql, ps, pr, ks, kr, kl = sems
    _, c, k = places()
    copies = []
    for d, peer in enumerate(chip_peers()):
        c2 = lax.rem(c + d + 1, 8)
        copies.append(remote(dctx.at[c2], dctx_in.at[c], ds_.at[d], dr.at[c], peer))
        copies[-1].start()
    own = pltpu.make_async_copy(dctx.at[c], dctx_in.at[c], dl)
    own.start()
    own.wait()
    yield
    left, pairs = [], {}

    def finish(i):
        pairs[i].wait_recv()
        summed[i] = (total[2 * i + k] + other[i]).astype(BF16)
        left.append(to_chip(i, summed.at[i], dkv_in.at[c], ks.at[i], kr.at[c], kl))

    for i in reversed(range(8)):
        n, blocks = 256 * (i + 1), 2 * (i + 1)
        from_chip(i, dctx_in.at[i], ds_.at[0], dr.at[i])
        keys = kv[0:blocks].reshape(n, 128)
        sc = scores_of(q[i], keys, low[i], high[i])
        soft = jnp.exp(sc - lse[i])
        dsoft = dot(dctx_in[i], keys, 1, 1)
        term = jnp.sum(soft * dsoft, axis=-1, keepdims=True)
        dscore = (soft * (dsoft - term)).astype(BF16)
        dq[i] = (dot(dscore, keys, 1, 0) * 0.125).astype(BF16)
        left.append(to_chip(i, dq.at[i], dq_in.at[c], qs.at[i], qr.at[c], ql))
        both = jnp.concatenate([dscore, soft.astype(BF16)], axis=0)
        right = jnp.concatenate([q[i], dctx_in[i]], axis=0)
        fresh = dot(both, right, 0, 0).reshape(blocks, 128, 128)
        if i == 7:
            total[...] = fresh
        else:
            total[0:blocks] += fresh
        pairs[i] = remote(total.at[2 * i + 1 - k], other.at[i], ps.at[i], pr.at[i], spot.partner)
        pairs[i].start()
        if i < 7:
            finish(i + 1)
        yield
    finish(0)
    for copy in pairs.values():
        copy.wait_send()
    yield
    for i in reversed(range(8)):
        from_chip(i, dq_in.at[i], qs.at[i], qr.at[i])
        from_chip(i, dkv_in.at[i], ks.at[i], kr.at[i])
    for wait in left:
        wait()
    for copy in copies:
        copy.wait_send()


def attention_back_kernel(firsts, *refs):
    count = len(firsts)
    ins, srcs = refs[:6], refs[6 : 6 + count]
    refs = refs[6 + count :]
    outs, sums = refs[:2], refs[2 : 2 + count]
    refs = refs[2 + count :]
    spot = Spot()
    greet(seq_peers(spot))
    jobs = [attention_back(spot, *ins, *outs, *refs[:16])]
    rest = refs[16:]
    for a in range(count):
        jobs.append(ring_scatter(spot, srcs[a], sums[a], firsts[a], *rest[7 * a : 7 * a + 7]))
    drive(jobs)


def attend_back(dctx, kv, q, lse, low, high, arrays, firsts, ident):
    sds, dma = jax.ShapeDtypeStruct, pltpu.SemaphoreType.DMA
    vmem = pl.BlockSpec(memory_space=pltpu.VMEM)
    ins = [a.reshape(16, 2, 32, a.shape[1]) for a in arrays]
    block, wide = (8, 128, 128), (16, 128, 128)
    return pl.pallas_call(
        functools.partial(attention_back_kernel, firsts),
        out_shape=(sds(block, BF16), sds(block, BF16))
        + tuple(sds(a.shape[2:], F32) for a in ins),
        in_specs=[vmem] * (6 + len(ins)),
        out_specs=[vmem] * (2 + len(ins)),
        scratch_shapes=[
            pltpu.VMEM(block, BF16),
            pltpu.VMEM(block, BF16),
            pltpu.VMEM(wide, F32),
            pltpu.VMEM(block, F32),
            pltpu.VMEM(block, BF16),
            dma((7,)),
            dma((8,)),
            dma(()),
            dma((8,)),
            dma((8,)),
            dma(()),
            dma((8,)),
            dma((8,)),
            dma((8,)),
            dma((8,)),
            dma(()),
        ]
        + [item for a in ins for item in scatter_scratch(a)],
        compiler_params=pltpu.CompilerParams(
            collective_id=ident, has_side_effects=True, vmem_limit_bytes=VLIM
        ),
        name="attend_back",
    )(dctx, kv, q, lse, low, high, *ins)


def feed_kernel(
    x, ctx_in, h2, outer, expand, bias, shift, u, both, x_out, part, out, buf, held, *sems
):
    greet_tensor(False)
    spot = Spot()
    lane = lax.broadcasted_iota(jnp.int32, (128, 128), 1)
    for m in range(2):
        for h in range(2):
            left = pltpu.roll(ctx_in[m * 4 + 2 * h].astype(F32), 64, axis=1)
            right = ctx_in[m * 4 + 2 * h + 1].astype(F32)
            both[m * 128 : (m + 1) * 128, 128 * h : 128 * (h + 1)] = jnp.where(
                lane < 64, left, right
            ).astype(BF16)
    inner = dot(h2[...], expand[...], 1, 0) + bias[...]
    u[...] = inner
    both[:, 256:] = (0.5 * inner * (1.0 + lax.erf(inner * 0.7071067811865476))).astype(BF16)
    greet_tensor(True)

    def make(t):
        part[t] = dot(both[...], outer[quarter(t), :], 1, 1).astype(BF16)

    drive(ring_jobs(spot, part, out, buf, held, sems, make))
    with_branch(x, out, shift, x_out)


def feed(*args):
    sds = jax.ShapeDtypeStruct
    return comm_call(
        feed_kernel,
        (sds((256, 1024), F32), sds((256, 1280), BF16), sds((256, 1024), F32)),
        ring_scratch(),
        6,
        pltpu.VMEM,
        pltpu.VMEM,
        len(args),
        "feed",
    )(*args)


def feed_back_kernel(grad, x, g2, u, both, h2, outer, expand, dctx, w_outer, w_expand, z2, small):
    gb = grad[...].astype(BF16)
    dact = dot(gb, outer[:, 256:], 1, 0)
    inner = u[...]
    slope = 0.5 * (1.0 + lax.erf(inner * 0.7071067811865476)) + inner * (
        0.3989422804014327 * jnp.exp(-0.5 * inner * inner)
    )
    du = (dact * slope).astype(BF16)
    dc = dot(gb, outer[:, :256], 1, 0)
    lane = lax.broadcasted_iota(jnp.int32, (128, 128), 1)
    for m in range(2):
        for h in range(4):
            piece = dc[m * 128 : (m + 1) * 128, 128 * (h // 2) : 128 * (h // 2 + 1)]
            if h % 2 == 0:
                piece = pltpu.roll(piece, 64, axis=1)
            dctx[m * 4 + h] = jnp.where(lane >= 64, piece, 0.0).astype(BF16)
    w_outer[...] = dot(gb, both[...], 0, 0).astype(BF16)
    w_expand[...] = dot(h2[...], du, 0, 0).astype(BF16)
    dh2 = dot(du, expand[...], 1, 1)
    hat, _ = normal(x[...])
    z2[...] = dh2 * g2[...]
    small[0:1] = jnp.sum(dh2 * hat, axis=0, keepdims=True)
    small[1:2] = jnp.sum(dh2, axis=0, keepdims=True)
    small[2:3] = jnp.sum(gb.astype(F32), axis=0, keepdims=True)
    small[3:4] = jnp.sum(du.astype(F32), axis=0, keepdims=True)


def feed_back(*args):
    sds = jax.ShapeDtypeStruct
    return local_call(
        feed_back_kernel,
        (
            sds((8, 128, 128), BF16),
            sds((1024, 1280), BF16),
            sds((1024, 1024), BF16),
            sds((256, 1024), F32),
            sds((4, 1024), F32),
        ),
        wholes(*args),
        "feed_back",
    )(*args)


def project_back_kernel(
    dq, dkv, cosine, sine, h1, weight, z2, x, g1, small2, grad, *refs
):
    w_left, w_right, small, bias_grad, grad_out = refs[:5]
    dproj, hat, vec, got, vs, vr, part, out, buf, held, *sems = refs[5:]
    greet_tensor(False)
    spot = Spot()
    cos, sin = cosine[...], -sine[...]
    lane = lax.broadcasted_iota(jnp.int32, (128, 128), 1)
    for m in range(2):
        rows = pl.ds(m * 128, 128)
        for h in range(4):
            dproj[rows, 128 * h : 128 * (h + 1)] = turned(
                dkv[m * 4 + h].astype(F32), cos, sin
            ).astype(BF16)
        for h in range(2):
            left = turned(dq[m * 4 + 2 * h].astype(F32), cos, sin)
            right = turned(dq[m * 4 + 2 * h + 1].astype(F32), cos, sin)
            dproj[rows, 512 + 128 * h : 640 + 128 * h] = jnp.where(
                lane < 64, left, pltpu.roll(right, 64, axis=1)
            ).astype(BF16)
    dp = dproj[...]
    hat[...] = normal(x[...])[0]
    vec[2:4] = small2[0:2]
    greet_tensor(True)

    def make(t):
        at = quarter(t)
        dh1 = dot(dp, weight[at, :], 1, 1)
        vec[0:1, at] = jnp.sum(dh1 * hat[:, at], axis=0, keepdims=True)
        vec[1:2, at] = jnp.sum(dh1, axis=0, keepdims=True)
        part[t] = (dh1 * g1[:, at] + z2[:, at]).astype(BF16)

    def beside():
        yield
        yield
        yield from direct_sum(vec, small, got, vs, vr)

    def weights():
        yield
        fresh = dot(h1[...], dp, 0, 0).astype(BF16)
        w_left[...] = fresh[:, :384]
        w_right[...] = fresh[:, 384:]
        bias_grad[...] = jnp.sum(dp.astype(F32), axis=0, keepdims=True)

    drive(ring_jobs(spot, part, out, buf, held, sems, make) + [weights(), beside()])
    norm_back(grad, out, x, grad_out)


def project_back(*args):
    sds, dma = jax.ShapeDtypeStruct, pltpu.SemaphoreType.DMA
    return comm_call(
        project_back_kernel,
        (
            sds((1024, 384), BF16),
            sds((1024, 384), BF16),
            sds((4, 1024), F32),
            sds((1, 768), F32),
            sds((256, 1024), F32),
        ),
        [
            pltpu.VMEM((256, 768), BF16),
            pltpu.VMEM((256, 1024), F32),
            pltpu.VMEM((4, 1024), F32),
            pltpu.VMEM((4, 4, 1024), F32),
            dma((3,)),
            dma((3,)),
        ]
        + ring_scratch(),
        7,
        pltpu.VMEM,
        pltpu.VMEM,
        len(args),
        "project_back",
    )(*args)


def head_order(value):
    lead = value.shape[:-1]
    parts = value.reshape(*lead, 4, 3, HEAD)
    keys = parts[..., 1:3, :].reshape(*lead, 512)
    return jnp.concatenate([keys, parts[..., 0, :].reshape(*lead, 256)], axis=-1)


def head_order_back(value):
    lead = value.shape[:-1]
    keys = value[..., :512].reshape(*lead, 4, 2, HEAD)
    queries = value[..., 512:].reshape(*lead, 4, 1, HEAD)
    return jnp.concatenate([queries, keys], axis=-2).reshape(*lead, 768)


def from_quarters(value):
    return value.transpose(1, 0, 2).reshape(256, 1024).astype(F32)


def local(
    hidden_in,
    document_ids,
    first_gain,
    first_shift,
    second_gain,
    second_shift,
    attn_weight,
    attn_bias,
    dense_weight,
    dense_bias,
    expand_weight,
    expand_bias,
    shrink_weight,
    shrink_bias,
    output_grad,
):
    seq_at = lax.axis_index("seq")
    chip, core = seq_at // 2, lax.rem(seq_at, 2)
    unit_micro = chip // 4
    lead = jnp.arange(ROT // 2, dtype=F32) * 2
    inverse = 10000.0 ** (-lead / ROT)
    place = (seq_at * 128 + jnp.arange(128, dtype=jnp.int32)).astype(F32)
    angles = place[:, None] * inverse[None, :]
    cos, sin = jnp.cos(angles), jnp.sin(angles)
    ones, zeros = jnp.ones((128, 112), F32), jnp.zeros((128, 112), F32)
    cosine = jnp.concatenate([cos, cos, ones], axis=1)
    sine = jnp.concatenate([-sin, sin, zeros], axis=1)

    attn = head_order(attn_weight)
    outer = jnp.concatenate(
        [jnp.swapaxes(dense_weight, 1, 2), jnp.swapaxes(shrink_weight, 1, 2)], axis=2
    )
    idents = jnp.pad(document_ids[:, 0], ((0, 6), (0, 0)))
    weight, idents = gather_plane([attn[0], idents], (0, 1), 1)
    weight = weight.reshape(1024, 768)
    idents = idents.reshape(2, 16, 8, 128)
    idents = lax.dynamic_index_in_dim(idents, lax.axis_index("batch"), 0, keepdims=False)
    mine = lax.dynamic_index_in_dim(idents, unit_micro, 1, keepdims=False).reshape(2048)
    count0 = jnp.sum((mine == 0).astype(jnp.int32))
    count1 = jnp.sum((mine == 1).astype(jnp.int32))
    start = jnp.where(mine == 0, 0, jnp.where(mine == 1, count0, count0 + count1))
    high = jnp.arange(2048, dtype=jnp.int32).reshape(8, 2, 128)
    high = lax.dynamic_index_in_dim(high, core, 1, keepdims=False)[..., None]
    low = lax.dynamic_index_in_dim(start.reshape(8, 2, 128), core, 1, keepdims=False)[..., None]
    bias_order = head_order(attn_bias)

    x = hidden_in.reshape(256, 1024)
    shift = dense_bias + shrink_bias
    kept = []
    for layer in range(LAYERS):
        row = slice(layer, layer + 1)
        h1, h2, qkv = project(
            x,
            first_gain[row],
            first_shift[row],
            second_gain[row],
            second_shift[row],
            bias_order[row],
            weight,
            cosine,
            sine,
        )
        shards = [outer[layer], expand_weight[layer]] + ([attn[1]] if layer == 0 else [])
        kv, q, lse, ctx_in, *wide = attend(
            qkv, low, high, shards, (0, 1, 1)[: len(shards)], 2 + layer
        )
        wide = [w.reshape(1024, w.shape[3]) for w in wide]
        u, both, x_next = feed(x, ctx_in, h2, *wide[:2], expand_bias[row], shift[row])
        kept.append((x, h1, h2, kv, q, lse, u, both, weight, wide[:2]))
        weight, x = wide[-1], x_next
    hidden_out = x.reshape(2, 1, 128, 1024)

    grad = output_grad.reshape(256, 1024)
    by_all, by_rows = [None] * 2, [None] * 2
    pending, sums = [], []
    for layer in reversed(range(LAYERS)):
        row = slice(layer, layer + 1)
        x, h1, h2, kv, q, lse, u, both, weight, wide = kept[layer]
        dctx, w_outer, w_expand, z2, small2 = feed_back(
            grad, x, second_gain[row], u, both, h2, *wide
        )
        arrays = [w_outer, w_expand] + pending
        dq_in, dkv_in, *ready = attend_back(
            dctx, kv, q, lse, low, high, arrays, (0, 1, 0, 1)[: len(arrays)], 4 + layer
        )
        sums += ready
        *pending, by_all[layer], bias_grad, grad = project_back(
            dq_in, dkv_in, cosine, sine, h1, weight, z2, x, first_gain[row], small2, grad
        )
        by_rows[layer] = jnp.concatenate([bias_grad[0], small2[2], small2[3]], axis=0)
    input_grad = grad.reshape(2, 1, 128, 1024)

    small = jnp.concatenate([v.reshape(-1) for v in by_all + by_rows]).reshape(32, 432)
    small = jnp.pad(small, ((0, 0), (0, 592))).reshape(16, 2, 8, 128)
    left, right, small = scatter_sum(pending, small)
    narrow_sum = jnp.stack(
        [jnp.concatenate([left, right], axis=1), jnp.concatenate(sums[4:6], axis=1)]
    )
    narrow_sum = head_order_back(narrow_sum)
    outer_sum, expand_sum = jnp.stack([sums[2], sums[0]]), jnp.stack([sums[3], sums[1]])
    small = small.reshape(32, 1024)[:, :432].reshape(13824)
    norms, rows = small[:8192].reshape(2, 4, 1024), small[8192:].reshape(2, 2816)
    branch_bias = rows[:, 768:1792]
    return (
        hidden_out,
        input_grad,
        norms[:, 0],
        norms[:, 1],
        norms[:, 2],
        norms[:, 3],
        narrow_sum,
        head_order_back(rows[:, :768]),
        jnp.swapaxes(outer_sum[..., :256], 1, 2),
        branch_bias,
        expand_sum,
        rows[:, 1792:],
        jnp.swapaxes(outer_sum[..., 256:], 1, 2),
        branch_bias,
    )


def solution(mesh):
    rows, spread, split = P(None, "batch", "seq", None), P(None, ("batch", "seq"), "tensor"), P(
        None, "tensor"
    )
    across = P(None, "tensor", ("batch", "seq"))
    return jax.shard_map(
        local,
        mesh=mesh,
        in_specs=(
            rows,
            P(None, "batch", "seq"),
            P(),
            P(),
            P(),
            P(),
            spread,
            split,
            across,
            P(),
            spread,
            split,
            across,
            P(),
            rows,
        ),
        out_specs=(
            rows,
            rows,
            P(),
            P(),
            P(),
            P(),
            spread,
            split,
            across,
            P(),
            spread,
            split,
            across,
            P(),
        ),
        check_vma=False,
    )
```

```python
import functools

import jax
import jax.numpy as jnp
from jax import lax
from jax.experimental import pallas as pl
from jax.experimental.pallas import tpu as pltpu
from jax.sharding import PartitionSpec as P

HEAD = 64
ROT = 16
LAYERS = 2
MASKED = -1000000000.0
MESH = pl.DeviceIdType.MESH
F32, BF16 = jnp.float32, jnp.bfloat16
VLIM = 56 * 1024 * 1024


def dot(a, b, ca, cb):
    return lax.dot_general(a, b, (((ca,), (cb,)), ((), ())), preferred_element_type=F32)


def places():
    s = lax.axis_index("seq")
    return s, s // 2, lax.rem(s, 2)


def greet(peers):
    barrier = pltpu.get_barrier_semaphore()
    for peer in peers:
        pl.semaphore_signal(barrier, inc=1, device_id=peer, device_id_type=MESH)
    pl.semaphore_wait(barrier, len(peers))


def remote(src, dst, send, recv, peer):
    return pltpu.make_async_remote_copy(
        src_ref=src, dst_ref=dst, send_sem=send, recv_sem=recv, device_id=peer, device_id_type=MESH
    )


def chip_peers():
    _, c, k = places()
    return [{"seq": lax.rem(c + d, 8) * 2 + k} for d in range(1, 8)]


def comm_call(body, out_shape, scratch, ident, in_space, out_space, n_in, name):
    single = not isinstance(out_shape, (tuple, list))
    return pl.pallas_call(
        body,
        out_shape=out_shape,
        in_specs=[pl.BlockSpec(memory_space=in_space)] * n_in,
        out_specs=pl.BlockSpec(memory_space=out_space)
        if single
        else [pl.BlockSpec(memory_space=out_space)] * len(out_shape),
        scratch_shapes=scratch,
        compiler_params=pltpu.CompilerParams(
            collective_id=ident, has_side_effects=True, vmem_limit_bytes=VLIM
        ),
        name=name,
    )


class Spot:
    def __init__(self):
        b = lax.axis_index("batch")
        s, c, self.core = places()
        self.pos = (lax.rem(c, 4), (c // 4) * 2 + b)
        self.partner = {"seq": s + 1 - 2 * self.core}

    def ring(self, r):
        k = self.core
        return [r, lax.rem(r + 3 - 2 * k, 4), lax.rem(r + 1 + 2 * k, 4), lax.rem(r + 2, 4)]

    def device(self, x, y):
        return {"batch": lax.rem(y, 2), "seq": ((y // 2) * 4 + x) * 2 + self.core}

    def neighbours(self):
        x, y = self.pos
        xs, ys = self.ring(x), self.ring(y)
        return [self.device(x2, y) for x2 in xs[1:3]] + [self.device(x, y2) for y2 in ys[1:3]]


def flat(x, y):
    return lax.rem(y, 2) * 8 + (y // 2) * 4 + x


def drive(jobs):
    jobs = list(jobs)
    while jobs:
        for job in list(jobs):
            try:
                next(job)
            except StopIteration:
                jobs.remove(job)


def ring_gather(spot, src, out, first, ss, rs, fs, fr, ls):
    k = spot.core
    along, other = spot.ring(spot.pos[first]), spot.ring(spot.pos[1 - first])

    def place(i, j):
        at = (along[i], other[j])
        return at if first == 0 else at[::-1]

    def slot(i, j):
        return out.at[flat(*place(i, j)), k]

    sent, passed = [], []

    def send(i, j, idx, to):
        piece = slot(i, j)
        copy = remote(src if (i, j) == (0, 0) else piece, piece, ss.at[idx], rs.at[idx], to)
        copy.start()
        sent.append(copy)
        return copy

    def share(i, j):
        piece, idx = slot(i, j), 4 * i + j
        copy = remote(
            src if idx == 0 else piece, piece, fs.at[idx], fr.at[idx], spot.partner
        )
        copy.start()
        passed.append(copy)

    ahead1, behind1 = spot.device(*place(2, 0)), spot.device(*place(1, 0))
    ahead2, behind2 = spot.device(*place(0, 2)), spot.device(*place(0, 1))
    own = pltpu.make_async_copy(src, slot(0, 0), ls)
    own.start()
    m0 = send(0, 0, 0, ahead1)
    m1 = send(0, 0, 1, behind1)

    def second(i):
        return send(i, 0, 3 + 3 * i, ahead2), send(i, 0, 4 + 3 * i, behind2)

    n = {0: second(0)}
    share(0, 0)
    yield
    m0.wait_recv()
    m2 = send(1, 0, 2, ahead1)
    n[1] = second(1)
    share(1, 0)
    yield
    m1.wait_recv()
    n[2] = second(2)
    share(2, 0)
    yield
    far = {}

    def middle(i):
        n[i][0].wait_recv()
        far[i] = send(i, 1, 5 + 3 * i, ahead2)
        share(i, 1)
        n[i][1].wait_recv()
        share(i, 2)

    middle(0)
    yield
    m2.wait_recv()
    n[3] = second(3)
    share(3, 0)
    yield
    for i in range(1, 4):
        middle(i)
        yield
    for i in range(4):
        far[i].wait_recv()
        share(i, 3)
        yield
    own.wait()
    for copy in sent:
        copy.wait_send()
    for copy in passed:
        copy.wait()


def gather_sems():
    dma = pltpu.SemaphoreType.DMA
    return [dma((15,)), dma((15,)), dma((16,)), dma((16,)), dma(())]


def gather_kernel(firsts, *refs):
    count = len(firsts)
    srcs, outs, sems = refs[:count], refs[count : 2 * count], refs[2 * count :]
    spot = Spot()
    greet(spot.neighbours() + [spot.partner])
    drive(
        ring_gather(spot, srcs[a], outs[a], firsts[a], *sems[5 * a : 5 * a + 5])
        for a in range(count)
    )


def gather_plane(arrays, firsts, ident):
    count = len(arrays)
    return comm_call(
        functools.partial(gather_kernel, firsts),
        tuple(jax.ShapeDtypeStruct((16, 2, *a.shape), a.dtype) for a in arrays),
        [sem for _ in arrays for sem in gather_sems()],
        ident,
        pl.ANY,
        pl.ANY,
        count,
        "gather_plane",
    )(*arrays)


def ring_sum(spot, part, out, rows, buf, held, ss, rs, make):
    t, behind, ahead, across = spot.ring(lax.axis_index("tensor"))
    to_ahead, to_behind = {"tensor": ahead}, {"tensor": behind}
    sent = []

    def send(src, dst, idx, to):
        copy = remote(src, dst, ss.at[idx], rs.at[idx], to)
        copy.start()
        sent.append(copy)
        return copy

    make("across", across)
    far = send(part.at[across, rows], buf.at[0, rows], 0, to_ahead)
    make("behind", behind)
    back = send(part.at[behind, rows], buf.at[2, rows], 2, to_behind)
    yield
    make("ahead", ahead)
    far.wait_recv()
    held[rows] = (part[ahead, rows].astype(F32) + buf[0, rows].astype(F32)).astype(BF16)
    on = send(held.at[rows], buf.at[1, rows], 1, to_ahead)
    make("own", t)
    yield
    back.wait_recv()
    on.wait_recv()
    total = part[t, rows].astype(F32) + buf[1, rows].astype(F32) + buf[2, rows].astype(F32)
    out[t, rows] = total.astype(BF16)
    mine, theirs = out.at[t, rows], out.at[behind, rows]
    first = send(mine, mine, 3, to_ahead)
    second = send(mine, mine, 4, to_behind)
    yield
    first.wait_recv()
    third = send(theirs, theirs, 5, to_ahead)
    yield
    second.wait_recv()
    third.wait_recv()
    for copy in sent:
        copy.wait_send()


def direct_sum(vec, vec_out, got, ss, rs):
    t = lax.axis_index("tensor")
    copies = []
    for d in range(3):
        to = {"tensor": lax.rem(t + d + 1, 4)}
        copies.append(remote(vec, got.at[t], ss.at[d], rs.at[d], to))
        copies[-1].start()
    got[t] = vec[...]
    yield
    yield
    yield
    for copy in copies:
        copy.wait()
    vec_out[...] = (got[0] + got[1]) + (got[2] + got[3])


def once(make):
    seen = set()

    def call(key, t):
        if key not in seen:
            seen.add(key)
            make(t)

    return call


def greet_tensor(wait):
    barrier = pltpu.get_barrier_semaphore()
    if wait:
        pl.semaphore_wait(barrier, 3)
    else:
        t = lax.axis_index("tensor")
        for d in range(1, 4):
            to = {"tensor": lax.rem(t + d, 4)}
            pl.semaphore_signal(barrier, inc=1, device_id=to, device_id_type=MESH)


def ring_jobs(spot, part, out, buf, held, sems, make):
    make = once(make)
    return [
        ring_sum(
            spot, part, out, pl.ds(64 * n, 64), buf, held, sems[2 * n], sems[2 * n + 1], make
        )
        for n in range(4)
    ]


def ring_scratch():
    quarters = (4, 256, 256)
    return [
        pltpu.VMEM(quarters, BF16),
        pltpu.VMEM(quarters, BF16),
        pltpu.VMEM((3, 256, 256), BF16),
        pltpu.VMEM((256, 256), BF16),
    ] + [pltpu.SemaphoreType.DMA((6,))] * 8


def quarter(t):
    return pl.ds(pl.multiple_of(t * 256, 256), 256)


def ring_scatter(spot, src, out, first, pair, left, got, ps, pr, ss, rs):
    k = spot.core
    along, other = spot.ring(spot.pos[first]), spot.ring(spot.pos[1 - first])
    kind = pair.dtype

    def place(i, j):
        at = (along[i], other[j])
        return at if first == 0 else at[::-1]

    order = (3, 2, 1, 0)
    theirs = (0, 2, 1, 3)
    pairs, sent = {}, []
    for i in order:
        for j in order:
            at = flat(*place(theirs[i], theirs[j]))
            idx = 4 * i + j
            copy = remote(src.at[at, 1 - k], pair.at[idx], ps.at[idx], pr.at[idx], spot.partner)
            copy.start()
            pairs[idx] = copy
    yield

    def both(i, j):
        pairs[4 * i + j].wait_recv()
        return src[flat(*place(i, j)), k].astype(F32) + pair[4 * i + j].astype(F32)

    def send(value, idx, to):
        left[idx] = value.astype(kind)
        copy = remote(left.at[idx], got.at[idx], ss.at[idx], rs.at[idx], to)
        copy.start()
        sent.append(copy)
        return copy

    ahead1, behind1 = spot.device(*place(2, 0)), spot.device(*place(1, 0))
    ahead2, behind2 = spot.device(*place(0, 2)), spot.device(*place(0, 1))
    far, on, back = {}, {}, {}
    for j in order:
        far[j] = send(both(3, j), j, ahead1)
        back[j] = send(both(1, j), 8 + j, behind1)
        yield
    for j in order:
        far[j].wait_recv()
        on[j] = send(both(2, j) + got[j].astype(F32), 4 + j, ahead1)
        yield

    def settled(j):
        on[j].wait_recv()
        back[j].wait_recv()
        return both(0, j) + got[4 + j].astype(F32) + got[8 + j].astype(F32)

    far2 = send(settled(3), 12, ahead2)
    yield
    ready = settled(2)
    back2 = send(settled(1), 14, behind2)
    yield
    far2.wait_recv()
    on2 = send(ready + got[12].astype(F32), 13, ahead2)
    total = settled(0)
    yield
    back2.wait_recv()
    total = total + got[14].astype(F32)
    on2.wait_recv()
    out[...] = total + got[13].astype(F32)
    for copy in pairs.values():
        copy.wait_send()
    for copy in sent:
        copy.wait_send()


def small_sum(spot, src, shared, pair, sums, got, pp, ss, rs, gs, gr, fs, fr):
    k = spot.core
    p = flat(*spot.pos)
    others = [plane_peer(lax.rem(p + d, 16), k) for d in range(1, 16)]
    first = remote(src.at[:, 1 - k], pair, pp.at[0], pp.at[1], spot.partner)
    first.start()
    yield
    first.wait_recv()
    sums[...] = src[:, k] + pair[...]
    sent = []
    for d, peer in enumerate(others):
        sent.append(
            remote(sums.at[lax.rem(p + d + 1, 16)], got.at[p], ss.at[d], rs.at[d], peer)
        )
        sent[-1].start()
    got[p] = sums[p]
    yield
    for copy in sent:
        copy.wait_recv()
    shared[p, k] = jnp.sum(got[...], axis=0)
    here = shared.at[p, k]
    spread = [remote(here, here, gs.at[d], gr.at[d], peer) for d, peer in enumerate(others)]
    onward = [remote(here, here, fs.at[0], fr.at[0], spot.partner)]
    for copy in spread + onward:
        copy.start()
    yield
    for d in range(1, 16):
        spread[d - 1].wait_recv()
        at = shared.at[lax.rem(p - d + 16, 16), k]
        onward.append(remote(at, at, fs.at[d], fr.at[d], spot.partner))
        onward[-1].start()
    yield
    for copy in [first] + sent + spread:
        copy.wait_send()
    for copy in onward:
        copy.wait()


def plane_peer(p, k):
    return {"batch": p // 8, "seq": lax.rem(p, 8) * 2 + k}


def scatter_kernel(count, *refs):
    ins, outs = refs[: count + 1], refs[count + 1 : 2 * count + 2]
    rest = refs[2 * count + 2 :]
    spot = Spot()
    p = flat(*spot.pos)
    greet([plane_peer(lax.rem(p + d, 16), spot.core) for d in range(1, 16)] + [spot.partner])
    jobs = [
        ring_scatter(spot, ins[a], outs[a], a % 2, *rest[7 * a : 7 * a + 7]) for a in range(count)
    ]
    jobs.append(small_sum(spot, ins[count], outs[count], *rest[7 * count :]))
    drive(jobs)


def scatter_scratch(a):
    dma = pltpu.SemaphoreType.DMA
    return [
        pltpu.VMEM((16, *a.shape[2:]), a.dtype),
        pltpu.VMEM((15, *a.shape[2:]), a.dtype),
        pltpu.VMEM((15, *a.shape[2:]), a.dtype),
        dma((16,)),
        dma((16,)),
        dma((15,)),
        dma((15,)),
    ]


def scatter_sum(arrays, small):
    dma = pltpu.SemaphoreType.DMA
    ins = [a.reshape(16, 2, 32, a.shape[1]) for a in arrays] + [small]
    scratch = [item for a in ins[:-1] for item in scatter_scratch(a)]
    scratch += [pltpu.VMEM((16, 8, 128), F32)] * 3
    scratch += [dma((2,)), dma((15,)), dma((15,)), dma((15,)), dma((15,)), dma((16,)), dma((16,))]
    return comm_call(
        functools.partial(scatter_kernel, len(arrays)),
        tuple(jax.ShapeDtypeStruct(a.shape[2:], F32) for a in ins[:-1])
        + (jax.ShapeDtypeStruct(small.shape, F32),),
        scratch,
        8,
        pltpu.VMEM,
        pltpu.VMEM,
        len(ins),
        "scatter_sum",
    )(*ins)


def turned(values, cosine, sine):
    lane = lax.broadcasted_iota(jnp.int32, values.shape, 1)
    swapped = jnp.where(
        lane < 8, pltpu.roll(values, 120, axis=1), pltpu.roll(values, 8, axis=1)
    )
    return values * cosine + swapped * sine


def normal(values):
    centred = values - jnp.mean(values, axis=-1, keepdims=True)
    rstd = lax.rsqrt(jnp.mean(centred * centred, axis=-1, keepdims=True) + 1e-05)
    return centred * rstd, rstd


def with_branch(x, branch, shift, out):
    for t in range(4):
        at = slice(256 * t, 256 * (t + 1))
        out[:, at] = x[:, at] + branch[t].astype(F32) + shift[:, at]


def norm_back(grad, z, x, out):
    hat, rstd = normal(x[...])
    flow = jnp.concatenate([z[t].astype(F32) for t in range(4)], axis=1)
    out[...] = grad[...] + rstd * (
        flow
        - jnp.mean(flow, axis=-1, keepdims=True)
        - hat * jnp.mean(flow * hat, axis=-1, keepdims=True)
    )


def project_kernel(x, g1, b1, g2, b2, bias, weight, cosine, sine, h1, h2, qkv):
    hat, _ = normal(x[...])
    h1[...] = (hat * g1[...] + b1[...]).astype(BF16)
    h2[...] = (hat * g2[...] + b2[...]).astype(BF16)
    proj = dot(h1[...], weight[...], 1, 0) + bias[...]
    cos, sin = cosine[...], sine[...]
    lane = lax.broadcasted_iota(jnp.int32, (128, 128), 1)
    for m in range(2):
        rows = proj[m * 128 : (m + 1) * 128]
        for h in range(4):
            pair = rows[:, 128 * h : 128 * (h + 1)]
            qkv[m * 4 + h, 0] = turned(pair, cos, sin).astype(BF16)
            q = rows[:, 512 + 128 * (h // 2) : 640 + 128 * (h // 2)]
            if h % 2:
                q = pltpu.roll(q, 64, axis=1)
            q = turned(q, cos, sin) * 0.125
            qkv[m * 4 + h, 1] = jnp.where(lane < 64, q, 0.0).astype(BF16)


def local_call(body, out_shape, in_specs, name, scratch=()):
    return pl.pallas_call(
        body,
        out_shape=out_shape,
        grid=(1,),
        in_specs=in_specs,
        out_specs=jax.tree.map(lambda o: whole(o.shape), out_shape),
        scratch_shapes=scratch,
        compiler_params=pltpu.CompilerParams(vmem_limit_bytes=VLIM),
        name=name,
    )


def whole(shape):
    return pl.BlockSpec(shape, lambda i: (0,) * len(shape))


def wholes(*arrays):
    return [whole(a.shape) for a in arrays]


def project(*args):
    sds = jax.ShapeDtypeStruct
    return local_call(
        project_kernel,
        (
            sds((256, 1024), BF16),
            sds((256, 1024), BF16),
            sds((8, 2, 128, 128), BF16),
        ),
        wholes(*args),
        "project",
    )(*args)


def scores_of(q, keys, low, high):
    s = dot(q, keys, 1, 1)
    place = lax.broadcasted_iota(jnp.int32, s.shape, 1)
    return jnp.where((place >= low) & (place <= high), s, MASKED)


def to_chip(i, src, dst, ss, rs, local):
    _, c, k = places()
    far = remote(src, dst, ss, rs, {"seq": 2 * i + k})
    near = pltpu.make_async_copy(src, dst, local)

    @pl.when(c != i)
    def _():
        far.start()

    @pl.when(c == i)
    def _():
        near.start()

    def left():
        @pl.when(c != i)
        def _():
            far.wait_send()

        @pl.when(c == i)
        def _():
            near.wait()

    return left


def from_chip(i, dst, ss, rs):
    _, c, k = places()

    @pl.when(c != i)
    def _():
        remote(dst, dst, ss, rs, {"seq": 2 * i + k}).wait_recv()


def seq_peers(spot):
    x, y = spot.pos
    ys = spot.ring(y)
    return chip_peers() + [spot.device(x, ys[1]), spot.device(x, ys[2]), spot.partner]


def attention(spot, src, low, high, kv_out, q_out, lse, ctx_in, ctx_out, *sems):
    ssem, rsem, fs, fr, lsem, cs, cr, cl = sems
    s, c, k = places()
    others = chip_peers()
    copies, copies_q = [], []
    for d, peer in enumerate(others):
        c2 = lax.rem(c + d + 1, 8)
        copies.append(remote(src.at[c2, 0], kv_out.at[s], ssem.at[0, d], rsem.at[0, d], peer))
        copies[-1].start()
    for d, peer in enumerate(others):
        c2 = lax.rem(c + d + 1, 8)
        copies_q.append(remote(src.at[c2, 1], q_out.at[c], ssem.at[1, d], rsem.at[1, d], peer))
        copies_q[-1].start()
    onward = [remote(src.at[c, 0], kv_out.at[s], fs.at[0], fr.at[0], spot.partner)]
    onward[0].start()
    own_kv = pltpu.make_async_copy(src.at[c, 0], kv_out.at[s], lsem.at[0])
    own_q = pltpu.make_async_copy(src.at[c, 1], q_out.at[c], lsem.at[1])
    own_kv.start()
    own_q.start()
    yield
    for d in range(1, 8):
        copies[d - 1].wait_recv()
        at = kv_out.at[lax.rem(c - d + 8, 8) * 2 + k]
        copy = remote(at, at, fs.at[d], fr.at[d], spot.partner)
        copy.start()
        onward.append(copy)
        yield
    own_kv.wait()
    own_q.wait()
    for copy in copies_q:
        copy.wait_recv()
    for copy in onward:
        copy.wait_recv()
    left = []
    for i in reversed(range(8)):
        n = 256 * (i + 1)
        keys = kv_out[0 : 2 * (i + 1)].reshape(n, 128)
        sc = scores_of(q_out[i], keys, low[i], high[i])
        top = jnp.max(sc, axis=-1, keepdims=True)
        e = jnp.exp(sc - top)
        total = jnp.sum(e, axis=-1, keepdims=True)
        soft = (e * (1.0 / total)).astype(BF16)
        ctx_out[i] = dot(soft, keys, 1, 0).astype(BF16)
        lse[i] = top + jnp.log(total)
        left.append(to_chip(i, ctx_out.at[i], ctx_in.at[c], cs.at[i], cr.at[c], cl))
        yield
    for i in reversed(range(8)):
        from_chip(i, ctx_in.at[i], cs.at[i], cr.at[i])
    for wait in left:
        wait()
    for copy in copies + copies_q + onward:
        copy.wait_send()


def attention_kernel(firsts, *refs):
    count = len(firsts)
    (src, low, high), srcs = refs[:3], refs[3 : 3 + count]
    refs = refs[3 + count :]
    (kv, q, lse, ctx_in), outs = refs[:4], refs[4 : 4 + count]
    refs = refs[4 + count :]
    spot = Spot()
    greet(seq_peers(spot))
    ctx_out, *sems = refs[:9]
    jobs = [attention(spot, src, low, high, kv, q, lse, ctx_in, ctx_out, *sems)]
    rest = refs[9:]
    for a in range(count):
        jobs.append(ring_gather(spot, srcs[a], outs[a], firsts[a], *rest[5 * a : 5 * a + 5]))
    drive(jobs)


def attend(qkv, low, high, shards, firsts, ident):
    sds, dma, count = jax.ShapeDtypeStruct, pltpu.SemaphoreType.DMA, len(shards)
    vmem, hbm = pl.BlockSpec(memory_space=pltpu.VMEM), pl.BlockSpec(memory_space=pl.ANY)
    return pl.pallas_call(
        functools.partial(attention_kernel, firsts),
        out_shape=(
            sds((16, 128, 128), BF16),
            sds((8, 128, 128), BF16),
            sds((8, 128, 1), F32),
            sds((8, 128, 128), BF16),
        )
        + tuple(sds((16, 2, *a.shape), a.dtype) for a in shards),
        in_specs=[vmem] * 3 + [hbm] * count,
        out_specs=[vmem] * 4 + [hbm] * count,
        scratch_shapes=[
            pltpu.VMEM((8, 128, 128), BF16),
            dma((2, 7)),
            dma((2, 7)),
            dma((8,)),
            dma((8,)),
            dma((2,)),
            dma((8,)),
            dma((8,)),
            dma(()),
        ]
        + [sem for _ in shards for sem in gather_sems()],
        compiler_params=pltpu.CompilerParams(
            collective_id=ident, has_side_effects=True, vmem_limit_bytes=VLIM
        ),
        name="attend",
    )(qkv, low, high, *shards)


def attention_back(
    spot, dctx, kv, q, lse, low, high, dq_in, dkv_in, dctx_in, dq, total, other, summed, *sems
):
    ds_, dr, dl, qs, qr, ql, ps, pr, ks, kr, kl = sems
    _, c, k = places()
    copies = []
    for d, peer in enumerate(chip_peers()):
        c2 = lax.rem(c + d + 1, 8)
        copies.append(remote(dctx.at[c2], dctx_in.at[c], ds_.at[d], dr.at[c], peer))
        copies[-1].start()
    own = pltpu.make_async_copy(dctx.at[c], dctx_in.at[c], dl)
    own.start()
    own.wait()
    yield
    left, pairs = [], {}

    def finish(i):
        pairs[i].wait_recv()
        summed[i] = (total[2 * i + k] + other[i]).astype(BF16)
        left.append(to_chip(i, summed.at[i], dkv_in.at[c], ks.at[i], kr.at[c], kl))

    for i in reversed(range(8)):
        n, blocks = 256 * (i + 1), 2 * (i + 1)
        from_chip(i, dctx_in.at[i], ds_.at[0], dr.at[i])
        keys = kv[0:blocks].reshape(n, 128)
        sc = scores_of(q[i], keys, low[i], high[i])
        soft = jnp.exp(sc - lse[i])
        dsoft = dot(dctx_in[i], keys, 1, 1)
        term = jnp.sum(soft * dsoft, axis=-1, keepdims=True)
        dscore = (soft * (dsoft - term)).astype(BF16)
        dq[i] = (dot(dscore, keys, 1, 0) * 0.125).astype(BF16)
        left.append(to_chip(i, dq.at[i], dq_in.at[c], qs.at[i], qr.at[c], ql))
        both = jnp.concatenate([dscore, soft.astype(BF16)], axis=0)
        right = jnp.concatenate([q[i], dctx_in[i]], axis=0)
        fresh = dot(both, right, 0, 0).reshape(blocks, 128, 128)
        if i == 7:
            total[...] = fresh
        else:
            total[0:blocks] += fresh
        pairs[i] = remote(total.at[2 * i + 1 - k], other.at[i], ps.at[i], pr.at[i], spot.partner)
        pairs[i].start()
        if i < 7:
            finish(i + 1)
        yield
    finish(0)
    for copy in pairs.values():
        copy.wait_send()
    yield
    for i in reversed(range(8)):
        from_chip(i, dq_in.at[i], qs.at[i], qr.at[i])
        from_chip(i, dkv_in.at[i], ks.at[i], kr.at[i])
    for wait in left:
        wait()
    for copy in copies:
        copy.wait_send()


def attention_back_kernel(firsts, *refs):
    count = len(firsts)
    ins, srcs = refs[:6], refs[6 : 6 + count]
    refs = refs[6 + count :]
    outs, sums = refs[:2], refs[2 : 2 + count]
    refs = refs[2 + count :]
    spot = Spot()
    greet(seq_peers(spot))
    jobs = [attention_back(spot, *ins, *outs, *refs[:16])]
    rest = refs[16:]
    for a in range(count):
        jobs.append(ring_scatter(spot, srcs[a], sums[a], firsts[a], *rest[7 * a : 7 * a + 7]))
    drive(jobs)


def attend_back(dctx, kv, q, lse, low, high, arrays, firsts, ident):
    sds, dma = jax.ShapeDtypeStruct, pltpu.SemaphoreType.DMA
    vmem = pl.BlockSpec(memory_space=pltpu.VMEM)
    ins = [a.reshape(16, 2, 32, a.shape[1]) for a in arrays]
    block, wide = (8, 128, 128), (16, 128, 128)
    return pl.pallas_call(
        functools.partial(attention_back_kernel, firsts),
        out_shape=(sds(block, BF16), sds(block, BF16))
        + tuple(sds(a.shape[2:], F32) for a in ins),
        in_specs=[vmem] * (6 + len(ins)),
        out_specs=[vmem] * (2 + len(ins)),
        scratch_shapes=[
            pltpu.VMEM(block, BF16),
            pltpu.VMEM(block, BF16),
            pltpu.VMEM(wide, F32),
            pltpu.VMEM(block, F32),
            pltpu.VMEM(block, BF16),
            dma((7,)),
            dma((8,)),
            dma(()),
            dma((8,)),
            dma((8,)),
            dma(()),
            dma((8,)),
            dma((8,)),
            dma((8,)),
            dma((8,)),
            dma(()),
        ]
        + [item for a in ins for item in scatter_scratch(a)],
        compiler_params=pltpu.CompilerParams(
            collective_id=ident, has_side_effects=True, vmem_limit_bytes=VLIM
        ),
        name="attend_back",
    )(dctx, kv, q, lse, low, high, *ins)


def feed_kernel(
    x, ctx_in, h2, outer, expand, bias, shift, u, both, x_out, part, out, buf, held, *sems
):
    greet_tensor(False)
    spot = Spot()
    lane = lax.broadcasted_iota(jnp.int32, (128, 128), 1)
    for m in range(2):
        for h in range(2):
            left = pltpu.roll(ctx_in[m * 4 + 2 * h].astype(F32), 64, axis=1)
            right = ctx_in[m * 4 + 2 * h + 1].astype(F32)
            both[m * 128 : (m + 1) * 128, 128 * h : 128 * (h + 1)] = jnp.where(
                lane < 64, left, right
            ).astype(BF16)
    inner = dot(h2[...], expand[...], 1, 0) + bias[...]
    u[...] = inner
    both[:, 256:] = (0.5 * inner * (1.0 + lax.erf(inner * 0.7071067811865476))).astype(BF16)
    greet_tensor(True)

    def make(t):
        part[t] = dot(both[...], outer[quarter(t), :], 1, 1).astype(BF16)

    drive(ring_jobs(spot, part, out, buf, held, sems, make))
    with_branch(x, out, shift, x_out)


def feed(*args):
    sds = jax.ShapeDtypeStruct
    return comm_call(
        feed_kernel,
        (sds((256, 1024), F32), sds((256, 1280), BF16), sds((256, 1024), F32)),
        ring_scratch(),
        6,
        pltpu.VMEM,
        pltpu.VMEM,
        len(args),
        "feed",
    )(*args)


def feed_back_kernel(grad, x, g2, u, both, h2, outer, expand, dctx, w_outer, w_expand, z2, small):
    gb = grad[...].astype(BF16)
    dact = dot(gb, outer[:, 256:], 1, 0)
    inner = u[...]
    slope = 0.5 * (1.0 + lax.erf(inner * 0.7071067811865476)) + inner * (
        0.3989422804014327 * jnp.exp(-0.5 * inner * inner)
    )
    du = (dact * slope).astype(BF16)
    dc = dot(gb, outer[:, :256], 1, 0)
    lane = lax.broadcasted_iota(jnp.int32, (128, 128), 1)
    for m in range(2):
        for h in range(4):
            piece = dc[m * 128 : (m + 1) * 128, 128 * (h // 2) : 128 * (h // 2 + 1)]
            if h % 2 == 0:
                piece = pltpu.roll(piece, 64, axis=1)
            dctx[m * 4 + h] = jnp.where(lane >= 64, piece, 0.0).astype(BF16)
    w_outer[...] = dot(gb, both[...], 0, 0).astype(BF16)
    w_expand[...] = dot(h2[...], du, 0, 0).astype(BF16)
    dh2 = dot(du, expand[...], 1, 1)
    hat, _ = normal(x[...])
    z2[...] = dh2 * g2[...]
    small[0:1] = jnp.sum(dh2 * hat, axis=0, keepdims=True)
    small[1:2] = jnp.sum(dh2, axis=0, keepdims=True)
    small[2:3] = jnp.sum(gb.astype(F32), axis=0, keepdims=True)
    small[3:4] = jnp.sum(du.astype(F32), axis=0, keepdims=True)


def feed_back(*args):
    sds = jax.ShapeDtypeStruct
    return local_call(
        feed_back_kernel,
        (
            sds((8, 128, 128), BF16),
            sds((1024, 1280), BF16),
            sds((1024, 1024), BF16),
            sds((256, 1024), F32),
            sds((4, 1024), F32),
        ),
        wholes(*args),
        "feed_back",
    )(*args)


def project_back_kernel(
    dq, dkv, cosine, sine, h1, weight, z2, x, g1, small2, grad, *refs
):
    w_left, w_right, small, bias_grad, grad_out = refs[:5]
    dproj, hat, vec, got, vs, vr, part, out, buf, held, *sems = refs[5:]
    greet_tensor(False)
    spot = Spot()
    cos, sin = cosine[...], -sine[...]
    lane = lax.broadcasted_iota(jnp.int32, (128, 128), 1)
    for m in range(2):
        rows = pl.ds(m * 128, 128)
        for h in range(4):
            dproj[rows, 128 * h : 128 * (h + 1)] = turned(
                dkv[m * 4 + h].astype(F32), cos, sin
            ).astype(BF16)
        for h in range(2):
            left = turned(dq[m * 4 + 2 * h].astype(F32), cos, sin)
            right = turned(dq[m * 4 + 2 * h + 1].astype(F32), cos, sin)
            dproj[rows, 512 + 128 * h : 640 + 128 * h] = jnp.where(
                lane < 64, left, pltpu.roll(right, 64, axis=1)
            ).astype(BF16)
    dp = dproj[...]
    hat[...] = normal(x[...])[0]
    vec[2:4] = small2[0:2]
    greet_tensor(True)

    def make(t):
        at = quarter(t)
        dh1 = dot(dp, weight[at, :], 1, 1)
        vec[0:1, at] = jnp.sum(dh1 * hat[:, at], axis=0, keepdims=True)
        vec[1:2, at] = jnp.sum(dh1, axis=0, keepdims=True)
        part[t] = (dh1 * g1[:, at] + z2[:, at]).astype(BF16)

    def beside():
        yield
        yield
        yield from direct_sum(vec, small, got, vs, vr)

    def weights():
        yield
        fresh = dot(h1[...], dp, 0, 0).astype(BF16)
        w_left[...] = fresh[:, :384]
        w_right[...] = fresh[:, 384:]
        bias_grad[...] = jnp.sum(dp.astype(F32), axis=0, keepdims=True)

    drive(ring_jobs(spot, part, out, buf, held, sems, make) + [weights(), beside()])
    norm_back(grad, out, x, grad_out)


def project_back(*args):
    sds, dma = jax.ShapeDtypeStruct, pltpu.SemaphoreType.DMA
    return comm_call(
        project_back_kernel,
        (
            sds((1024, 384), BF16),
            sds((1024, 384), BF16),
            sds((4, 1024), F32),
            sds((1, 768), F32),
            sds((256, 1024), F32),
        ),
        [
            pltpu.VMEM((256, 768), BF16),
            pltpu.VMEM((256, 1024), F32),
            pltpu.VMEM((4, 1024), F32),
            pltpu.VMEM((4, 4, 1024), F32),
            dma((3,)),
            dma((3,)),
        ]
        + ring_scratch(),
        7,
        pltpu.VMEM,
        pltpu.VMEM,
        len(args),
        "project_back",
    )(*args)


def head_order(value):
    lead = value.shape[:-1]
    parts = value.reshape(*lead, 4, 3, HEAD)
    keys = parts[..., 1:3, :].reshape(*lead, 512)
    return jnp.concatenate([keys, parts[..., 0, :].reshape(*lead, 256)], axis=-1)


def head_order_back(value):
    lead = value.shape[:-1]
    keys = value[..., :512].reshape(*lead, 4, 2, HEAD)
    queries = value[..., 512:].reshape(*lead, 4, 1, HEAD)
    return jnp.concatenate([queries, keys], axis=-2).reshape(*lead, 768)


def from_quarters(value):
    return value.transpose(1, 0, 2).reshape(256, 1024).astype(F32)


def local(
    hidden_in,
    document_ids,
    first_gain,
    first_shift,
    second_gain,
    second_shift,
    attn_weight,
    attn_bias,
    dense_weight,
    dense_bias,
    expand_weight,
    expand_bias,
    shrink_weight,
    shrink_bias,
    output_grad,
):
    seq_at = lax.axis_index("seq")
    chip, core = seq_at // 2, lax.rem(seq_at, 2)
    unit_micro = chip // 4
    lead = jnp.arange(ROT // 2, dtype=F32) * 2
    inverse = 10000.0 ** (-lead / ROT)
    place = (seq_at * 128 + jnp.arange(128, dtype=jnp.int32)).astype(F32)
    angles = place[:, None] * inverse[None, :]
    cos, sin = jnp.cos(angles), jnp.sin(angles)
    ones, zeros = jnp.ones((128, 112), F32), jnp.zeros((128, 112), F32)
    cosine = jnp.concatenate([cos, cos, ones], axis=1)
    sine = jnp.concatenate([-sin, sin, zeros], axis=1)

    attn = head_order(attn_weight)
    outer = jnp.concatenate(
        [jnp.swapaxes(dense_weight, 1, 2), jnp.swapaxes(shrink_weight, 1, 2)], axis=2
    )
    idents = jnp.pad(document_ids[:, 0], ((0, 6), (0, 0)))
    weight, idents = gather_plane([attn[0], idents], (0, 1), 1)
    weight = weight.reshape(1024, 768)
    idents = idents.reshape(2, 16, 8, 128)
    idents = lax.dynamic_index_in_dim(idents, lax.axis_index("batch"), 0, keepdims=False)
    mine = lax.dynamic_index_in_dim(idents, unit_micro, 1, keepdims=False).reshape(2048)
    count0 = jnp.sum((mine == 0).astype(jnp.int32))
    count1 = jnp.sum((mine == 1).astype(jnp.int32))
    start = jnp.where(mine == 0, 0, jnp.where(mine == 1, count0, count0 + count1))
    high = jnp.arange(2048, dtype=jnp.int32).reshape(8, 2, 128)
    high = lax.dynamic_index_in_dim(high, core, 1, keepdims=False)[..., None]
    low = lax.dynamic_index_in_dim(start.reshape(8, 2, 128), core, 1, keepdims=False)[..., None]
    bias_order = head_order(attn_bias)

    x = hidden_in.reshape(256, 1024)
    shift = dense_bias + shrink_bias
    kept = []
    for layer in range(LAYERS):
        row = slice(layer, layer + 1)
        h1, h2, qkv = project(
            x,
            first_gain[row],
            first_shift[row],
            second_gain[row],
            second_shift[row],
            bias_order[row],
            weight,
            cosine,
            sine,
        )
        shards = [outer[layer], expand_weight[layer]] + ([attn[1]] if layer == 0 else [])
        kv, q, lse, ctx_in, *wide = attend(
            qkv, low, high, shards, (0, 1, 1)[: len(shards)], 2 + layer
        )
        wide = [w.reshape(1024, w.shape[3]) for w in wide]
        u, both, x_next = feed(x, ctx_in, h2, *wide[:2], expand_bias[row], shift[row])
        kept.append((x, h1, h2, kv, q, lse, u, both, weight, wide[:2]))
        weight, x = wide[-1], x_next
    hidden_out = x.reshape(2, 1, 128, 1024)

    grad = output_grad.reshape(256, 1024)
    by_all, by_rows = [None] * 2, [None] * 2
    pending, sums = [], []
    for layer in reversed(range(LAYERS)):
        row = slice(layer, layer + 1)
        x, h1, h2, kv, q, lse, u, both, weight, wide = kept[layer]
        dctx, w_outer, w_expand, z2, small2 = feed_back(
            grad, x, second_gain[row], u, both, h2, *wide
        )
        arrays = [w_outer, w_expand] + pending
        dq_in, dkv_in, *ready = attend_back(
            dctx, kv, q, lse, low, high, arrays, (0, 1, 0, 1)[: len(arrays)], 4 + layer
        )
        sums += ready
        *pending, by_all[layer], bias_grad, grad = project_back(
            dq_in, dkv_in, cosine, sine, h1, weight, z2, x, first_gain[row], small2, grad
        )
        by_rows[layer] = jnp.concatenate([bias_grad[0], small2[2], small2[3]], axis=0)
    input_grad = grad.reshape(2, 1, 128, 1024)

    small = jnp.concatenate([v.reshape(-1) for v in by_all + by_rows]).reshape(32, 432)
    small = jnp.pad(small, ((0, 0), (0, 592))).reshape(16, 2, 8, 128)
    left, right, small = scatter_sum(pending, small)
    narrow_sum = jnp.stack(
        [jnp.concatenate([left, right], axis=1), jnp.concatenate(sums[4:6], axis=1)]
    )
    narrow_sum = head_order_back(narrow_sum)
    outer_sum, expand_sum = jnp.stack([sums[2], sums[0]]), jnp.stack([sums[3], sums[1]])
    small = small.reshape(32, 1024)[:, :432].reshape(13824)
    norms, rows = small[:8192].reshape(2, 4, 1024), small[8192:].reshape(2, 2816)
    branch_bias = rows[:, 768:1792]
    return (
        hidden_out,
        input_grad,
        norms[:, 0],
        norms[:, 1],
        norms[:, 2],
        norms[:, 3],
        narrow_sum,
        head_order_back(rows[:, :768]),
        jnp.swapaxes(outer_sum[..., :256], 1, 2),
        branch_bias,
        expand_sum,
        rows[:, 1792:],
        jnp.swapaxes(outer_sum[..., 256:], 1, 2),
        branch_bias,
    )


def solution(mesh):
    rows, spread, split = P(None, "batch", "seq", None), P(None, ("batch", "seq"), "tensor"), P(
        None, "tensor"
    )
    across = P(None, "tensor", ("batch", "seq"))
    return jax.shard_map(
        local,
        mesh=mesh,
        in_specs=(
            rows,
            P(None, "batch", "seq"),
            P(),
            P(),
            P(),
            P(),
            spread,
            split,
            across,
            P(),
            spread,
            split,
            across,
            P(),
            rows,
        ),
        out_specs=(
            rows,
            rows,
            P(),
            P(),
            P(),
            P(),
            spread,
            split,
            across,
            P(),
            spread,
            split,
            across,
            P(),
        ),
        check_vma=False,
    )
```
